32 devices in a mesh: grp: 4 (over z), ep: 8 (over y, x, core).
Axes of the slice: x: 2, y: 2, z: 4, core: 2. Of those that a mesh axis runs over, the one named last changes fastest.
Arguments:
- pol_hidden: bfloat16 [1280, 1024], P(('grp', 'ep')), may hold values from -80 to 80
- ref_hidden: bfloat16 [1280, 1024], P(('grp', 'ep')), may hold values from -80 to 80
- pol_routes: int32 [1280, 8], P(('grp', 'ep')), may hold values from 0 to 63, all different within a row; in each aligned block of 40 rows (0 to 39, 40 to 79, ...) at most 7 rows name the same one
- ref_routes: int32 [1280, 8], P(('grp', 'ep')), may hold values from 0 to 63, all different within a row; in each aligned block of 40 rows (0 to 39, 40 to 79, ...) at most 7 rows name the same one
- pol_gates: float32 [1280, 8], P(('grp', 'ep')), may hold values from 0.02 to 0.3
- ref_gates: float32 [1280, 8], P(('grp', 'ep')), may hold values from 0.02 to 0.3
- w_gate: bfloat16 [64, 1024, 384], P('ep'), may hold values from -0.1875 to 0.1875
- w_up: bfloat16 [64, 1024, 384], P('ep'), may hold values from -0.1875 to 0.1875
- w_down: bfloat16 [64, 384, 1024], P('ep'), may hold values from -0.3125 to 0.3125
- norm_gain: float32 [1024], replicated, may hold values from 0.5 to 1.5
- vocab_head: bfloat16 [77824, 1024], P(('grp', 'ep')), may hold values from -2 to 2
- targets: int32 [1280], P(('grp', 'ep')), may hold values from 0 to 77823
- seq_lengths: int32 [32], replicated, may hold values from 1 to 640, 1280 in all
- owners: int32 [32], replicated, may hold values from 0 to 31, each once
Outputs:
- token_ratio: float32 [1280], P(('grp', 'ep'))
- owned_mean: float32 [32], P(('grp', 'ep'))
The draws below stay inside these ranges and needn't reach their ends.
Inputs may be any that keep to these rules, and one draw needn't show every extreme that they name: `pol_routes`: each row names 8 different experts; among the 40 rows of one device no expert is named by more than 7 rows, a bound that some block reaches. `ref_routes`: each row names 8 different experts; among the 40 rows of one device no expert is named by more than 7 rows, a bound that some block reaches. `seq_lengths`: the lengths sum to 1280; the longest is exactly 640. `owners`: every device index appears exactly once.
All inputs are finite; a program needn't handle non-finite values.
Results may differ from the reference program's by a relative error of at most 0.0062.
Values may be sent and summed in bfloat16 or wider, within the bound.
No kernel may reach another device: no remote copies, remote signals or barrier semaphores. Data moves between devices by JAX's collectives and lax.ppermute only.
A program may use at most 128 MiB of HBM per device.

```python
import math
import jax
import jax.numpy as jnp
import numpy as np
from jax import lax

D = 1024
TOP = 8
FF = 384
EXPERTS = 64
VOCAB = 77824
TOK_DEV = 40
TOKENS = 1280
SEQS = 32
MOST_LEN = 640
CAP = 7


def hidden_law(key, salt):
    inner_key = jax.random.fold_in(key, salt)
    key_base, key_rows, key_cols = jax.random.split(inner_key, 3)
    row_scale = jnp.exp(jax.random.uniform(key_rows, (TOKENS, 1), jnp.float32, math.log(0.5), math.log(5.0)))
    col_scale = jnp.exp(jax.random.uniform(key_cols, (1, D), jnp.float32, math.log(0.3), math.log(3.0)))
    base = jnp.clip(jax.random.normal(key_base, (TOKENS, D), jnp.float32), -4.0, 4.0)
    values = base * row_scale * col_scale
    return values.astype(jnp.bfloat16)


def draw_pol_hidden(key, part):
    return hidden_law(key, 11)


def draw_ref_hidden(key, part):
    return hidden_law(key, 12)


def draw_vocab_head(key, part):
    inner_key = jax.random.fold_in(key, 21)
    key_base, key_rows = jax.random.split(inner_key, 2)
    row_scale = jnp.exp(jax.random.uniform(key_rows, (VOCAB, 1), jnp.float32, 0.0, math.log(10.0))) * D ** (-0.5)
    values = jnp.clip(jax.random.normal(key_base, (VOCAB, D), jnp.float32), -4.0, 4.0) * row_scale
    return values.astype(jnp.bfloat16)


def place_ends(drawn, stream_key, smallest, largest):
    dims = drawn.shape
    spot = [jax.random.randint(jax.random.fold_in(stream_key, axis), (), 0, dims[axis]) for axis in range(len(dims))]
    drawn = drawn.at[tuple(spot)].set(smallest)
    longest = dims.index(max(dims))
    spot[longest] = (spot[longest] + 1) % dims[longest]
    return drawn.at[tuple(spot)].set(largest)


def shard_levels(stream_key, shape, cuts, least, high):
    level = 1.0
    for position, parts in cuts:
        steps = jax.random.uniform(jax.random.fold_in(jax.random.fold_in(stream_key, 6), position), (parts,), jnp.float32, least / len(cuts), high / len(cuts))
        level = level * jnp.repeat(jnp.exp(steps), shape[position] // parts).reshape((-1,) + (1,) * (len(shape) - 1 - position))
    return level


def skewed_wide(own_key, extent, amount, slope):
    portions = [min(1 << octave, amount + 1 - (1 << octave)) * (1 << 20) // math.isqrt((1 << octave) ** slope) + 1 for octave in range((amount + 1).bit_length()) if 1 << octave <= amount]
    deviation = 1 + sum(portions) // (1 << 30)
    listing = np.cumsum(np.array([max(1, weight // deviation) for weight in portions]))
    lot = jax.random.randint(jax.random.fold_in(own_key, 1), extent, 0, int(listing[len(portions) - 1]))
    start = jnp.left_shift(1, jnp.searchsorted(jnp.asarray(listing, jnp.int32), lot, side="right").astype(jnp.int32))
    standing = start - 1 + jax.random.randint(jax.random.fold_in(own_key, 4), extent, 0, 1 << 30) % jnp.minimum(start, amount + 1 - start)
    return jax.random.permutation(jax.random.fold_in(own_key, 2), amount)[standing].astype(jnp.int32)


def split_up(number_of, total, limit, skew):
    weights = [(1 << 20) // math.isqrt(grade ** skew) + 1 for grade in range(2, number_of + 1)]
    spare, counts = total - limit - (number_of - 1), [1] * (number_of - 1)
    while spare > 0:
        movable = [i for i in range(number_of - 1) if counts[i] < limit]
        whole, budget = sum([weights[i] for i in movable]), spare
        for i in movable:
            more = min(limit - counts[i], max(1, budget * weights[i] // whole), spare)
            counts[i] = counts[i] + more
            spare = spare - more
    return np.array([limit] + counts)


def ragged_sizes(key, number_of, total, bound, skew):
    if number_of == 2:
        one = jax.random.randint(key, (), max(1, total - bound), min(bound, total - 1) + 1)
        return jnp.stack([one, total - one])
    lengths = jnp.asarray(split_up(number_of, total, bound, skew), jnp.int32)
    twos = (number_of - 1) // 2
    giver, receiver = lengths[1:1 + 2 * twos:2], lengths[2:2 + 2 * twos:2]
    slack = jnp.minimum(giver - 1, bound - receiver)
    passed = jax.random.randint(jax.random.fold_in(key, 1), (twos,), 0, 1 << 20) % (slack + 1)
    lengths = lengths.at[1:1 + 2 * twos:2].set(giver - passed).at[2:2 + 2 * twos:2].set(receiver + passed)
    return lengths[jax.random.permutation(jax.random.fold_in(key, 2), number_of)]


def shared_out(rng, own, number, rows, count, top, bound, lean):
    order = jax.random.permutation(rng, count)
    packed, ordinary = load_shares(count, rows * top, bound, lean, True), load_shares(count, rows * top, bound, lean, False)
    places = jnp.arange(count)

    def named(tallies, offset_by):
        used = int((tallies > 0).sum())
        fixed = max(1, used // 4)
        shifted = fixed + (places - fixed + offset_by * (used - fixed)) % max(1, count - fixed)
        return jnp.zeros((count,), jnp.int32).at[order[jnp.where(places < fixed, places, shifted)]].set(jnp.asarray(tallies, jnp.int32))

    tallies = jnp.where(number % 4 == 0, named(packed, number // 4), named(ordinary, number - number // 4 - 1))
    mixed = jax.random.permutation(jax.random.fold_in(own, 3), count)
    donor, sink = mixed[0:count // 2 * 2:2], mixed[1:count // 2 * 2:2]
    slack = jnp.minimum(tallies[donor] - 1, bound - tallies[sink]) // 2
    slack = jnp.where((donor == order[0]) | (sink == order[0]) | (tallies[sink] == 0), 0, jnp.maximum(slack, 0))
    shifted = jax.random.randint(jax.random.fold_in(own, 4), (count // 2,), 0, 1 << 20) % (slack + 1)
    tallies = tallies.at[donor].add(-shifted).at[sink].add(shifted)
    labels = jnp.searchsorted(jnp.cumsum(tallies), jnp.arange(rows * top), side="right").astype(jnp.int32)
    table = labels.reshape(top, rows).T
    table = table[jax.random.permutation(jax.random.fold_in(own, 1), rows)]
    offset_by = jax.random.randint(jax.random.fold_in(own, 2), (rows, 1), 0, top)
    return jnp.take_along_axis(table, (jnp.arange(top)[None, :] + offset_by) % top, axis=1)


def load_shares(amount, total, most, skew, full):
    loads = [(1 << 20) // math.isqrt(rank ** skew) + 1 for rank in range(1, amount + 1)]
    largest = most if full else min(most, max(-(-total // amount), total * loads[0] // sum(loads)))
    least = 1 if total - largest >= amount - 1 else 0
    given, rest = [largest] + [least] * (amount - 1), total - largest - least * (amount - 1)
    while rest > 0:
        movable = [i for i in range(1, amount) if given[i] < largest] or [i for i in range(1, amount) if given[i] < most]
        whole, budget = sum([loads[i] for i in movable]), rest
        for i in movable:
            more = min(most - given[i], max(1, budget * loads[i] // whole), rest)
            given[i] = given[i] + more
            rest = rest - more
    return np.array(given)


def bell_draw(own_key, dims, spread, bound, pieces=(), kind=jnp.bfloat16):
    drawn = jax.random.normal(own_key, dims, jnp.float32) * spread
    if len(pieces) > 0:
        drawn = shard_levels(own_key, dims, pieces, -0.22, 0.18) * drawn
    return jnp.clip(drawn, min=-bound, max=bound).astype(kind)


def setup_inputs(seed: int = 0) -> dict:
    seeds = jax.random.split(jax.random.key(seed), 15)
    pol_hidden = draw_pol_hidden(jax.random.fold_in(seeds[14], 71), 0)
    ref_hidden = draw_ref_hidden(jax.random.fold_in(seeds[14], 71), 0)
    pol_routes_keys = jax.random.split(jax.random.fold_in(seeds[2], 1), TOKENS // TOK_DEV)
    pol_routes_turns = jax.random.permutation(jax.random.fold_in(seeds[2], 3), TOKENS // TOK_DEV)
    pol_routes = jax.vmap(lambda own, number: shared_out(jax.random.fold_in(seeds[2], 2), own, number, TOK_DEV, EXPERTS, TOP, CAP, 2))(pol_routes_keys, pol_routes_turns).reshape((TOKENS, TOP))
    ref_routes_keys = jax.random.split(jax.random.fold_in(seeds[3], 1), TOKENS // TOK_DEV)
    ref_routes_turns = jax.random.permutation(jax.random.fold_in(seeds[3], 3), TOKENS // TOK_DEV)
    ref_routes = jax.vmap(lambda own, number: shared_out(jax.random.fold_in(seeds[3], 2), own, number, TOK_DEV, EXPERTS, TOP, CAP, 2))(ref_routes_keys, ref_routes_turns).reshape((TOKENS, TOP))
    pol_gates = jnp.clip(jnp.exp(math.log(0.3) - 2.7080503 * jax.random.uniform(seeds[4], (TOKENS, TOP), jnp.float32) ** shard_levels(seeds[4], (TOKENS, TOP), ((0, 32),), -0.2, 0.2)), 0.02, 0.3)
    ref_gates = jnp.clip(jnp.exp(math.log(0.3) - 2.7080503 * jax.random.uniform(seeds[5], (TOKENS, TOP), jnp.float32) ** shard_levels(seeds[5], (TOKENS, TOP), ((0, 32),), -0.2, 0.2)), 0.02, 0.3)
    w_gate = bell_draw(seeds[6], (EXPERTS, D, FF), D ** -0.5, 0.1875, ((0, 8),))
    w_up = bell_draw(seeds[7], (EXPERTS, D, FF), D ** -0.5, 0.1875, ((0, 8),))
    w_down = bell_draw(seeds[8], (EXPERTS, FF, D), FF ** -0.5, 0.3125, ((0, 8),))
    norm_gain = jnp.clip(1.0 + 0.1 * jax.random.normal(seeds[9], (D,), jnp.float32), 0.5, 1.5)
    vocab_head = draw_vocab_head(jax.random.fold_in(seeds[14], 71), 0)
    targets = place_ends(skewed_wide(seeds[11], (TOKENS,), VOCAB, 2), jax.random.fold_in(seeds[11], 3), 0, VOCAB - 1).astype(jnp.int32)
    seq_lengths = ragged_sizes(seeds[12], SEQS, TOKENS, MOST_LEN, 2).astype(jnp.int32)
    owners = jax.random.permutation(seeds[13], SEQS).astype(jnp.int32)
    return {"pol_hidden": pol_hidden, "ref_hidden": ref_hidden, "pol_routes": pol_routes, "ref_routes": ref_routes, "pol_gates": pol_gates, "ref_gates": ref_gates, "w_gate": w_gate, "w_up": w_up, "w_down": w_down, "norm_gain": norm_gain, "vocab_head": vocab_head, "targets": targets, "seq_lengths": seq_lengths, "owners": owners}


def expert_layer(hidden, routes, gates, w_gate, w_up, w_down):

    def one_expert(carry, items):
        gate_w, up_w, down_w, expert_id = items
        gate_act = jnp.dot(hidden, gate_w, preferred_element_type=jnp.float32)
        up_act = jnp.dot(hidden, up_w, preferred_element_type=jnp.float32)
        inner = (jax.nn.silu(gate_act) * up_act).astype(jnp.bfloat16)
        output = jnp.dot(inner, down_w, preferred_element_type=jnp.float32).astype(jnp.bfloat16)
        weight = lax.optimization_barrier(jnp.sum(jnp.where(routes == expert_id, gates, jnp.zeros_like(gates)), axis=1))
        return (carry + weight[:, None] * output.astype(gates.dtype), None)
    start_value = hidden.astype(gates.dtype)
    expert_ids = jnp.arange(w_gate.shape[0], dtype=jnp.int32)
    mixed, unused = lax.scan(one_expert, start_value, (w_gate, w_up, w_down, expert_ids))
    return mixed

def log_probs(normed, vocab_head, wanted):
    total_rows = normed.shape[0]
    block_rows = math.gcd(total_rows, 256)
    blocks = normed.reshape(total_rows // block_rows, block_rows, normed.shape[1])
    wanted_blocks = wanted.reshape(total_rows // block_rows, block_rows)

    def one_block(items):
        row_block, wanted_block = items
        logits = jnp.dot(row_block, vocab_head.T, preferred_element_type=jnp.float32)
        peak = lax.optimization_barrier(jnp.max(logits, axis=1))
        lse = peak + jnp.log(lax.optimization_barrier(jnp.sum(jnp.exp(logits - peak[:, None]), axis=1)))
        picked = jnp.take_along_axis(logits, wanted_block[:, None], axis=1)[:, 0]
        return picked - lse
    return lax.map(one_block, (blocks, wanted_blocks)).reshape(total_rows)

def reference(pol_hidden, ref_hidden, pol_routes, ref_routes, pol_gates, ref_gates, w_gate, w_up, w_down, norm_gain, vocab_head, targets, seq_lengths, owners):
    hidden = jnp.concatenate((pol_hidden, ref_hidden), axis=0)
    routes = jnp.concatenate((pol_routes, ref_routes), axis=0)
    gates = jnp.concatenate((pol_gates, ref_gates), axis=0)
    mixed = expert_layer(hidden, routes, gates, w_gate, w_up, w_down)
    scale = lax.rsqrt(lax.optimization_barrier(jnp.mean(mixed * mixed, axis=1, keepdims=True)) + 1e-06)
    normed = (mixed * scale * norm_gain).astype(jnp.bfloat16)
    wanted = jnp.concatenate((targets, targets), axis=0)
    logprob = log_probs(normed, vocab_head, wanted)
    token_ratio = logprob[:TOKENS] - logprob[TOKENS:]
    offsets = jnp.cumsum(seq_lengths) - seq_lengths
    positions = jnp.arange(TOKENS, dtype=jnp.int32)
    segment_ids = (lax.optimization_barrier(jnp.sum((positions[:, None] >= offsets[None, :]).astype(jnp.int32), axis=1)) - 1).astype(jnp.int32)
    sums = jax.ops.segment_sum(token_ratio, segment_ids, num_segments=SEQS)
    means = sums / seq_lengths.astype(token_ratio.dtype)
    owned_mean = jnp.zeros((SEQS,), token_ratio.dtype).at[owners].set(means)
    return (token_ratio, owned_mean)
```

```python
import functools

import jax
import jax.numpy as jnp
from jax import lax
from jax.experimental import pallas as pl
from jax.experimental.pallas import tpu as pltpu
from jax.sharding import Mesh, PartitionSpec as P

MIB = 1 << 20
LOW = -1e30


def round_up(value, step):
    return -(-value // step) * step


def largest_tile(rows, limit, step):
    best = rows
    for tile in range(step, min(rows, limit) + 1, step):
        if rows % tile == 0:
            best = tile
    return best


def expert_kernel(
    block, slots, width, experts, place_ref, x_ref, gate_ref, up_ref, down_ref, keep_ref, give_ref,
    table, pick, mix_hi, mix_lo, picked, made,
):
    step = pl.program_id(0)
    last = pl.num_programs(0) - 1
    rows = x_ref.shape[0]
    local_experts = pick.shape[0] // slots

    @pl.when(step == 0)
    def _():
        gates = x_ref[:, width:].astype(jnp.float32).T
        hits = (gates > 0.0).astype(jnp.bfloat16)
        before = lax.broadcasted_iota(jnp.int32, (rows, rows), 0)
        after = lax.broadcasted_iota(jnp.int32, (rows, rows), 1)
        first = after - after % block
        order = ((before < after) & (before >= first)).astype(jnp.bfloat16)
        rank = jnp.dot(hits, order, preferred_element_type=jnp.float32)
        token = lax.broadcasted_iota(jnp.int32, rank.shape, 1)
        per_block = slots // (rows // block)
        slot = rank + ((token // block) * per_block).astype(jnp.float32)
        table[0] = jnp.where(gates > 0.0, slot, -1.0)
        table[1] = gates
        spot = lax.broadcasted_iota(jnp.int32, (slots, rows), 0).astype(jnp.float32)
        for e in range(local_experts):
            row = place_ref[0] * local_experts + e
            chosen = table[0, pl.ds(row, 1), :] == spot
            band = pl.ds(e * slots, slots)
            pick[band, :] = jnp.where(chosen, 1.0, 0.0).astype(jnp.bfloat16)
            mix_hi[band, :] = jnp.where(chosen, table[1, pl.ds(row, 1), :], 0.0).astype(
                jnp.bfloat16
            )
            mix_lo[band, :] = jnp.where(
                chosen, table[1, pl.ds(row + experts, 1), :], 0.0
            ).astype(jnp.bfloat16)
        picked[...] = jnp.dot(
            pick[...], x_ref[:, :width], preferred_element_type=jnp.float32
        ).astype(jnp.bfloat16)

    band = pl.ds(pl.multiple_of(step * slots, slots), slots)
    mine = picked[band, :]
    gate_act = jnp.dot(mine, gate_ref[0], preferred_element_type=jnp.float32)
    up_act = jnp.dot(mine, up_ref[0], preferred_element_type=jnp.float32)
    inner = (gate_act / (1.0 + jnp.exp(-gate_act)) * up_act).astype(jnp.bfloat16)
    made[band, :] = jnp.dot(inner, down_ref[0], preferred_element_type=jnp.float32).astype(
        jnp.bfloat16
    )

    @pl.when(step == last)
    def _():
        over_slots = (((0,), (0,)), ((), ()))
        total = lax.dot_general(
            mix_hi[...], made[...], over_slots, preferred_element_type=jnp.float32
        )
        total += lax.dot_general(
            mix_lo[...], made[...], over_slots, preferred_element_type=jnp.float32
        )
        core = place_ref[0] % 2
        chips, share, _ = keep_ref.shape
        for owner in range(2):
            target = [total[(2 * c + owner) * share:(2 * c + owner + 1) * share] for c in range(chips)]

            @pl.when(core == owner)
            def _():
                for c in range(chips):
                    keep_ref[c] = target[c]

            @pl.when(core != owner)
            def _():
                for c in range(chips):
                    give_ref[c] = target[c]


def expert_sums(place, rows_in, w_gate, w_up, w_down, block, capacity, width, experts):
    rows = rows_in.shape[0]
    local_experts, _, hidden = w_gate.shape
    slots = round_up(capacity, 8) * (rows // block)
    every = local_experts * slots
    half = jax.ShapeDtypeStruct((rows // (4 * block), 2 * block, width), jnp.float32)
    return pl.pallas_call(
        functools.partial(expert_kernel, block, slots, width, experts),
        out_shape=(half, half),
        grid_spec=pltpu.PrefetchScalarGridSpec(
            num_scalar_prefetch=1,
            grid=(local_experts,),
            in_specs=[
                pl.BlockSpec(rows_in.shape, lambda e, place: (0, 0)),
                pl.BlockSpec((1, width, hidden), lambda e, place: (e, 0, 0)),
                pl.BlockSpec((1, width, hidden), lambda e, place: (e, 0, 0)),
                pl.BlockSpec((1, hidden, width), lambda e, place: (e, 0, 0)),
            ],
            out_specs=(
                pl.BlockSpec(half.shape, lambda e, place: (0, 0, 0)),
                pl.BlockSpec(half.shape, lambda e, place: (0, 0, 0)),
            ),
            scratch_shapes=[
                pltpu.VMEM((2, rows_in.shape[1] - width, rows), jnp.float32),
                pltpu.VMEM((every, rows), jnp.bfloat16),
                pltpu.VMEM((every, rows), jnp.bfloat16),
                pltpu.VMEM((every, rows), jnp.bfloat16),
                pltpu.VMEM((every, width), jnp.bfloat16),
                pltpu.VMEM((every, width), jnp.bfloat16),
            ],
        ),
        compiler_params=pltpu.CompilerParams(vmem_limit_bytes=56 * MIB),
        cost_estimate=pl.CostEstimate(
            flops=2 * every * width * (3 * hidden + 3 * rows),
            bytes_accessed=w_gate.size * 6 + rows_in.size * 2 + rows * width * 2,
            transcendentals=every * hidden,
        ),
    )(place, rows_in, w_gate, w_up, w_down)


def head_kernel(
    base_ref, wanted_ref, x_ref, head_a, head_b, lse_ref, hit_ref,
    peak, total, found, logits_a, logits_b,
):
    step = pl.program_id(1)
    last = pl.num_programs(1) - 1
    tile, columns = logits_a.shape
    lane_band = 128

    def product(head_ref, logits):
        logits[...] = lax.dot_general(
            head_ref[...], x_ref[...], (((1,), (1,)), ((), ())),
            preferred_element_type=jnp.float32,
        )

    def absorb(logits, first):
        row = lax.broadcasted_iota(jnp.int32, (tile, lane_band), 0)
        for start in range(0, columns, lane_band):
            band = pl.ds(start, lane_band)
            values = logits[:, band]
            old = peak[:, band]
            new = jnp.maximum(old, jnp.max(values.reshape(tile // 8, 8, lane_band), axis=0))
            grown = jnp.exp(values.reshape(tile // 8, 8, lane_band) - new[None])
            total[:, band] = total[:, band] * jnp.exp(old - new) + jnp.sum(grown, axis=0)
            same = row == wanted_ref[:, band] - first
            kept = jnp.where(same, values, 0.0).reshape(tile // 8, 8, lane_band)
            found[:, band] += jnp.sum(kept, axis=0)
            peak[:, band] = new

    @pl.when(step == 0)
    def _():
        peak[...] = jnp.full_like(peak, LOW)
        total[...] = jnp.zeros_like(total)
        found[...] = jnp.zeros_like(found)
        logits_b[...] = jnp.full_like(logits_b, LOW)

    product(head_a, logits_a)
    absorb(logits_b, jnp.where(step == 0, -(1 << 28), base_ref[1] + (step - 1) * tile))
    product(head_b, logits_b)
    absorb(logits_a, base_ref[0] + step * tile)

    @pl.when(step == last)
    def _():
        absorb(logits_b, base_ref[1] + step * tile)
        top = jnp.max(peak[...], axis=0, keepdims=True)
        full = jnp.sum(total[...] * jnp.exp(peak[...] - top), axis=0, keepdims=True)
        lse_ref[...] = top + jnp.log(full)
        hit_ref[...] = jnp.sum(found[...], axis=0, keepdims=True)


def head_stats(base, wanted, rows_in, head_a, head_b):
    rows, width = rows_in.shape
    chunk = largest_tile(rows, 1280, 128)
    tile = largest_tile(head_a.shape[0], 608, 16)
    steps = head_a.shape[0] // tile
    line = jax.ShapeDtypeStruct((1, rows), jnp.float32)
    return pl.pallas_call(
        head_kernel,
        out_shape=(line, line),
        grid_spec=pltpu.PrefetchScalarGridSpec(
            num_scalar_prefetch=1,
            grid=(rows // chunk, steps),
            in_specs=[
                pl.BlockSpec((1, chunk), lambda c, s, base: (0, c)),
                pl.BlockSpec((chunk, width), lambda c, s, base: (c, 0)),
                pl.BlockSpec((tile, width), lambda c, s, base: (s, 0)),
                pl.BlockSpec((tile, width), lambda c, s, base: (s, 0)),
            ],
            out_specs=(
                pl.BlockSpec((1, chunk), lambda c, s, base: (0, c)),
                pl.BlockSpec((1, chunk), lambda c, s, base: (0, c)),
            ),
            scratch_shapes=[
                pltpu.VMEM((8, chunk), jnp.float32),
                pltpu.VMEM((8, chunk), jnp.float32),
                pltpu.VMEM((8, chunk), jnp.float32),
                pltpu.VMEM((tile, chunk), jnp.float32),
                pltpu.VMEM((tile, chunk), jnp.float32),
            ],
        ),
        compiler_params=pltpu.CompilerParams(vmem_limit_bytes=56 * MIB),
        cost_estimate=pl.CostEstimate(
            flops=4 * rows * width * head_a.shape[0],
            bytes_accessed=head_a.size * 4 + rows_in.size * 2,
            transcendentals=2 * rows * head_a.shape[0],
        ),
    )(base, wanted, rows_in, head_a, head_b)


def gate_table(routes, gates, experts):
    hits = routes[:, :, None] == jnp.arange(experts, dtype=jnp.int32)[None, None, :]
    dense = jnp.sum(jnp.where(hits, gates[:, :, None], 0.0), axis=1)
    high = dense.astype(jnp.bfloat16)
    low = (dense - high.astype(jnp.float32)).astype(jnp.bfloat16)
    return jnp.concatenate((high, low), axis=1)


def local(
    pol_hidden, ref_hidden, pol_routes, ref_routes, pol_gates, ref_gates,
    w_gate, w_up, w_down, norm_gain, vocab_head, targets, seq_lengths, owners,
):
    plane = ("chip", "core")
    band = ("grp", "chip")
    everyone = ("grp", "chip", "core")
    core = lax.axis_index("core")
    device = lax.axis_index(everyone)
    devices = lax.axis_size(everyone)
    peers = lax.axis_size(band)
    experts = w_gate.shape[0] * lax.axis_size(plane)
    tokens, width = pol_hidden.shape
    capacity = tokens * pol_routes.shape[1] // experts + 2
    vocab_rows = vocab_head.shape[0]

    other_head = lax.ppermute(vocab_head, "core", ((0, 1), (1, 0)))
    wanted = lax.all_gather(targets, band, axis=0)
    wanted = jnp.concatenate((wanted, wanted), axis=1).reshape(1, -1)

    hidden = jnp.concatenate((pol_hidden, ref_hidden), axis=0)
    tables = jnp.concatenate(
        (gate_table(pol_routes, pol_gates, experts), gate_table(ref_routes, ref_gates, experts)),
        axis=0,
    )
    send = jnp.concatenate((hidden, tables), axis=1)
    plane_rows = lax.all_gather(send, plane, axis=0, tiled=True)
    place = lax.axis_index(plane).reshape(1)
    keep, give = expert_sums(
        place, plane_rows, w_gate, w_up, w_down, tokens, capacity, width, experts
    )
    parts = keep + lax.ppermute(give, "core", ((0, 1), (1, 0)))
    parts = lax.all_to_all(parts, "chip", split_axis=0, concat_axis=0, tiled=True)
    mixed = hidden.astype(jnp.float32) + jnp.sum(parts, axis=0)
    scale = lax.rsqrt(jnp.mean(mixed * mixed, axis=1, keepdims=True) + 1e-06)
    normed = (mixed * scale * norm_gain).astype(jnp.bfloat16)

    rows = lax.all_gather(normed, band, axis=0, tiled=True)
    base = jnp.stack((device, device + 1 - 2 * core)).astype(jnp.int32) * vocab_rows
    lse, hit = head_stats(base, wanted, rows, vocab_head, other_head)
    stats = jnp.stack((lse.reshape(peers, -1), hit.reshape(peers, -1)), axis=1)
    stats = lax.all_to_all(stats, band, split_axis=0, concat_axis=0, tiled=True)
    top = jnp.max(stats[:, 0], axis=0)
    whole = top + jnp.log(jnp.sum(jnp.exp(stats[:, 0] - top[None]), axis=0))
    logprob = jnp.sum(stats[:, 1], axis=0) - whole
    token_ratio = logprob[:tokens] - logprob[tokens:]

    ends = jnp.cumsum(seq_lengths)
    offsets = ends - seq_lengths
    positions = device * tokens + jnp.arange(tokens, dtype=jnp.int32)
    inside = (positions[None, :] >= offsets[:, None]) & (positions[None, :] < ends[:, None])
    share = jnp.sum(jnp.where(inside, token_ratio[None, :], 0.0), axis=1)
    share = share / seq_lengths.astype(jnp.float32)
    to_owner = owners[None, :] == jnp.arange(devices, dtype=jnp.int32)[:, None]
    outgoing = jnp.sum(jnp.where(to_owner, share[None, :], 0.0), axis=1).reshape(devices, 1)
    incoming = lax.all_to_all(outgoing, everyone, split_axis=0, concat_axis=0, tiled=True)
    return (token_ratio, jnp.sum(incoming).reshape(1))


def solution(mesh):
    names = ("grp", "chip", "core")
    groups, plane = mesh.devices.shape
    fine = Mesh(mesh.devices.reshape(groups, plane // 2, 2), names)
    return jax.shard_map(
        local,
        mesh=fine,
        in_specs=(
            P(names, None), P(names, None), P(names, None), P(names, None),
            P(names, None), P(names, None),
            P(names[1:], None, None), P(names[1:], None, None), P(names[1:], None, None),
            P(), P(names, None), P(names), P(), P(),
        ),
        out_specs=(P(names), P(names)),
        check_vma=False,
    )
```

```python
import functools
import math

import jax
import jax.numpy as jnp
from jax import lax
from jax.experimental import pallas as pl
from jax.experimental.pallas import tpu as pltpu
from jax.sharding import Mesh, PartitionSpec as P

MIB = 1 << 20
LOW = -1e30


def round_up(value, step):
    return -(-value // step) * step


def largest_tile(rows, limit, step):
    best = rows
    for tile in range(step, min(rows, limit) + 1, step):
        if rows % tile == 0:
            best = tile
    return best


def pack_kernel(pol_ref, ref_ref, pol_routes, ref_routes, pol_gates, ref_gates, out_ref, room):
    tokens, width = pol_ref.shape
    experts = (room.shape[1] - width) // 2
    parts = ((pol_ref, pol_routes, pol_gates), (ref_ref, ref_routes, ref_gates))
    for index, (hidden, routes, gates) in enumerate(parts):
        band = pl.ds(index * tokens, tokens)
        room[band, :width] = hidden[...].astype(jnp.float32)
        expert = lax.broadcasted_iota(jnp.int32, (experts, tokens), 0)
        dense = jnp.zeros((experts, tokens), jnp.float32)
        for k in range(routes.shape[0]):
            dense = jnp.where(expert == routes[pl.ds(k, 1), :], gates[pl.ds(k, 1), :], dense)
        high = dense.astype(jnp.bfloat16).astype(jnp.float32)
        table = jnp.concatenate((high, dense - high), axis=0)
        room[band, width:] = table.T
    out_ref[...] = room[...].astype(jnp.bfloat16)


def pack_rows(pol_hidden, ref_hidden, pol_routes, ref_routes, pol_gates, ref_gates, experts):
    tokens, width = pol_hidden.shape
    shape = (2 * tokens, width + 2 * experts)
    return pl.pallas_call(
        pack_kernel,
        out_shape=jax.ShapeDtypeStruct(shape, jnp.bfloat16),
        scratch_shapes=[pltpu.VMEM(shape, jnp.float32)],
        compiler_params=pltpu.CompilerParams(vmem_limit_bytes=16 * MIB),
    )(pol_hidden, ref_hidden, pol_routes.T, ref_routes.T, pol_gates.T, ref_gates.T)


def expert_kernel(block, slots, width, experts, chips, place_ref, *refs):
    count = 2 * chips
    blocks, refs = refs[:count], refs[count:]
    gate_ref, up_ref, down_ref, keep_ref, give_ref = refs[:5]
    rows_in, table, pick, mix_hi, mix_lo, picked, made = refs[5:]
    step = pl.program_id(0)
    last = pl.num_programs(0) - 1
    rows = rows_in.shape[0]
    share = rows // count
    local_experts = pick.shape[0] // slots
    chip, core = place_ref[0], place_ref[1]

    @pl.when(step == 0)
    def _():
        for index, ref in enumerate(blocks):
            owner = 2 * (chip ^ (index % chips)) + (core ^ (index // chips))
            rows_in[pl.ds(pl.multiple_of(owner * share, 16), share), :] = ref[...]
        gates = rows_in[:, width:].astype(jnp.float32).T
        hits = (gates > 0.0).astype(jnp.bfloat16)
        span = math.gcd(rows, 16 * block)
        before = lax.broadcasted_iota(jnp.int32, (span, span), 0)
        after = lax.broadcasted_iota(jnp.int32, (1, span), 1)
        first = after - after % block
        order = ((before < after) & (before >= first)).astype(jnp.bfloat16)
        per_block = slots // (rows // block)
        for start in range(0, rows, span):
            band = slice(start, start + span)
            rank = jnp.dot(hits[:, band], order, preferred_element_type=jnp.float32)
            slot = rank + ((start + after) // block * per_block).astype(jnp.float32)
            table[0, :, band] = jnp.where(gates[:, band] > 0.0, slot, -1.0)
        table[1] = gates
        spot = lax.broadcasted_iota(jnp.int32, (slots, rows), 0).astype(jnp.float32)
        for e in range(local_experts):
            row = (2 * chip + core) * local_experts + e
            chosen = table[0, pl.ds(row, 1), :] == spot
            band = pl.ds(e * slots, slots)
            pick[band, :] = jnp.where(chosen, 1.0, 0.0).astype(jnp.bfloat16)
            mix_hi[band, :] = jnp.where(chosen, table[1, pl.ds(row, 1), :], 0.0).astype(
                jnp.bfloat16
            )
            mix_lo[band, :] = jnp.where(
                chosen, table[1, pl.ds(row + experts, 1), :], 0.0
            ).astype(jnp.bfloat16)
        picked[...] = jnp.dot(
            pick[...], rows_in[:, :width], preferred_element_type=jnp.float32
        ).astype(jnp.bfloat16)

    band = pl.ds(pl.multiple_of(step * slots, slots), slots)
    mine = picked[band, :]
    gate_act = jnp.dot(mine, gate_ref[0], preferred_element_type=jnp.float32)
    up_act = jnp.dot(mine, up_ref[0], preferred_element_type=jnp.float32)
    inner = (gate_act / (1.0 + jnp.exp(-gate_act)) * up_act).astype(jnp.bfloat16)
    made[band, :] = jnp.dot(inner, down_ref[0], preferred_element_type=jnp.float32).astype(
        jnp.bfloat16
    )

    @pl.when(step == last)
    def _():
        over_slots = (((0,), (0,)), ((), ()))
        span = math.gcd(rows, 16 * block)
        for start in range(0, rows, span):
            band = pl.ds(start, span)
            total = lax.dot_general(
                mix_hi[:, band], made[...], over_slots, preferred_element_type=jnp.float32
            )
            total += lax.dot_general(
                mix_lo[:, band], made[...], over_slots, preferred_element_type=jnp.float32
            )
            for index in range(span // share):
                c, owner = divmod(start // share + index, 2)
                target = total[index * share:(index + 1) * share]

                @pl.when(core == owner)
                def _():
                    keep_ref[c ^ chip] = target

                @pl.when(core != owner)
                def _():
                    give_ref[c ^ chip] = target


def expert_sums(place, blocks, w_gate, w_up, w_down, block, capacity, width, experts):
    count = len(blocks)
    share, wide = blocks[0].shape
    rows = count * share
    local_experts, _, hidden = w_gate.shape
    slots = round_up(capacity, 8) * (rows // block)
    every = local_experts * slots
    half = jax.ShapeDtypeStruct((count // 2, share, width), jnp.float32)
    whole = pl.BlockSpec(
        (share, wide), lambda e, place: (0, 0), pipeline_mode=pl.Buffered(1)
    )
    return pl.pallas_call(
        functools.partial(expert_kernel, block, slots, width, experts, count // 2),
        out_shape=(half, half),
        grid_spec=pltpu.PrefetchScalarGridSpec(
            num_scalar_prefetch=1,
            grid=(local_experts,),
            in_specs=[whole] * count + [
                pl.BlockSpec((1, width, hidden), lambda e, place: (e, 0, 0)),
                pl.BlockSpec((1, width, hidden), lambda e, place: (e, 0, 0)),
                pl.BlockSpec((1, hidden, width), lambda e, place: (e, 0, 0)),
            ],
            out_specs=(
                pl.BlockSpec(
                    half.shape, lambda e, place: (0, 0, 0), pipeline_mode=pl.Buffered(1)
                ),
                pl.BlockSpec(
                    half.shape, lambda e, place: (0, 0, 0), pipeline_mode=pl.Buffered(1)
                ),
            ),
            scratch_shapes=[
                pltpu.VMEM((rows, wide), jnp.bfloat16),
                pltpu.VMEM((2, wide - width, rows), jnp.float32),
                pltpu.VMEM((every, rows), jnp.bfloat16),
                pltpu.VMEM((every, rows), jnp.bfloat16),
                pltpu.VMEM((every, rows), jnp.bfloat16),
                pltpu.VMEM((every, width), jnp.bfloat16),
                pltpu.VMEM((every, width), jnp.bfloat16),
            ],
        ),
        compiler_params=pltpu.CompilerParams(vmem_limit_bytes=58 * MIB),
        cost_estimate=pl.CostEstimate(
            flops=2 * every * width * (3 * hidden + 3 * rows),
            bytes_accessed=w_gate.size * 6 + rows * wide * 2 + rows * width * 4,
            transcendentals=every * hidden,
        ),
    )(place, *blocks, w_gate, w_up, w_down)


def pair_kernel(keep_ref, came_ref, own_ref, *sends):
    own_ref[...] = keep_ref[0] + came_ref[0]
    for index, send in enumerate(sends):
        send[...] = keep_ref[index + 1] + came_ref[index + 1]


def pair_sums(keep, came):
    chips, share, width = keep.shape
    own = jax.ShapeDtypeStruct((share, width), jnp.float32)
    return pl.pallas_call(
        pair_kernel,
        out_shape=(own,) * chips,
        compiler_params=pltpu.CompilerParams(vmem_limit_bytes=32 * MIB),
    )(keep, came)


def norm_kernel(hidden_ref, gain_ref, own_ref, *refs):
    width = own_ref.shape[1]
    mixed = hidden_ref[:, :width].astype(jnp.float32) + own_ref[...]
    for ref in refs[:-1]:
        mixed += ref[...]
    scale = lax.rsqrt(jnp.mean(mixed * mixed, axis=1, keepdims=True) + 1e-06)
    refs[-1][...] = (mixed * scale * gain_ref[...]).astype(jnp.bfloat16)


def norm_rows(hidden, gain, own, others):
    return pl.pallas_call(
        norm_kernel,
        out_shape=jax.ShapeDtypeStruct(own.shape, jnp.bfloat16),
        compiler_params=pltpu.CompilerParams(vmem_limit_bytes=16 * MIB),
    )(hidden, gain.reshape(1, -1), own, *others)


def head_kernel(count, spots_ref, wanted_ref, *refs):
    blocks, refs = refs[:count], refs[count:]
    head_a, head_b, out_ref, rows_in, peak, total, found, logits_a, logits_b = refs
    step = pl.program_id(0)
    last = pl.num_programs(0) - 1
    tile, columns = logits_a.shape
    lane_band = 128
    share = columns // out_ref.shape[0]
    base_a, base_b = spots_ref[0], spots_ref[1]

    def product(head_ref, logits):
        logits[...] = lax.dot_general(
            head_ref[...], rows_in[...], (((1,), (1,)), ((), ())),
            preferred_element_type=jnp.float32,
        )

    def absorb(logits, first):
        row = lax.broadcasted_iota(jnp.int32, (tile, lane_band), 0)
        for start in range(0, columns, lane_band):
            band = pl.ds(start, lane_band)
            values = logits[:, band]
            old = peak[:, band]
            new = jnp.maximum(old, jnp.max(values.reshape(tile // 8, 8, lane_band), axis=0))
            grown = jnp.exp(values.reshape(tile // 8, 8, lane_band) - new[None])
            total[:, band] = total[:, band] * jnp.exp(old - new) + jnp.sum(grown, axis=0)
            same = row == wanted_ref[:, band] - first
            kept = jnp.where(same, values, 0.0).reshape(tile // 8, 8, lane_band)
            found[:, band] += jnp.sum(kept, axis=0)
            peak[:, band] = new

    @pl.when(step == 0)
    def _():
        start = 0
        for ref in blocks:
            rows_in[start:start + ref.shape[0], :] = ref[...]
            start += ref.shape[0]
        peak[...] = jnp.full_like(peak, LOW)
        total[...] = jnp.zeros_like(total)
        found[...] = jnp.zeros_like(found)
        logits_b[...] = jnp.full_like(logits_b, LOW)

    product(head_a, logits_a)
    absorb(logits_b, jnp.where(step == 0, -(1 << 28), base_b + (step - 1) * tile))
    product(head_b, logits_b)
    absorb(logits_a, base_a + step * tile)

    @pl.when(step == last)
    def _():
        absorb(logits_b, base_b + step * tile)
        top = jnp.max(peak[...], axis=0, keepdims=True)
        full = jnp.sum(total[...] * jnp.exp(peak[...] - top), axis=0, keepdims=True)
        lse = top + jnp.log(full)
        hit = jnp.sum(found[...], axis=0, keepdims=True)
        for index in range(out_ref.shape[0]):
            band = slice(index * share, (index + 1) * share)
            spot = spots_ref[2 + index]
            out_ref[spot, 0:1, :] = lse[:, band]
            out_ref[spot, 1:2, :] = hit[:, band]


def head_stats(spots, wanted, blocks, head_a, head_b, share):
    rows = sum(block.shape[0] for block in blocks)
    width = head_a.shape[1]
    tile = largest_tile(head_a.shape[0], 608 * 1280 // rows, 16)
    steps = head_a.shape[0] // tile
    return pl.pallas_call(
        functools.partial(head_kernel, len(blocks)),
        out_shape=jax.ShapeDtypeStruct((rows // share, 2, share), jnp.float32),
        grid_spec=pltpu.PrefetchScalarGridSpec(
            num_scalar_prefetch=1,
            grid=(steps,),
            in_specs=[pl.BlockSpec((1, rows), lambda s, spots: (0, 0))] + [
                pl.BlockSpec(block.shape, lambda s, spots: (0, 0), pipeline_mode=pl.Buffered(1))
                for block in blocks
            ] + [
                pl.BlockSpec((tile, width), lambda s, spots: (s, 0)),
                pl.BlockSpec((tile, width), lambda s, spots: (s, 0)),
            ],
            out_specs=pl.BlockSpec((rows // share, 2, share), lambda s, spots: (0, 0, 0)),
            scratch_shapes=[
                pltpu.VMEM((rows, width), jnp.bfloat16),
                pltpu.VMEM((8, rows), jnp.float32),
                pltpu.VMEM((8, rows), jnp.float32),
                pltpu.VMEM((8, rows), jnp.float32),
                pltpu.VMEM((tile, rows), jnp.float32),
                pltpu.VMEM((tile, rows), jnp.float32),
            ],
        ),
        compiler_params=pltpu.CompilerParams(vmem_limit_bytes=58 * MIB),
        cost_estimate=pl.CostEstimate(
            flops=4 * rows * width * head_a.shape[0],
            bytes_accessed=head_a.size * 4 + rows * width * 2,
            transcendentals=2 * rows * head_a.shape[0],
        ),
    )(spots, wanted, *blocks, head_a, head_b)


def combine(parts):
    top = functools.reduce(jnp.maximum, [part[:, 0] for part in parts])
    total = sum(jnp.exp(part[:, 0] - top) for part in parts)
    return top + jnp.log(total), sum(part[:, 1] for part in parts)


def across(value, offset):
    chips = lax.axis_size("chip")
    return lax.ppermute(value, "chip", [(c, c ^ offset) for c in range(chips)])


def along(value, offset):
    groups = lax.axis_size("grp")
    return lax.ppermute(value, "grp", [(g, (g + offset) % groups) for g in range(groups)])


def partner(value):
    return lax.ppermute(value, "core", ((0, 1), (1, 0)))


def local(
    pol_hidden, ref_hidden, pol_routes, ref_routes, pol_gates, ref_gates,
    w_gate, w_up, w_down, norm_gain, vocab_head, targets, seq_lengths, owners,
):
    chip, core, group = lax.axis_index("chip"), lax.axis_index("core"), lax.axis_index("grp")
    chips, groups = lax.axis_size("chip"), lax.axis_size("grp")
    device = (group * chips + chip) * 2 + core
    experts = w_gate.shape[0] * chips * 2
    tokens, width = pol_hidden.shape
    share = 2 * tokens
    capacity = tokens * pol_routes.shape[1] // experts + 2
    vocab_rows = vocab_head.shape[0]
    offsets = range(1, chips)

    send = pack_rows(
        pol_hidden, ref_hidden, pol_routes, ref_routes, pol_gates, ref_gates, experts
    )
    plane = [send] + [across(send, d) for d in offsets]
    plane = plane + [partner(rows) for rows in plane]

    goal = targets.reshape(1, tokens)
    goal = jnp.concatenate([goal] + [along(goal, k) for k in range(1, groups)], axis=0)
    goal = jnp.stack([goal] + [across(goal, d) for d in offsets])
    wanted = jnp.concatenate((goal, goal), axis=2).reshape(1, -1)
    other_head = partner(vocab_head)

    place = jnp.stack((chip, core)).astype(jnp.int32)
    keep, give = expert_sums(place, plane, w_gate, w_up, w_down, tokens, capacity, width, experts)
    own, *sends = pair_sums(keep, partner(give))
    came = [across(rows, d) for d, rows in zip(offsets, sends)]
    normed = norm_rows(send, norm_gain, own, came)

    column = [normed] + [along(normed, k) for k in range(1, groups)]
    if chips == 4:
        near = [across(rows, 1) for rows in column]
        far = [across(rows, 2) for rows in column]
        half = groups // 2
        cross = [across(rows, 2) for rows in near[:half]] + [
            across(rows, 1) for rows in far[half:]
        ]
        blocks = column + near + far + cross
    else:
        column = jnp.concatenate(column, axis=0)
        blocks = [column] + [across(column, d) for d in offsets]
    home = (group - jnp.arange(groups, dtype=jnp.int32)) % groups
    spots = home[None, :] * chips + (chip ^ jnp.arange(chips, dtype=jnp.int32))[:, None]
    base = jnp.stack((device, device + 1 - 2 * core)).astype(jnp.int32) * vocab_rows
    rows = groups * chips * share
    if rows <= 1280:
        spots = jnp.concatenate((base, spots.reshape(-1)))
        stats = head_stats(spots, wanted, blocks, vocab_head, other_head, share)
    else:
        lines = groups * share
        pieces = [
            head_stats(
                jnp.concatenate((base, jnp.arange(groups, dtype=jnp.int32))),
                wanted[:, d * lines:(d + 1) * lines], [block], vocab_head, other_head, share,
            )
            for d, block in enumerate(blocks)
        ]
        pieces = jnp.concatenate(pieces, axis=0)
        stats = jnp.zeros_like(pieces).at[spots.reshape(-1)].set(pieces)

    lse, hit = combine([stats] + [along(stats, k) for k in range(1, groups)])
    stats = jnp.stack((lse, hit), axis=1)
    lse, hit = combine([stats] + [across(stats, d) for d in offsets])
    logprob = hit - lse
    ratio = logprob[:, :tokens] - logprob[:, tokens:]
    other = partner(ratio)
    token_ratio = lax.dynamic_index_in_dim(ratio, group * chips + chip, keepdims=False)

    mine = owners == device
    ends = jnp.cumsum(seq_lengths)
    length = jnp.sum(jnp.where(mine, seq_lengths, 0))
    end = jnp.sum(jnp.where(mine, ends, 0))
    row = jnp.arange(groups * chips, dtype=jnp.int32)[:, None]
    lane = jnp.arange(tokens, dtype=jnp.int32)[None, :]
    position = (2 * row + core) * tokens + lane
    inside = (position >= end - length) & (position < end)
    position = (2 * row + 1 - core) * tokens + lane
    inside_other = (position >= end - length) & (position < end)
    mean = jnp.sum(jnp.where(inside, ratio, 0.0) + jnp.where(inside_other, other, 0.0))
    return (token_ratio, (mean / length.astype(jnp.float32)).reshape(1))


def solution(mesh):
    names = ("grp", "chip", "core")
    groups, plane = mesh.devices.shape
    fine = Mesh(mesh.devices.reshape(groups, plane // 2, 2), names)
    return jax.shard_map(
        local,
        mesh=fine,
        in_specs=(
            P(names, None), P(names, None), P(names, None), P(names, None),
            P(names, None), P(names, None),
            P(names[1:], None, None), P(names[1:], None, None), P(names[1:], None, None),
            P(), P(names, None), P(names), P(), P(),
        ),
        out_specs=(P(names), P(names)),
        check_vma=False,
    )
```

```python
import functools
import math

import jax
import jax.numpy as jnp
from jax import lax
from jax.experimental import pallas as pl
from jax.experimental.pallas import tpu as pltpu
from jax.sharding import Mesh, PartitionSpec as P

MIB = 1 << 20
LOW = -1e30


def round_up(value, step):
    return -(-value // step) * step


def largest_tile(rows, limit, step):
    best = rows
    for tile in range(step, min(rows, limit) + 1, step):
        if rows % tile == 0:
            best = tile
    return best


def pack_kernel(pol_ref, ref_ref, pol_routes, ref_routes, pol_gates, ref_gates, out_ref, room):
    tokens, width = pol_ref.shape
    experts = (room.shape[1] - width) // 2
    parts = ((pol_ref, pol_routes, pol_gates), (ref_ref, ref_routes, ref_gates))
    for index, (hidden, routes, gates) in enumerate(parts):
        band = pl.ds(index * tokens, tokens)
        room[band, :width] = hidden[...].astype(jnp.float32)
        expert = lax.broadcasted_iota(jnp.int32, (experts, tokens), 0)
        dense = jnp.zeros((experts, tokens), jnp.float32)
        for k in range(routes.shape[0]):
            dense = jnp.where(expert == routes[pl.ds(k, 1), :], gates[pl.ds(k, 1), :], dense)
        high = dense.astype(jnp.bfloat16).astype(jnp.float32)
        table = jnp.concatenate((high, dense - high), axis=0)
        room[band, width:] = table.T
    out_ref[...] = room[...].astype(jnp.bfloat16)


def pack_rows(pol_hidden, ref_hidden, pol_routes, ref_routes, pol_gates, ref_gates, experts):
    tokens, width = pol_hidden.shape
    shape = (2 * tokens, width + 2 * experts)
    return pl.pallas_call(
        pack_kernel,
        out_shape=jax.ShapeDtypeStruct(shape, jnp.bfloat16),
        scratch_shapes=[pltpu.VMEM(shape, jnp.float32)],
        compiler_params=pltpu.CompilerParams(vmem_limit_bytes=58 * MIB),
    )(pol_hidden, ref_hidden, pol_routes.T, ref_routes.T, pol_gates.T, ref_gates.T)


def expert_kernel(block, slots, width, experts, chips, place_ref, early_ref, *refs):
    del early_ref
    count = 2 * chips
    blocks, refs = refs[:count], refs[count:]
    gate_ref, up_ref, down_ref, keep_ref, give_ref = refs[:5]
    rows_in, table, pick, mix_hi, mix_lo, picked, made = refs[5:]
    step = pl.program_id(0)
    last = pl.num_programs(0) - 1
    rows = rows_in.shape[0]
    share = rows // count
    local_experts = pick.shape[0] // slots
    chip, core = place_ref[0], place_ref[1]

    @pl.when(step == 0)
    def _():
        for index, ref in enumerate(blocks):
            owner = 2 * (chip ^ (index % chips)) + (core ^ (index // chips))
            rows_in[pl.ds(pl.multiple_of(owner * share, 16), share), :] = ref[...]
        gates = rows_in[:, width:].astype(jnp.float32).T
        hits = (gates > 0.0).astype(jnp.bfloat16)
        span = math.gcd(rows, 16 * block)
        before = lax.broadcasted_iota(jnp.int32, (span, span), 0)
        after = lax.broadcasted_iota(jnp.int32, (1, span), 1)
        first = after - after % block
        order = ((before < after) & (before >= first)).astype(jnp.bfloat16)
        per_block = slots // (rows // block)
        for start in range(0, rows, span):
            band = slice(start, start + span)
            rank = jnp.dot(hits[:, band], order, preferred_element_type=jnp.float32)
            slot = rank + ((start + after) // block * per_block).astype(jnp.float32)
            table[0, :, band] = jnp.where(gates[:, band] > 0.0, slot, -1.0)
        table[1] = gates
        spot = lax.broadcasted_iota(jnp.int32, (slots, rows), 0).astype(jnp.float32)
        for e in range(local_experts):
            row = (2 * chip + core) * local_experts + e
            chosen = table[0, pl.ds(row, 1), :] == spot
            band = pl.ds(e * slots, slots)
            pick[band, :] = jnp.where(chosen, 1.0, 0.0).astype(jnp.bfloat16)
            mix_hi[band, :] = jnp.where(chosen, table[1, pl.ds(row, 1), :], 0.0).astype(
                jnp.bfloat16
            )
            mix_lo[band, :] = jnp.where(
                chosen, table[1, pl.ds(row + experts, 1), :], 0.0
            ).astype(jnp.bfloat16)
        picked[...] = jnp.dot(
            pick[...], rows_in[:, :width], preferred_element_type=jnp.float32
        ).astype(jnp.bfloat16)

    band = pl.ds(pl.multiple_of(step * slots, slots), slots)
    mine = picked[band, :]
    gate_act = jnp.dot(mine, gate_ref[0], preferred_element_type=jnp.float32)
    up_act = jnp.dot(mine, up_ref[0], preferred_element_type=jnp.float32)
    inner = (gate_act / (1.0 + jnp.exp(-gate_act)) * up_act).astype(jnp.bfloat16)
    made[band, :] = jnp.dot(inner, down_ref[0], preferred_element_type=jnp.float32).astype(
        jnp.bfloat16
    )

    @pl.when(step == last)
    def _():
        over_slots = (((0,), (0,)), ((), ()))
        span = math.gcd(rows, 16 * block)
        for start in range(0, rows, span):
            band = pl.ds(start, span)
            total = lax.dot_general(
                mix_hi[:, band], made[...], over_slots, preferred_element_type=jnp.float32
            )
            total += lax.dot_general(
                mix_lo[:, band], made[...], over_slots, preferred_element_type=jnp.float32
            )
            for index in range(span // share):
                c, owner = divmod(start // share + index, 2)
                target = total[index * share:(index + 1) * share]

                @pl.when(core == owner)
                def _():
                    keep_ref[c ^ chip] = target

                @pl.when(core != owner)
                def _():
                    give_ref[c ^ chip] = target


def expert_sums(place, early, blocks, w_gate, w_up, w_down, block, capacity, width, experts):
    count = len(blocks)
    share, wide = blocks[0].shape
    rows = count * share
    local_experts, _, hidden = w_gate.shape
    slots = round_up(capacity, 8) * (rows // block)
    every = local_experts * slots
    half = jax.ShapeDtypeStruct((count // 2, share, width), jnp.float32)
    whole = pl.BlockSpec(
        (share, wide), lambda e, place: (0, 0), pipeline_mode=pl.Buffered(1)
    )
    return pl.pallas_call(
        functools.partial(expert_kernel, block, slots, width, experts, count // 2),
        out_shape=(half, half),
        grid_spec=pltpu.PrefetchScalarGridSpec(
            num_scalar_prefetch=1,
            grid=(local_experts,),
            in_specs=[pl.BlockSpec(memory_space=pl.ANY)] + [whole] * count + [
                pl.BlockSpec((1, width, hidden), lambda e, place: (e, 0, 0)),
                pl.BlockSpec((1, width, hidden), lambda e, place: (e, 0, 0)),
                pl.BlockSpec((1, hidden, width), lambda e, place: (e, 0, 0)),
            ],
            out_specs=(
                pl.BlockSpec(
                    half.shape, lambda e, place: (0, 0, 0), pipeline_mode=pl.Buffered(1)
                ),
                pl.BlockSpec(
                    half.shape, lambda e, place: (0, 0, 0), pipeline_mode=pl.Buffered(1)
                ),
            ),
            scratch_shapes=[
                pltpu.VMEM((rows, wide), jnp.bfloat16),
                pltpu.VMEM((2, wide - width, rows), jnp.float32),
                pltpu.VMEM((every, rows), jnp.bfloat16),
                pltpu.VMEM((every, rows), jnp.bfloat16),
                pltpu.VMEM((every, rows), jnp.bfloat16),
                pltpu.VMEM((every, width), jnp.bfloat16),
                pltpu.VMEM((every, width), jnp.bfloat16),
            ],
        ),
        compiler_params=pltpu.CompilerParams(vmem_limit_bytes=58 * MIB),
        cost_estimate=pl.CostEstimate(
            flops=2 * every * width * (3 * hidden + 3 * rows),
            bytes_accessed=w_gate.size * 6 + rows * wide * 2 + rows * width * 4,
            transcendentals=every * hidden,
        ),
    )(place, early, *blocks, w_gate, w_up, w_down)


def pair_kernel(keep_ref, came_ref, own_ref, *sends):
    own_ref[...] = keep_ref[0] + came_ref[0]
    for index, send in enumerate(sends):
        send[...] = keep_ref[index + 1] + came_ref[index + 1]


def pair_sums(keep, came):
    chips, share, width = keep.shape
    own = jax.ShapeDtypeStruct((share, width), jnp.float32)
    return pl.pallas_call(
        pair_kernel,
        out_shape=(own,) * chips,
        compiler_params=pltpu.CompilerParams(vmem_limit_bytes=58 * MIB),
    )(keep, came)


def norm_kernel(hidden_ref, gain_ref, own_ref, *refs):
    width = own_ref.shape[1]
    mixed = hidden_ref[:, :width].astype(jnp.float32) + own_ref[...]
    for ref in refs[:-1]:
        mixed += ref[...]
    scale = lax.rsqrt(jnp.mean(mixed * mixed, axis=1, keepdims=True) + 1e-06)
    refs[-1][...] = (mixed * scale * gain_ref[...]).astype(jnp.bfloat16)


def norm_rows(hidden, gain, own, others):
    return pl.pallas_call(
        norm_kernel,
        out_shape=jax.ShapeDtypeStruct(own.shape, jnp.bfloat16),
        compiler_params=pltpu.CompilerParams(vmem_limit_bytes=58 * MIB),
    )(hidden, gain.reshape(1, -1), own, *others)


def head_kernel(count, before, spots_ref, wanted_ref, *refs):
    blocks, refs = refs[:count], refs[count:]
    earlier, refs = refs[:before], refs[before:]
    head_a, head_b, out_ref, rows_in, peak, total, found, logits_a, logits_b = refs
    step = pl.program_id(0)
    last = pl.num_programs(0) - 1
    tile, columns = logits_a.shape
    share = out_ref.shape[2]
    base_a, base_b = spots_ref[0], spots_ref[1]

    def product(head_ref, logits):
        logits[...] = lax.dot_general(
            head_ref[...], rows_in[...], (((1,), (1,)), ((), ())),
            preferred_element_type=jnp.float32,
        )

    def absorb(logits, first):
        for start in range(0, columns, 128):
            lanes = min(128, columns - start)
            band = pl.ds(start, lanes)
            row = lax.broadcasted_iota(jnp.int32, (tile, lanes), 0)
            values = logits[:, band]
            old = peak[:, band]
            new = jnp.maximum(old, jnp.max(values.reshape(tile // 8, 8, lanes), axis=0))
            grown = jnp.exp(values.reshape(tile // 8, 8, lanes) - new[None])
            total[:, band] = total[:, band] * jnp.exp(old - new) + jnp.sum(grown, axis=0)
            same = row == wanted_ref[:, band] - first
            kept = jnp.where(same, values, 0.0).reshape(tile // 8, 8, lanes)
            found[:, band] += jnp.sum(kept, axis=0)
            peak[:, band] = new

    @pl.when(step == 0)
    def _():
        start = 0
        for ref in blocks:
            rows_in[start:start + ref.shape[0], :] = ref[...]
            start += ref.shape[0]
        peak[...] = jnp.full_like(peak, LOW)
        total[...] = jnp.zeros_like(total)
        found[...] = jnp.zeros_like(found)
        logits_b[...] = jnp.full_like(logits_b, LOW)

    product(head_a, logits_a)
    absorb(logits_b, jnp.where(step == 0, -(1 << 28), base_b + (step - 1) * tile))
    product(head_b, logits_b)
    absorb(logits_a, base_a + step * tile)

    @pl.when(step == last)
    def _():
        absorb(logits_b, base_b + step * tile)
        top = jnp.max(peak[...], axis=0, keepdims=True)
        full = jnp.sum(total[...] * jnp.exp(peak[...] - top), axis=0, keepdims=True)
        lse = top + jnp.log(full)
        hit = jnp.sum(found[...], axis=0, keepdims=True)
        done = 0
        for ref in earlier:
            for index in range(ref.shape[0]):
                out_ref[spots_ref[2 + done + index]] = ref[index]
            done += ref.shape[0]
        for index in range(columns // share):
            band = slice(index * share, (index + 1) * share)
            spot = spots_ref[2 + done + index]
            out_ref[spot, 0:1, :] = lse[:, band]
            out_ref[spot, 1:2, :] = hit[:, band]


def head_stats(spots, wanted, blocks, earlier, head_a, head_b, share):
    places = spots.shape[0] - 2
    rows = sum(block.shape[0] for block in blocks)
    width = head_a.shape[1]
    tile = largest_tile(head_a.shape[0], 608 * 1280 // rows, 16)
    steps = head_a.shape[0] // tile
    return pl.pallas_call(
        functools.partial(head_kernel, len(blocks), len(earlier)),
        out_shape=jax.ShapeDtypeStruct((places, 2, share), jnp.float32),
        grid_spec=pltpu.PrefetchScalarGridSpec(
            num_scalar_prefetch=1,
            grid=(steps,),
            in_specs=[pl.BlockSpec((1, rows), lambda s, spots: (0, 0))] + [
                pl.BlockSpec(block.shape, lambda s, spots: (0, 0), pipeline_mode=pl.Buffered(1))
                for block in blocks
            ] + [
                pl.BlockSpec(part.shape, lambda s, spots: (0, 0, 0)) for part in earlier
            ] + [
                pl.BlockSpec((tile, width), lambda s, spots: (s, 0)),
                pl.BlockSpec((tile, width), lambda s, spots: (s, 0)),
            ],
            out_specs=pl.BlockSpec((places, 2, share), lambda s, spots: (0, 0, 0)),
            scratch_shapes=[
                pltpu.VMEM((rows, width), jnp.bfloat16),
                pltpu.VMEM((8, rows), jnp.float32),
                pltpu.VMEM((8, rows), jnp.float32),
                pltpu.VMEM((8, rows), jnp.float32),
                pltpu.VMEM((tile, rows), jnp.float32),
                pltpu.VMEM((tile, rows), jnp.float32),
            ],
        ),
        compiler_params=pltpu.CompilerParams(vmem_limit_bytes=58 * MIB),
        cost_estimate=pl.CostEstimate(
            flops=4 * rows * width * head_a.shape[0],
            bytes_accessed=head_a.size * 4 + rows * width * 2,
            transcendentals=2 * rows * head_a.shape[0],
        ),
    )(spots, wanted, *blocks, *earlier, head_a, head_b)


def combine(parts):
    top = functools.reduce(jnp.maximum, [part[:, 0] for part in parts])
    total = sum(jnp.exp(part[:, 0] - top) for part in parts)
    return top + jnp.log(total), sum(part[:, 1] for part in parts)


def across(value, offset):
    chips = lax.axis_size("chip")
    return lax.ppermute(value, "chip", [(c, c ^ offset) for c in range(chips)])


def along(value, offset):
    groups = lax.axis_size("grp")
    return lax.ppermute(value, "grp", [(g, (g + offset) % groups) for g in range(groups)])


def partner(value):
    return lax.ppermute(value, "core", ((0, 1), (1, 0)))


def local(
    pol_hidden, ref_hidden, pol_routes, ref_routes, pol_gates, ref_gates,
    w_gate, w_up, w_down, norm_gain, vocab_head, targets, seq_lengths, owners,
):
    chip, core, group = lax.axis_index("chip"), lax.axis_index("core"), lax.axis_index("grp")
    chips, groups = lax.axis_size("chip"), lax.axis_size("grp")
    device = (group * chips + chip) * 2 + core
    experts = w_gate.shape[0] * chips * 2
    tokens, width = pol_hidden.shape
    share = 2 * tokens
    capacity = tokens * pol_routes.shape[1] // experts + 2
    vocab_rows = vocab_head.shape[0]
    offsets = range(1, chips)

    send = pack_rows(
        pol_hidden, ref_hidden, pol_routes, ref_routes, pol_gates, ref_gates, experts
    )
    plane = [send] + [across(send, d) for d in offsets]
    plane = plane + [partner(rows) for rows in plane]

    home = (group - jnp.arange(groups, dtype=jnp.int32)) % groups
    spots = home[None, :] * chips + (chip ^ jnp.arange(chips, dtype=jnp.int32))[:, None]
    spots = spots.reshape(-1)
    goal = jnp.broadcast_to(targets[None], (groups * chips, tokens))
    goal = lax.all_to_all(goal, ("grp", "chip"), split_axis=0, concat_axis=0, tiled=True)
    place = spots[:, None] == jnp.arange(groups * chips, dtype=jnp.int32)[None, :]
    goal = jnp.sum(jnp.where(place[:, :, None], goal[None], 0), axis=1)
    wanted = jnp.concatenate((goal, goal), axis=1).reshape(1, -1)
    other_head = partner(vocab_head)

    place = jnp.stack((chip, core)).astype(jnp.int32)
    keep, give = expert_sums(
        place, wanted, plane, w_gate, w_up, w_down, tokens, capacity, width, experts
    )
    own, *sends = pair_sums(keep, partner(give))
    came = [across(rows, d) for d, rows in zip(offsets, sends)]
    normed = norm_rows(send, norm_gain, own, came)

    column = [normed] + [along(normed, k) for k in range(1, groups)]
    if chips == 4:
        near = [across(rows, 1) for rows in column]
        far = [across(rows, 2) for rows in column]
        half = groups // 2
        cross = [across(rows, 2) for rows in near[:half]] + [
            across(rows, 1) for rows in far[half:]
        ]
    else:
        column = jnp.concatenate(column, axis=0)
        blocks = [column] + [across(column, d) for d in offsets]
    base = jnp.stack((device, device + 1 - 2 * core)).astype(jnp.int32) * vocab_rows
    lines = groups * share
    fixed = jnp.arange(groups * chips, dtype=jnp.int32)

    def stats_of(spots, start, blocks, earlier):
        end = start + sum(block.shape[0] for block in blocks)
        spots = jnp.concatenate((base, spots))
        return head_stats(
            spots, wanted[:, start:end], blocks, earlier, vocab_head, other_head, share
        )

    if chips == 4:
        first = stats_of(fixed[:groups], 0, column, ())
        second = stats_of(fixed[:3 * groups], lines, near + far, (first,))
        stats = stats_of(spots, 3 * lines, cross, (second,))
    else:
        pieces = [
            stats_of(fixed[:groups], d * lines, [block], ()) for d, block in enumerate(blocks)
        ]
        pieces = jnp.concatenate(pieces, axis=0)
        stats = jnp.zeros_like(pieces).at[spots].set(pieces)

    lse, hit = combine([stats] + [along(stats, k) for k in range(1, groups)])
    stats = jnp.stack((lse, hit), axis=1)
    lse, hit = combine([stats] + [across(stats, d) for d in offsets])
    logprob = hit - lse
    ratio = logprob[:, :tokens] - logprob[:, tokens:]
    other = partner(ratio)
    token_ratio = lax.dynamic_index_in_dim(ratio, group * chips + chip, keepdims=False)

    mine = owners == device
    ends = jnp.cumsum(seq_lengths)
    length = jnp.sum(jnp.where(mine, seq_lengths, 0))
    end = jnp.sum(jnp.where(mine, ends, 0))
    row = jnp.arange(groups * chips, dtype=jnp.int32)[:, None]
    lane = jnp.arange(tokens, dtype=jnp.int32)[None, :]
    position = (2 * row + core) * tokens + lane
    inside = (position >= end - length) & (position < end)
    position = (2 * row + 1 - core) * tokens + lane
    inside_other = (position >= end - length) & (position < end)
    mean = jnp.sum(jnp.where(inside, ratio, 0.0) + jnp.where(inside_other, other, 0.0))
    return (token_ratio, (mean / length.astype(jnp.float32)).reshape(1))


def solution(mesh):
    names = ("grp", "chip", "core")
    groups, plane = mesh.devices.shape
    fine = Mesh(mesh.devices.reshape(groups, plane // 2, 2), names)
    return jax.shard_map(
        local,
        mesh=fine,
        in_specs=(
            P(names, None), P(names, None), P(names, None), P(names, None),
            P(names, None), P(names, None),
            P(names[1:], None, None), P(names[1:], None, None), P(names[1:], None, None),
            P(), P(names, None), P(names), P(), P(),
        ),
        out_specs=(P(names), P(names)),
        check_vma=False,
    )
```

```python
import functools
import math

import jax
import jax.numpy as jnp
from jax import lax
from jax.experimental import pallas as pl
from jax.experimental.pallas import tpu as pltpu
from jax.sharding import Mesh, PartitionSpec as P

MIB = 1 << 20
LOW = -1e30


def round_up(value, step):
    return -(-value // step) * step


def largest_tile(rows, limit, step):
    best = rows
    for tile in range(step, min(rows, limit) + 1, step):
        if rows % tile == 0:
            best = tile
    return best


def pack_kernel(pol_ref, ref_ref, pol_routes, ref_routes, pol_gates, ref_gates, out_ref, room):
    tokens, width = pol_ref.shape
    experts = (room.shape[1] - width) // 2
    parts = ((pol_ref, pol_routes, pol_gates), (ref_ref, ref_routes, ref_gates))
    for index, (hidden, routes, gates) in enumerate(parts):
        band = pl.ds(index * tokens, tokens)
        room[band, :width] = hidden[...].astype(jnp.float32)
        expert = lax.broadcasted_iota(jnp.int32, (experts, tokens), 0)
        dense = jnp.zeros((experts, tokens), jnp.float32)
        for k in range(routes.shape[0]):
            dense = jnp.where(expert == routes[pl.ds(k, 1), :], gates[pl.ds(k, 1), :], dense)
        high = dense.astype(jnp.bfloat16).astype(jnp.float32)
        table = jnp.concatenate((high, dense - high), axis=0)
        room[band, width:] = table.T
    out_ref[...] = room[...].astype(jnp.bfloat16)


def pack_rows(pol_hidden, ref_hidden, pol_routes, ref_routes, pol_gates, ref_gates, experts):
    tokens, width = pol_hidden.shape
    shape = (2 * tokens, width + 2 * experts)
    return pl.pallas_call(
        pack_kernel,
        out_shape=jax.ShapeDtypeStruct(shape, jnp.bfloat16),
        scratch_shapes=[pltpu.VMEM(shape, jnp.float32)],
        compiler_params=pltpu.CompilerParams(vmem_limit_bytes=58 * MIB),
    )(pol_hidden, ref_hidden, pol_routes.T, ref_routes.T, pol_gates.T, ref_gates.T)


def expert_kernel(block, slots, width, experts, chips, place_ref, *refs):
    count = 2 * chips
    blocks, refs = refs[:count], refs[count:]
    gate_ref, up_ref, down_ref, keep_ref, give_ref = refs[:5]
    rows_in, table, pick, weight, picked, made = refs[5:]
    step = pl.program_id(0)
    last = pl.num_programs(0) - 1
    rows = rows_in.shape[0]
    share = rows // count
    local_experts = pick.shape[0] // slots
    chip, core = place_ref[0], place_ref[1]

    @pl.when(step == 0)
    def _():
        for index, ref in enumerate(blocks):
            owner = 2 * (chip ^ (index % chips)) + (core ^ (index // chips))
            rows_in[pl.ds(pl.multiple_of(owner * share, 16), share), :] = ref[...]
        gates = rows_in[:, width:].astype(jnp.float32).T
        hits = (gates > 0.0).astype(jnp.bfloat16)
        span = math.gcd(rows, 16 * block)
        before = lax.broadcasted_iota(jnp.int32, (span, span), 0)
        after = lax.broadcasted_iota(jnp.int32, (1, span), 1)
        first = after - after % block
        order = ((before < after) & (before >= first)).astype(jnp.bfloat16)
        per_block = slots // (rows // block)
        for start in range(0, rows, span):
            band = slice(start, start + span)
            rank = jnp.dot(hits[:, band], order, preferred_element_type=jnp.float32)
            slot = rank + ((start + after) // block * per_block).astype(jnp.float32)
            table[0, :, band] = jnp.where(gates[:, band] > 0.0, slot, -1.0)
        table[1] = gates
        spot = lax.broadcasted_iota(jnp.int32, (slots, rows), 0).astype(jnp.float32)
        for e in range(local_experts):
            row = (2 * chip + core) * local_experts + e
            chosen = table[0, pl.ds(row, 1), :] == spot
            band = pl.ds(e * slots, slots)
            pick[band, :] = jnp.where(chosen, 1.0, 0.0).astype(jnp.bfloat16)
            gate = table[1, pl.ds(row, 1), :] + table[1, pl.ds(row + experts, 1), :]
            weight[band, :] = jnp.sum(jnp.where(chosen, gate, 0.0), axis=1, keepdims=True)
        picked[...] = jnp.dot(
            pick[...], rows_in[:, :width], preferred_element_type=jnp.float32
        ).astype(jnp.bfloat16)

    band = pl.ds(pl.multiple_of(step * slots, slots), slots)
    mine = picked[band, :]
    gate_act = jnp.dot(mine, gate_ref[0], preferred_element_type=jnp.float32)
    up_act = jnp.dot(mine, up_ref[0], preferred_element_type=jnp.float32)
    inner = (gate_act / (1.0 + jnp.exp(-gate_act)) * up_act).astype(jnp.bfloat16)
    output = jnp.dot(inner, down_ref[0], preferred_element_type=jnp.float32).astype(jnp.bfloat16)
    scaled = output.astype(jnp.float32) * weight[band, :]
    high = scaled.astype(jnp.bfloat16)
    made[band, :width] = high
    made[band, width:] = (scaled - high.astype(jnp.float32)).astype(jnp.bfloat16)

    @pl.when(step == last)
    def _():
        over_slots = (((0,), (0,)), ((), ()))
        span = math.gcd(rows, 16 * block)
        for start in range(0, rows, span):
            band = pl.ds(start, span)
            total = lax.dot_general(
                pick[:, band], made[...], over_slots, preferred_element_type=jnp.float32
            )
            total = total[:, :width] + total[:, width:]
            for index in range(span // share):
                c, owner = divmod(start // share + index, 2)
                target = total[index * share:(index + 1) * share]

                @pl.when(core == owner)
                def _():
                    keep_ref[c ^ chip] = target

                @pl.when(core != owner)
                def _():
                    give_ref[c ^ chip] = target


def expert_sums(place, blocks, w_gate, w_up, w_down, block, capacity, width, experts):
    count = len(blocks)
    share, wide = blocks[0].shape
    rows = count * share
    local_experts, _, hidden = w_gate.shape
    slots = round_up(capacity, 8) * (rows // block)
    every = local_experts * slots
    half = jax.ShapeDtypeStruct((count // 2, share, width), jnp.float32)
    whole = pl.BlockSpec(
        (share, wide), lambda e, place: (0, 0), pipeline_mode=pl.Buffered(1)
    )
    return pl.pallas_call(
        functools.partial(expert_kernel, block, slots, width, experts, count // 2),
        out_shape=(half, half),
        grid_spec=pltpu.PrefetchScalarGridSpec(
            num_scalar_prefetch=1,
            grid=(local_experts,),
            in_specs=[whole] * count + [
                pl.BlockSpec((1, width, hidden), lambda e, place: (e, 0, 0)),
                pl.BlockSpec((1, width, hidden), lambda e, place: (e, 0, 0)),
                pl.BlockSpec((1, hidden, width), lambda e, place: (e, 0, 0)),
            ],
            out_specs=(
                pl.BlockSpec(
                    half.shape, lambda e, place: (0, 0, 0), pipeline_mode=pl.Buffered(1)
                ),
                pl.BlockSpec(
                    half.shape, lambda e, place: (0, 0, 0), pipeline_mode=pl.Buffered(1)
                ),
            ),
            scratch_shapes=[
                pltpu.VMEM((rows, wide), jnp.bfloat16),
                pltpu.VMEM((2, wide - width, rows), jnp.float32),
                pltpu.VMEM((every, rows), jnp.bfloat16),
                pltpu.VMEM((every, 1), jnp.float32),
                pltpu.VMEM((every, width), jnp.bfloat16),
                pltpu.VMEM((every, 2 * width), jnp.bfloat16),
            ],
        ),
        compiler_params=pltpu.CompilerParams(
            vmem_limit_bytes=(36 if rows <= 640 else 58) * MIB
        ),
        cost_estimate=pl.CostEstimate(
            flops=2 * every * width * (3 * hidden + 3 * rows),
            bytes_accessed=w_gate.size * 6 + rows * wide * 2 + rows * width * 4,
            transcendentals=every * hidden,
        ),
    )(place, *blocks, w_gate, w_up, w_down)


def pair_kernel(keep_ref, came_ref, targets_ref, goal_ref, *sums):
    for index, total in enumerate(sums):
        total[...] = keep_ref[index] + came_ref[index]
    goal_ref[...] = jnp.broadcast_to(targets_ref[...], goal_ref.shape)


def pair_sums(keep, came, targets, peers):
    chips, share, width = keep.shape
    part = jax.ShapeDtypeStruct((share, width), jnp.float32)
    goal = jax.ShapeDtypeStruct((peers, targets.shape[0]), jnp.int32)
    return pl.pallas_call(
        pair_kernel,
        out_shape=(goal,) + (part,) * chips,
        compiler_params=pltpu.CompilerParams(vmem_limit_bytes=24 * MIB),
    )(keep, came, targets.reshape(1, -1))


def norm_kernel(hidden_ref, gain_ref, early_ref, own_ref, *refs):
    del early_ref
    width = own_ref.shape[1]
    mixed = hidden_ref[:, :width].astype(jnp.float32) + own_ref[...]
    for ref in refs[:-1]:
        mixed += ref[...]
    scale = lax.rsqrt(jnp.mean(mixed * mixed, axis=1, keepdims=True) + 1e-06)
    refs[-1][...] = (mixed * scale * gain_ref[...]).astype(jnp.bfloat16)


def norm_rows(hidden, gain, early, own, others):
    return pl.pallas_call(
        norm_kernel,
        out_shape=jax.ShapeDtypeStruct(own.shape, jnp.bfloat16),
        compiler_params=pltpu.CompilerParams(vmem_limit_bytes=16 * MIB),
    )(hidden, gain.reshape(1, -1), early, own, *others)


def head_kernel(count, before, spots_ref, wanted_ref, *refs):
    blocks, refs = refs[:count], refs[count:]
    earlier, refs = refs[:before], refs[before:]
    head_a, head_b, out_ref, rows_in, peak, total, found, logits_a, logits_b = refs
    step = pl.program_id(0)
    last = pl.num_programs(0) - 1
    tile, columns = logits_a.shape
    share = out_ref.shape[2]
    base_a, base_b = spots_ref[0], spots_ref[1]

    def product(head_ref, logits):
        logits[...] = lax.dot_general(
            head_ref[...], rows_in[...], (((1,), (1,)), ((), ())),
            preferred_element_type=jnp.float32,
        )

    def absorb(logits, first):
        for start in range(0, columns, 128):
            lanes = min(128, columns - start)
            band = pl.ds(start, lanes)
            row = lax.broadcasted_iota(jnp.int32, (tile, lanes), 0)
            values = logits[:, band]
            old = peak[:, band]
            new = jnp.maximum(old, jnp.max(values.reshape(tile // 8, 8, lanes), axis=0))
            grown = jnp.exp(values.reshape(tile // 8, 8, lanes) - new[None])
            total[:, band] = total[:, band] * jnp.exp(old - new) + jnp.sum(grown, axis=0)
            same = row == wanted_ref[:, band] - first
            kept = jnp.where(same, values, 0.0).reshape(tile // 8, 8, lanes)
            found[:, band] += jnp.sum(kept, axis=0)
            peak[:, band] = new

    @pl.when(step == 0)
    def _():
        start = 0
        for ref in blocks:
            rows_in[start:start + ref.shape[0], :] = ref[...]
            start += ref.shape[0]
        peak[...] = jnp.full_like(peak, LOW)
        total[...] = jnp.zeros_like(total)
        found[...] = jnp.zeros_like(found)
        logits_b[...] = jnp.full_like(logits_b, LOW)

    product(head_a, logits_a)
    absorb(logits_b, jnp.where(step == 0, -(1 << 28), base_b + (step - 1) * tile))
    product(head_b, logits_b)
    absorb(logits_a, base_a + step * tile)

    @pl.when(step == last)
    def _():
        absorb(logits_b, base_b + step * tile)
        top = jnp.max(peak[...], axis=0, keepdims=True)
        full = jnp.sum(total[...] * jnp.exp(peak[...] - top), axis=0, keepdims=True)
        lse = top + jnp.log(full)
        hit = jnp.sum(found[...], axis=0, keepdims=True)
        done = 0
        for ref in earlier:
            for index in range(ref.shape[0]):
                out_ref[spots_ref[2 + done + index]] = ref[index]
            done += ref.shape[0]
        for index in range(columns // share):
            band = slice(index * share, (index + 1) * share)
            spot = spots_ref[2 + done + index]
            out_ref[spot, 0:1, :] = lse[:, band]
            out_ref[spot, 1:2, :] = hit[:, band]


def head_stats(spots, wanted, blocks, earlier, head_a, head_b, share):
    places = spots.shape[0] - 2
    rows = sum(block.shape[0] for block in blocks)
    width = head_a.shape[1]
    tile = largest_tile(head_a.shape[0], 608, 16)
    steps = head_a.shape[0] // tile
    return pl.pallas_call(
        functools.partial(head_kernel, len(blocks), len(earlier)),
        out_shape=jax.ShapeDtypeStruct((places, 2, share), jnp.float32),
        grid_spec=pltpu.PrefetchScalarGridSpec(
            num_scalar_prefetch=1,
            grid=(steps,),
            in_specs=[pl.BlockSpec((1, rows), lambda s, spots: (0, 0))] + [
                pl.BlockSpec(block.shape, lambda s, spots: (0, 0), pipeline_mode=pl.Buffered(1))
                for block in blocks
            ] + [
                pl.BlockSpec(part.shape, lambda s, spots: (0, 0, 0)) for part in earlier
            ] + [
                pl.BlockSpec((tile, width), lambda s, spots: (s, 0)),
                pl.BlockSpec((tile, width), lambda s, spots: (s, 0)),
            ],
            out_specs=pl.BlockSpec((places, 2, share), lambda s, spots: (0, 0, 0)),
            scratch_shapes=[
                pltpu.VMEM((rows, width), jnp.bfloat16),
                pltpu.VMEM((8, rows), jnp.float32),
                pltpu.VMEM((8, rows), jnp.float32),
                pltpu.VMEM((8, rows), jnp.float32),
                pltpu.VMEM((tile, rows), jnp.float32),
                pltpu.VMEM((tile, rows), jnp.float32),
            ],
        ),
        compiler_params=pltpu.CompilerParams(vmem_limit_bytes=58 * MIB),
        cost_estimate=pl.CostEstimate(
            flops=4 * rows * width * head_a.shape[0],
            bytes_accessed=head_a.size * 4 + rows * width * 2,
            transcendentals=2 * rows * head_a.shape[0],
        ),
    )(spots, wanted, *blocks, *earlier, head_a, head_b)


def combine(parts):
    top = functools.reduce(jnp.maximum, [part[:, 0] for part in parts])
    total = sum(jnp.exp(part[:, 0] - top) for part in parts)
    return top + jnp.log(total), sum(part[:, 1] for part in parts)


def across(value, offset):
    chips = lax.axis_size("chip")
    return lax.ppermute(value, "chip", [(c, c ^ offset) for c in range(chips)])


def along(value, offset):
    groups = lax.axis_size("grp")
    return lax.ppermute(value, "grp", [(g, (g + offset) % groups) for g in range(groups)])


def partner(value):
    return lax.ppermute(value, "core", ((0, 1), (1, 0)))


def local(
    pol_hidden, ref_hidden, pol_routes, ref_routes, pol_gates, ref_gates,
    w_gate, w_up, w_down, norm_gain, vocab_head, targets, seq_lengths, owners,
):
    chip, core, group = lax.axis_index("chip"), lax.axis_index("core"), lax.axis_index("grp")
    chips, groups = lax.axis_size("chip"), lax.axis_size("grp")
    device = (group * chips + chip) * 2 + core
    experts = w_gate.shape[0] * chips * 2
    tokens, width = pol_hidden.shape
    share = 2 * tokens
    capacity = tokens * pol_routes.shape[1] // experts + 2
    vocab_rows = vocab_head.shape[0]
    offsets = range(1, chips)

    send = pack_rows(
        pol_hidden, ref_hidden, pol_routes, ref_routes, pol_gates, ref_gates, experts
    )
    plane = [send] + [across(send, d) for d in offsets]
    plane = plane + [partner(rows) for rows in plane]

    home = (group - jnp.arange(groups, dtype=jnp.int32)) % groups
    spots = home[None, :] * chips + (chip ^ jnp.arange(chips, dtype=jnp.int32))[:, None]
    spots = spots.reshape(-1)
    other_head = partner(vocab_head)

    place = jnp.stack((chip, core)).astype(jnp.int32)
    keep, give = expert_sums(place, plane, w_gate, w_up, w_down, tokens, capacity, width, experts)
    goal, own, *sends = pair_sums(keep, partner(give), targets, groups * chips)
    came = [across(rows, d) for d, rows in zip(offsets, sends)]
    goal = lax.all_to_all(goal, ("grp", "chip"), split_axis=0, concat_axis=0, tiled=True)
    match = spots[:, None] == jnp.arange(groups * chips, dtype=jnp.int32)[None, :]
    goal = jnp.sum(jnp.where(match[:, :, None], goal[None], 0), axis=1)
    wanted = jnp.concatenate((goal, goal), axis=1).reshape(1, -1)
    normed = norm_rows(send, norm_gain, wanted, own, came)

    column = [normed] + [along(normed, k) for k in range(1, groups)]
    if chips == 4:
        near = [across(rows, 1) for rows in column]
        far = [across(rows, 2) for rows in column]
        half = groups // 2
        cross = [across(rows, 2) for rows in near[:half]] + [
            across(rows, 1) for rows in far[half:]
        ]
    else:
        column = jnp.concatenate(column, axis=0)
        blocks = [column] + [across(column, d) for d in offsets]
    base = jnp.stack((device, device + 1 - 2 * core)).astype(jnp.int32) * vocab_rows
    lines = groups * share
    fixed = jnp.arange(groups * chips, dtype=jnp.int32)

    def stats_of(spots, start, blocks, earlier):
        end = start + sum(block.shape[0] for block in blocks)
        spots = jnp.concatenate((base, spots))
        return head_stats(
            spots, wanted[:, start:end], blocks, earlier, vocab_head, other_head, share
        )

    if chips == 4:
        first = stats_of(fixed[:groups], 0, column, ())
        second = stats_of(fixed[:3 * groups], lines, near + far, (first,))
        stats = stats_of(spots, 3 * lines, cross, (second,))
    else:
        pieces = [
            stats_of(fixed[:groups], d * lines, [block], ()) for d, block in enumerate(blocks)
        ]
        pieces = jnp.concatenate(pieces, axis=0)
        stats = jnp.zeros_like(pieces).at[spots].set(pieces)

    lse, hit = combine([stats] + [along(stats, k) for k in range(1, groups)])
    stats = jnp.stack((lse, hit), axis=1)
    lse, hit = combine([stats] + [across(stats, d) for d in offsets])
    logprob = hit - lse
    ratio = logprob[:, :tokens] - logprob[:, tokens:]
    other = partner(ratio)
    token_ratio = lax.dynamic_index_in_dim(ratio, group * chips + chip, keepdims=False)

    mine = owners == device
    ends = jnp.cumsum(seq_lengths)
    length = jnp.sum(jnp.where(mine, seq_lengths, 0))
    end = jnp.sum(jnp.where(mine, ends, 0))
    row = jnp.arange(groups * chips, dtype=jnp.int32)[:, None]
    lane = jnp.arange(tokens, dtype=jnp.int32)[None, :]
    position = (2 * row + core) * tokens + lane
    inside = (position >= end - length) & (position < end)
    position = (2 * row + 1 - core) * tokens + lane
    inside_other = (position >= end - length) & (position < end)
    mean = jnp.sum(jnp.where(inside, ratio, 0.0) + jnp.where(inside_other, other, 0.0))
    return (token_ratio, (mean / length.astype(jnp.float32)).reshape(1))


def solution(mesh):
    names = ("grp", "chip", "core")
    groups, plane = mesh.devices.shape
    fine = Mesh(mesh.devices.reshape(groups, plane // 2, 2), names)
    return jax.shard_map(
        local,
        mesh=fine,
        in_specs=(
            P(names, None), P(names, None), P(names, None), P(names, None),
            P(names, None), P(names, None),
            P(names[1:], None, None), P(names[1:], None, None), P(names[1:], None, None),
            P(), P(names, None), P(names), P(), P(),
        ),
        out_specs=(P(names), P(names)),
        check_vma=False,
    )
```

```python
import functools
import math

import jax
import jax.numpy as jnp
from jax import lax
from jax.experimental import pallas as pl
from jax.experimental.pallas import tpu as pltpu
from jax.sharding import Mesh, PartitionSpec as P

MIB = 1 << 20
LOW = -1e30


def round_up(value, step):
    return -(-value // step) * step


def largest_tile(rows, limit, step):
    best = rows
    for tile in range(step, min(rows, limit) + 1, step):
        if rows % tile == 0:
            best = tile
    return best


def pack_kernel(pol_ref, ref_ref, pol_routes, ref_routes, pol_gates, ref_gates, out_ref, room):
    tokens, width = pol_ref.shape
    experts = (room.shape[1] - width) // 2
    parts = ((pol_ref, pol_routes, pol_gates), (ref_ref, ref_routes, ref_gates))
    for index, (hidden, routes, gates) in enumerate(parts):
        band = pl.ds(index * tokens, tokens)
        room[band, :width] = hidden[...].astype(jnp.float32)
        expert = lax.broadcasted_iota(jnp.int32, (experts, tokens), 0)
        dense = jnp.zeros((experts, tokens), jnp.float32)
        for k in range(routes.shape[0]):
            dense = jnp.where(expert == routes[pl.ds(k, 1), :], gates[pl.ds(k, 1), :], dense)
        high = dense.astype(jnp.bfloat16).astype(jnp.float32)
        table = jnp.concatenate((high, dense - high), axis=0)
        room[band, width:] = table.T
    out_ref[...] = room[...].astype(jnp.bfloat16)


def pack_rows(pol_hidden, ref_hidden, pol_routes, ref_routes, pol_gates, ref_gates, experts):
    tokens, width = pol_hidden.shape
    shape = (2 * tokens, width + 2 * experts)
    return pl.pallas_call(
        pack_kernel,
        out_shape=jax.ShapeDtypeStruct(shape, jnp.bfloat16),
        scratch_shapes=[pltpu.VMEM(shape, jnp.float32)],
        compiler_params=pltpu.CompilerParams(vmem_limit_bytes=58 * MIB),
    )(pol_hidden, ref_hidden, pol_routes.T, ref_routes.T, pol_gates.T, ref_gates.T)


def expert_kernel(block, slots, width, experts, chips, place_ref, *refs):
    count = 2 * chips
    blocks, refs = refs[:count], refs[count:]
    gate_ref, up_ref, down_ref, keep_ref, give_ref = refs[:5]
    rows_in, table, pick, weight, picked, made = refs[5:]
    step = pl.program_id(0)
    last = pl.num_programs(0) - 1
    rows = rows_in.shape[0]
    share = rows // count
    local_experts = pick.shape[0] // slots
    chip, core = place_ref[0], place_ref[1]

    @pl.when(step == 0)
    def _():
        for index, ref in enumerate(blocks):
            owner = 2 * (chip ^ (index % chips)) + (core ^ (index // chips))
            rows_in[pl.ds(pl.multiple_of(owner * share, 16), share), :] = ref[...]
        gates = rows_in[:, width:].astype(jnp.float32).T
        hits = (gates > 0.0).astype(jnp.bfloat16)
        span = math.gcd(rows, 16 * block)
        before = lax.broadcasted_iota(jnp.int32, (span, span), 0)
        after = lax.broadcasted_iota(jnp.int32, (1, span), 1)
        first = after - after % block
        order = ((before < after) & (before >= first)).astype(jnp.bfloat16)
        per_block = slots // (rows // block)
        for start in range(0, rows, span):
            band = slice(start, start + span)
            rank = jnp.dot(hits[:, band], order, preferred_element_type=jnp.float32)
            slot = rank + ((start + after) // block * per_block).astype(jnp.float32)
            table[0, :, band] = jnp.where(gates[:, band] > 0.0, slot, -1.0)
        table[1] = gates
        spot = lax.broadcasted_iota(jnp.int32, (slots, rows), 0).astype(jnp.float32)
        for e in range(local_experts):
            row = (2 * chip + core) * local_experts + e
            chosen = table[0, pl.ds(row, 1), :] == spot
            band = pl.ds(e * slots, slots)
            pick[band, :] = jnp.where(chosen, 1.0, 0.0).astype(jnp.bfloat16)
            gate = table[1, pl.ds(row, 1), :] + table[1, pl.ds(row + experts, 1), :]
            weight[band, :] = jnp.sum(jnp.where(chosen, gate, 0.0), axis=1, keepdims=True)
        picked[...] = jnp.dot(
            pick[...], rows_in[:, :width], preferred_element_type=jnp.float32
        ).astype(jnp.bfloat16)

    band = pl.ds(pl.multiple_of(step * slots, slots), slots)
    mine = picked[band, :]
    gate_act = jnp.dot(mine, gate_ref[0], preferred_element_type=jnp.float32)
    up_act = jnp.dot(mine, up_ref[0], preferred_element_type=jnp.float32)
    inner = (gate_act / (1.0 + jnp.exp(-gate_act)) * up_act).astype(jnp.bfloat16)
    output = jnp.dot(inner, down_ref[0], preferred_element_type=jnp.float32).astype(jnp.bfloat16)
    scaled = output.astype(jnp.float32) * weight[band, :]
    high = scaled.astype(jnp.bfloat16)
    made[band, :width] = high
    made[band, width:] = (scaled - high.astype(jnp.float32)).astype(jnp.bfloat16)

    @pl.when(step == last)
    def _():
        over_slots = (((0,), (0,)), ((), ()))
        span = math.gcd(rows, 16 * block)
        for start in range(0, rows, span):
            band = pl.ds(start, span)
            total = lax.dot_general(
                pick[:, band], made[...], over_slots, preferred_element_type=jnp.float32
            )
            total = total[:, :width] + total[:, width:]
            for index in range(span // share):
                c, owner = divmod(start // share + index, 2)
                target = total[index * share:(index + 1) * share]

                @pl.when(core == owner)
                def _():
                    keep_ref[c ^ chip] = target

                @pl.when(core != owner)
                def _():
                    give_ref[c ^ chip] = target


def expert_sums(place, blocks, w_gate, w_up, w_down, block, capacity, width, experts):
    count = len(blocks)
    share, wide = blocks[0].shape
    rows = count * share
    local_experts, _, hidden = w_gate.shape
    slots = round_up(capacity, 8) * (rows // block)
    every = local_experts * slots
    half = jax.ShapeDtypeStruct((count // 2, share, width), jnp.float32)
    whole = pl.BlockSpec(
        (share, wide), lambda e, place: (0, 0), pipeline_mode=pl.Buffered(1)
    )
    return pl.pallas_call(
        functools.partial(expert_kernel, block, slots, width, experts, count // 2),
        out_shape=(half, half),
        grid_spec=pltpu.PrefetchScalarGridSpec(
            num_scalar_prefetch=1,
            grid=(local_experts,),
            in_specs=[whole] * count + [
                pl.BlockSpec((1, width, hidden), lambda e, place: (e, 0, 0)),
                pl.BlockSpec((1, width, hidden), lambda e, place: (e, 0, 0)),
                pl.BlockSpec((1, hidden, width), lambda e, place: (e, 0, 0)),
            ],
            out_specs=(
                pl.BlockSpec(
                    half.shape, lambda e, place: (0, 0, 0), pipeline_mode=pl.Buffered(1)
                ),
                pl.BlockSpec(
                    half.shape, lambda e, place: (0, 0, 0), pipeline_mode=pl.Buffered(1)
                ),
            ),
            scratch_shapes=[
                pltpu.VMEM((rows, wide), jnp.bfloat16),
                pltpu.VMEM((2, wide - width, rows), jnp.float32),
                pltpu.VMEM((every, rows), jnp.bfloat16),
                pltpu.VMEM((every, 1), jnp.float32),
                pltpu.VMEM((every, width), jnp.bfloat16),
                pltpu.VMEM((every, 2 * width), jnp.bfloat16),
            ],
        ),
        compiler_params=pltpu.CompilerParams(
            vmem_limit_bytes=(55 if rows <= 640 else 58) * MIB
        ),
        cost_estimate=pl.CostEstimate(
            flops=2 * every * width * (3 * hidden + 3 * rows),
            bytes_accessed=w_gate.size * 6 + rows * wide * 2 + rows * width * 4,
            transcendentals=every * hidden,
        ),
    )(place, *blocks, w_gate, w_up, w_down)


def pair_kernel(keep_ref, came_ref, *sums):
    for index, total in enumerate(sums):
        total[...] = keep_ref[index] + came_ref[index]


def pair_sums(keep, came):
    chips, share, width = keep.shape
    part = jax.ShapeDtypeStruct((share, width), jnp.float32)
    return pl.pallas_call(
        pair_kernel,
        out_shape=(part,) * chips,
        compiler_params=pltpu.CompilerParams(vmem_limit_bytes=24 * MIB),
    )(keep, came)


def begin_kernel(own_ref, came_ref, targets_ref, sum_ref, goal_ref):
    sum_ref[...] = own_ref[...] + came_ref[...]
    goal_ref[...] = jnp.broadcast_to(targets_ref[...], goal_ref.shape)


def begin_rows(own, came, targets, peers):
    goal = jax.ShapeDtypeStruct((peers, targets.shape[0]), jnp.int32)
    return pl.pallas_call(
        begin_kernel,
        out_shape=(jax.ShapeDtypeStruct(own.shape, own.dtype), goal),
        compiler_params=pltpu.CompilerParams(vmem_limit_bytes=16 * MIB),
    )(own, came, targets.reshape(1, -1))


def norm_kernel(hidden_ref, gain_ref, early_ref, own_ref, *refs):
    del early_ref
    width = own_ref.shape[1]
    mixed = hidden_ref[:, :width].astype(jnp.float32) + own_ref[...]
    for ref in refs[:-1]:
        mixed += ref[...]
    scale = lax.rsqrt(jnp.mean(mixed * mixed, axis=1, keepdims=True) + 1e-06)
    refs[-1][...] = (mixed * scale * gain_ref[...]).astype(jnp.bfloat16)


def norm_rows(hidden, gain, early, own, others):
    return pl.pallas_call(
        norm_kernel,
        out_shape=jax.ShapeDtypeStruct(own.shape, jnp.bfloat16),
        compiler_params=pltpu.CompilerParams(vmem_limit_bytes=16 * MIB),
    )(hidden, gain.reshape(1, -1), early, own, *others)


def head_kernel(parts, before, spots_ref, wanted_ref, *refs):
    blocks, refs = refs[:len(parts)], refs[len(parts):]
    earlier, refs = refs[:before], refs[before:]
    head_a, head_b, out_ref, rows_in, peak, total, found, logits_a, logits_b = refs
    step = pl.program_id(0)
    last = pl.num_programs(0) - 1
    tile, columns = logits_a.shape
    base_a, base_b = spots_ref[0], spots_ref[1]

    def product(head_ref, logits):
        logits[...] = lax.dot_general(
            head_ref[...], rows_in[...], (((1,), (1,)), ((), ())),
            preferred_element_type=jnp.float32,
        )

    def absorb(logits, first):
        for start in range(0, columns, 128):
            lanes = min(128, columns - start)
            band = pl.ds(start, lanes)
            row = lax.broadcasted_iota(jnp.int32, (tile, lanes), 0)
            values = logits[:, band]
            old = peak[:, band]
            new = jnp.maximum(old, jnp.max(values.reshape(tile // 8, 8, lanes), axis=0))
            grown = jnp.exp(values.reshape(tile // 8, 8, lanes) - new[None])
            total[:, band] = total[:, band] * jnp.exp(old - new) + jnp.sum(grown, axis=0)
            same = row == wanted_ref[:, band] - first
            kept = jnp.where(same, values, 0.0).reshape(tile // 8, 8, lanes)
            found[:, band] += jnp.sum(kept, axis=0)
            peak[:, band] = new

    @pl.when(step == 0)
    def _():
        start = 0
        for ref, (low, high) in zip(blocks, parts):
            rows_in[start:start + high - low, :] = ref[low:high, :]
            start += high - low
        peak[...] = jnp.full_like(peak, LOW)
        total[...] = jnp.zeros_like(total)
        found[...] = jnp.zeros_like(found)
        logits_b[...] = jnp.full_like(logits_b, LOW)

    product(head_a, logits_a)
    absorb(logits_b, jnp.where(step == 0, -(1 << 28), base_b + (step - 1) * tile))
    product(head_b, logits_b)
    absorb(logits_a, base_a + step * tile)

    @pl.when(step == last)
    def _():
        absorb(logits_b, base_b + step * tile)
        top = jnp.max(peak[...], axis=0, keepdims=True)
        full = jnp.sum(total[...] * jnp.exp(peak[...] - top), axis=0, keepdims=True)
        lse = top + jnp.log(full)
        hit = jnp.sum(found[...], axis=0, keepdims=True)
        lse = jnp.concatenate([ref[0:1, :] for ref in earlier] + [lse], axis=1)
        hit = jnp.concatenate([ref[1:2, :] for ref in earlier] + [hit], axis=1)
        if len(out_ref.shape) == 2:
            out_ref[0:1, :] = lse
            out_ref[1:2, :] = hit
        else:
            share = out_ref.shape[2]
            for index in range(out_ref.shape[0]):
                band = slice(index * share, (index + 1) * share)
                spot = spots_ref[2 + index]
                out_ref[spot, 0:1, :] = lse[:, band]
                out_ref[spot, 1:2, :] = hit[:, band]


def head_stats(spots, wanted, blocks, parts, earlier, head_a, head_b, shape):
    rows = sum(high - low for low, high in parts)
    width = head_a.shape[1]
    whole = pl.BlockSpec(shape, lambda s, spots: (0,) * len(shape))
    tile = largest_tile(head_a.shape[0], 608, 16)
    steps = head_a.shape[0] // tile
    return pl.pallas_call(
        functools.partial(head_kernel, parts, len(earlier)),
        out_shape=jax.ShapeDtypeStruct(shape, jnp.float32),
        grid_spec=pltpu.PrefetchScalarGridSpec(
            num_scalar_prefetch=1,
            grid=(steps,),
            in_specs=[pl.BlockSpec((1, rows), lambda s, spots: (0, 0))] + [
                pl.BlockSpec(block.shape, lambda s, spots: (0, 0), pipeline_mode=pl.Buffered(1))
                for block in blocks
            ] + [
                pl.BlockSpec(part.shape, lambda s, spots: (0, 0)) for part in earlier
            ] + [
                pl.BlockSpec((tile, width), lambda s, spots: (s, 0)),
                pl.BlockSpec((tile, width), lambda s, spots: (s, 0)),
            ],
            out_specs=whole,
            scratch_shapes=[
                pltpu.VMEM((rows, width), jnp.bfloat16),
                pltpu.VMEM((8, rows), jnp.float32),
                pltpu.VMEM((8, rows), jnp.float32),
                pltpu.VMEM((8, rows), jnp.float32),
                pltpu.VMEM((tile, rows), jnp.float32),
                pltpu.VMEM((tile, rows), jnp.float32),
            ],
        ),
        compiler_params=pltpu.CompilerParams(vmem_limit_bytes=58 * MIB),
        cost_estimate=pl.CostEstimate(
            flops=4 * rows * width * head_a.shape[0],
            bytes_accessed=head_a.size * 4 + rows * width * 2,
            transcendentals=2 * rows * head_a.shape[0],
        ),
    )(spots, wanted, *blocks, *earlier, head_a, head_b)


def combine(parts):
    top = functools.reduce(jnp.maximum, [part[:, 0] for part in parts])
    total = sum(jnp.exp(part[:, 0] - top) for part in parts)
    return top + jnp.log(total), sum(part[:, 1] for part in parts)


def across(value, offset):
    chips = lax.axis_size("chip")
    return lax.ppermute(value, "chip", [(c, c ^ offset) for c in range(chips)])


def along(value, offset):
    groups = lax.axis_size("grp")
    return lax.ppermute(value, "grp", [(g, (g + offset) % groups) for g in range(groups)])


def partner(value):
    return lax.ppermute(value, "core", ((0, 1), (1, 0)))


def local(
    pol_hidden, ref_hidden, pol_routes, ref_routes, pol_gates, ref_gates,
    w_gate, w_up, w_down, norm_gain, vocab_head, targets, seq_lengths, owners,
):
    chip, core, group = lax.axis_index("chip"), lax.axis_index("core"), lax.axis_index("grp")
    chips, groups = lax.axis_size("chip"), lax.axis_size("grp")
    device = (group * chips + chip) * 2 + core
    experts = w_gate.shape[0] * chips * 2
    tokens, width = pol_hidden.shape
    share = 2 * tokens
    capacity = tokens * pol_routes.shape[1] // experts + 2
    vocab_rows = vocab_head.shape[0]
    offsets = range(1, chips)

    send = pack_rows(
        pol_hidden, ref_hidden, pol_routes, ref_routes, pol_gates, ref_gates, experts
    )
    plane = [send] + [across(send, d) for d in offsets]
    plane = plane + [partner(rows) for rows in plane]

    home = (group - jnp.arange(groups, dtype=jnp.int32)) % groups
    spots = home[None, :] * chips + (chip ^ jnp.arange(chips, dtype=jnp.int32))[:, None]
    spots = spots.reshape(-1)
    other_head = partner(vocab_head)

    place = jnp.stack((chip, core)).astype(jnp.int32)
    keep, give = expert_sums(place, plane, w_gate, w_up, w_down, tokens, capacity, width, experts)
    own, *sends = pair_sums(keep, partner(give))
    came = [across(rows, d) for d, rows in zip(offsets, sends)]
    own, goal = begin_rows(own, came[-1], targets, groups * chips)
    goal = lax.all_to_all(goal, ("grp", "chip"), split_axis=0, concat_axis=0, tiled=True)
    match = spots[:, None] == jnp.arange(groups * chips, dtype=jnp.int32)[None, :]
    goal = jnp.sum(jnp.where(match[:, :, None], goal[None], 0), axis=1)
    wanted = jnp.concatenate((goal, goal), axis=1).reshape(1, -1)
    normed = norm_rows(send, norm_gain, wanted, own, came[:-1])

    column = [normed] + [along(normed, k) for k in range(1, groups)]
    if chips == 4:
        near = [across(rows, 1) for rows in column]
        far = [across(rows, 2) for rows in column]
        half = groups // 2
        cross = [across(rows, 2) for rows in near[:half]] + [
            across(rows, 1) for rows in far[half:]
        ]
    else:
        column = jnp.concatenate(column, axis=0)
        blocks = [column] + [across(column, d) for d in offsets]
    base = jnp.stack((device, device + 1 - 2 * core)).astype(jnp.int32) * vocab_rows
    lines = groups * share

    def stats_of(places, start, pieces, earlier, shape):
        blocks, parts = [block for block, _ in pieces], tuple(part for _, part in pieces)
        end = start + sum(high - low for low, high in parts)
        places = jnp.concatenate((base, places))
        return head_stats(
            places, wanted[:, start:end], blocks, parts, earlier, vocab_head, other_head, shape
        )

    if chips == 4:
        blocks = column + near + far + cross
        cut = max(256, (3 * lines - share) // 256 * 256)
        before, after = [], []
        for index, block in enumerate(blocks):
            border = min(max(cut - index * share, 0), share)
            if border > 0:
                before.append((block, (0, border)))
            if border < share:
                after.append((block, (border, share)))
        first = stats_of(spots, 0, before, (), (2, cut))
        stats = stats_of(spots, cut, after, (first,), (groups * chips, 2, share))
    else:
        fixed = jnp.arange(groups, dtype=jnp.int32)
        pieces = [
            stats_of(fixed, d * lines, [(block, (0, lines))], (), (groups, 2, share))
            for d, block in enumerate(blocks)
        ]
        pieces = jnp.concatenate(pieces, axis=0)
        stats = jnp.zeros_like(pieces).at[spots].set(pieces)

    lse, hit = combine([stats] + [along(stats, k) for k in range(1, groups)])
    stats = jnp.stack((lse, hit), axis=1)
    lse, hit = combine([stats] + [across(stats, d) for d in offsets])
    logprob = hit - lse
    ratio = logprob[:, :tokens] - logprob[:, tokens:]
    other = partner(ratio)
    token_ratio = lax.dynamic_index_in_dim(ratio, group * chips + chip, keepdims=False)

    mine = owners == device
    ends = jnp.cumsum(seq_lengths)
    length = jnp.sum(jnp.where(mine, seq_lengths, 0))
    end = jnp.sum(jnp.where(mine, ends, 0))
    row = jnp.arange(groups * chips, dtype=jnp.int32)[:, None]
    lane = jnp.arange(tokens, dtype=jnp.int32)[None, :]
    position = (2 * row + core) * tokens + lane
    inside = (position >= end - length) & (position < end)
    position = (2 * row + 1 - core) * tokens + lane
    inside_other = (position >= end - length) & (position < end)
    mean = jnp.sum(jnp.where(inside, ratio, 0.0) + jnp.where(inside_other, other, 0.0))
    return (token_ratio, (mean / length.astype(jnp.float32)).reshape(1))


def solution(mesh):
    names = ("grp", "chip", "core")
    groups, plane = mesh.devices.shape
    fine = Mesh(mesh.devices.reshape(groups, plane // 2, 2), names)
    return jax.shard_map(
        local,
        mesh=fine,
        in_specs=(
            P(names, None), P(names, None), P(names, None), P(names, None),
            P(names, None), P(names, None),
            P(names[1:], None, None), P(names[1:], None, None), P(names[1:], None, None),
            P(), P(names, None), P(names), P(), P(),
        ),
        out_specs=(P(names), P(names)),
        check_vma=False,
    )
```

```python
import functools
import math

import jax
import jax.numpy as jnp
from jax import lax
from jax.experimental import pallas as pl
from jax.experimental.pallas import tpu as pltpu
from jax.sharding import Mesh, PartitionSpec as P

MIB = 1 << 20
LOW = -1e30


def round_up(value, step):
    return -(-value // step) * step


def largest_tile(rows, limit, step):
    best = rows
    for tile in range(step, min(rows, limit) + 1, step):
        if rows % tile == 0:
            best = tile
    return best


def pack_kernel(pol_ref, ref_ref, pol_routes, ref_routes, pol_gates, ref_gates, out_ref, room):
    tokens, width = pol_ref.shape
    experts = (room.shape[1] - width) // 2
    parts = ((pol_ref, pol_routes, pol_gates), (ref_ref, ref_routes, ref_gates))
    for index, (hidden, routes, gates) in enumerate(parts):
        band = pl.ds(index * tokens, tokens)
        room[band, :width] = hidden[...].astype(jnp.float32)
        expert = lax.broadcasted_iota(jnp.int32, (experts, tokens), 0)
        dense = jnp.zeros((experts, tokens), jnp.float32)
        for k in range(routes.shape[0]):
            dense = jnp.where(expert == routes[pl.ds(k, 1), :], gates[pl.ds(k, 1), :], dense)
        high = dense.astype(jnp.bfloat16).astype(jnp.float32)
        table = jnp.concatenate((high, dense - high), axis=0)
        room[band, width:] = table.T
    out_ref[...] = room[...].astype(jnp.bfloat16)


def pack_rows(pol_hidden, ref_hidden, pol_routes, ref_routes, pol_gates, ref_gates, experts):
    tokens, width = pol_hidden.shape
    shape = (2 * tokens, width + 2 * experts)
    return pl.pallas_call(
        pack_kernel,
        out_shape=jax.ShapeDtypeStruct(shape, jnp.bfloat16),
        scratch_shapes=[pltpu.VMEM(shape, jnp.float32)],
        compiler_params=pltpu.CompilerParams(vmem_limit_bytes=58 * MIB),
    )(pol_hidden, ref_hidden, pol_routes.T, ref_routes.T, pol_gates.T, ref_gates.T)


def expert_kernel(block, slots, width, experts, chips, place_ref, early_ref, *refs):
    del early_ref
    count = 2 * chips
    blocks, refs = refs[:count], refs[count:]
    gate_ref, up_ref, down_ref, keep_ref, give_ref = refs[:5]
    rows_in, table, pick, weight, picked, made, gate_buf, up_buf, down_buf, arrived = refs[5:]
    step = pl.program_id(0)
    last = pl.num_programs(0) - 1
    rows = rows_in.shape[0]
    share = rows // count
    local_experts = pick.shape[0] // slots
    chip, core = place_ref[0], place_ref[1]

    def weight_copies(e):
        pairs = ((gate_ref, gate_buf), (up_ref, up_buf), (down_ref, down_buf))
        return [
            pltpu.make_async_copy(source.at[e], buffer.at[e], arrived.at[index, e])
            for index, (source, buffer) in enumerate(pairs)
        ]

    @pl.when(step == 0)
    def _():
        for e in range(local_experts):
            for copy in weight_copies(e):
                copy.start()
        for index, ref in enumerate(blocks):
            owner = 2 * (chip ^ (index % chips)) + (core ^ (index // chips))
            rows_in[pl.ds(pl.multiple_of(owner * share, 16), share), :] = ref[...]
        gates = rows_in[:, width:].astype(jnp.float32).T
        hits = (gates > 0.0).astype(jnp.bfloat16)
        span = math.gcd(rows, 16 * block)
        before = lax.broadcasted_iota(jnp.int32, (span, span), 0)
        after = lax.broadcasted_iota(jnp.int32, (1, span), 1)
        first = after - after % block
        order = ((before < after) & (before >= first)).astype(jnp.bfloat16)
        per_block = slots // (rows // block)
        for start in range(0, rows, span):
            band = slice(start, start + span)
            rank = jnp.dot(hits[:, band], order, preferred_element_type=jnp.float32)
            slot = rank + ((start + after) // block * per_block).astype(jnp.float32)
            table[0, :, band] = jnp.where(gates[:, band] > 0.0, slot, -1.0)
        table[1] = gates
        spot = lax.broadcasted_iota(jnp.int32, (slots, rows), 0).astype(jnp.float32)
        for e in range(local_experts):
            row = (2 * chip + core) * local_experts + e
            chosen = table[0, pl.ds(row, 1), :] == spot
            band = pl.ds(e * slots, slots)
            pick[band, :] = jnp.where(chosen, 1.0, 0.0).astype(jnp.bfloat16)
            gate = table[1, pl.ds(row, 1), :] + table[1, pl.ds(row + experts, 1), :]
            weight[band, :] = jnp.sum(jnp.where(chosen, gate, 0.0), axis=1, keepdims=True)
        picked[...] = jnp.dot(
            pick[...], rows_in[:, :width], preferred_element_type=jnp.float32
        ).astype(jnp.bfloat16)

    band = pl.ds(pl.multiple_of(step * slots, slots), slots)
    mine = picked[band, :]
    for copy in weight_copies(step):
        copy.wait()
    gate_act = jnp.dot(mine, gate_buf[step], preferred_element_type=jnp.float32)
    up_act = jnp.dot(mine, up_buf[step], preferred_element_type=jnp.float32)
    inner = (gate_act / (1.0 + jnp.exp(-gate_act)) * up_act).astype(jnp.bfloat16)
    output = jnp.dot(inner, down_buf[step], preferred_element_type=jnp.float32).astype(jnp.bfloat16)
    scaled = output.astype(jnp.float32) * weight[band, :]
    high = scaled.astype(jnp.bfloat16)
    made[band, :width] = high
    made[band, width:] = (scaled - high.astype(jnp.float32)).astype(jnp.bfloat16)

    @pl.when(step == last)
    def _():
        over_slots = (((0,), (0,)), ((), ()))
        span = math.gcd(rows, 16 * block)
        for start in range(0, rows, span):
            band = pl.ds(start, span)
            total = lax.dot_general(
                pick[:, band], made[...], over_slots, preferred_element_type=jnp.float32
            )
            total = total[:, :width] + total[:, width:]
            for index in range(span // share):
                c, owner = divmod(start // share + index, 2)
                target = total[index * share:(index + 1) * share]

                @pl.when(core == owner)
                def _():
                    keep_ref[c ^ chip] = target

                @pl.when(core != owner)
                def _():
                    give_ref[c ^ chip] = target


def expert_sums(place, early, blocks, w_gate, w_up, w_down, block, capacity, width, experts):
    count = len(blocks)
    share, wide = blocks[0].shape
    rows = count * share
    local_experts, _, hidden = w_gate.shape
    slots = round_up(capacity, 8) * (rows // block)
    every = local_experts * slots
    half = jax.ShapeDtypeStruct((count // 2, share, width), jnp.float32)
    whole = pl.BlockSpec(
        (share, wide), lambda e, place: (0, 0), pipeline_mode=pl.Buffered(1)
    )
    return pl.pallas_call(
        functools.partial(expert_kernel, block, slots, width, experts, count // 2),
        out_shape=(half, half),
        grid_spec=pltpu.PrefetchScalarGridSpec(
            num_scalar_prefetch=1,
            grid=(local_experts,),
            in_specs=[pl.BlockSpec(memory_space=pl.ANY)] + [whole] * count + [
                pl.BlockSpec(memory_space=pl.ANY) for _ in range(3)
            ],
            out_specs=(
                pl.BlockSpec(
                    half.shape, lambda e, place: (0, 0, 0), pipeline_mode=pl.Buffered(1)
                ),
                pl.BlockSpec(
                    half.shape, lambda e, place: (0, 0, 0), pipeline_mode=pl.Buffered(1)
                ),
            ),
            scratch_shapes=[
                pltpu.VMEM((rows, wide), jnp.bfloat16),
                pltpu.VMEM((2, wide - width, rows), jnp.float32),
                pltpu.VMEM((every, rows), jnp.bfloat16),
                pltpu.VMEM((every, 1), jnp.float32),
                pltpu.VMEM((every, width), jnp.bfloat16),
                pltpu.VMEM((every, 2 * width), jnp.bfloat16),
                pltpu.VMEM(w_gate.shape, jnp.bfloat16),
                pltpu.VMEM(w_up.shape, jnp.bfloat16),
                pltpu.VMEM(w_down.shape, jnp.bfloat16),
                pltpu.SemaphoreType.DMA((3, local_experts)),
            ],
        ),
        compiler_params=pltpu.CompilerParams(
            vmem_limit_bytes=(55 if rows <= 640 else 58) * MIB
        ),
        cost_estimate=pl.CostEstimate(
            flops=2 * every * width * (3 * hidden + 3 * rows),
            bytes_accessed=w_gate.size * 6 + rows * wide * 2 + rows * width * 4,
            transcendentals=every * hidden,
        ),
    )(place, early, *blocks, w_gate, w_up, w_down)


def pair_kernel(keep_ref, came_ref, goal_ref, own_ref, *sends):
    own_ref[...] = keep_ref[0] + came_ref[0]
    share, lines = keep_ref.shape[1], goal_ref.shape[1]
    for index, send in enumerate(sends):
        send[:share] = keep_ref[index + 1] + came_ref[index + 1]
        send[share:] = jnp.zeros((send.shape[0] - share, send.shape[1]), jnp.float32)
        send[share:share + 1, :lines] = goal_ref[...]


def pair_sums(keep, came, goal):
    chips, share, width = keep.shape
    own = jax.ShapeDtypeStruct((share, width), jnp.float32)
    send = jax.ShapeDtypeStruct((share + 8, width), jnp.float32)
    return pl.pallas_call(
        pair_kernel,
        out_shape=(own,) + (send,) * (chips - 1),
        compiler_params=pltpu.CompilerParams(vmem_limit_bytes=24 * MIB),
    )(keep, came, goal)


def norm_kernel(hidden_ref, gain_ref, goal_ref, own_ref, *refs):
    came, normed_ref, wanted_ref = refs[:-2], refs[-2], refs[-1]
    share, width = own_ref.shape
    lines = goal_ref.shape[1]
    mixed = hidden_ref[:, :width].astype(jnp.float32) + own_ref[...]
    wanted_ref[0:1, :] = goal_ref[...].astype(jnp.int32)
    for index, ref in enumerate(came):
        mixed += ref[:share]
        wanted_ref[index + 1:index + 2, :] = ref[share:share + 1, :lines].astype(jnp.int32)
    scale = lax.rsqrt(jnp.mean(mixed * mixed, axis=1, keepdims=True) + 1e-06)
    normed_ref[...] = (mixed * scale * gain_ref[...]).astype(jnp.bfloat16)


def norm_rows(hidden, gain, goal, own, came):
    return pl.pallas_call(
        norm_kernel,
        out_shape=(
            jax.ShapeDtypeStruct(own.shape, jnp.bfloat16),
            jax.ShapeDtypeStruct((len(came) + 1, goal.shape[1]), jnp.int32),
        ),
        compiler_params=pltpu.CompilerParams(vmem_limit_bytes=16 * MIB),
    )(hidden, gain.reshape(1, -1), goal, own, *came)


def head_kernel(parts, before, spots_ref, wanted_ref, *refs):
    blocks, refs = refs[:len(parts)], refs[len(parts):]
    earlier, refs = refs[:before], refs[before:]
    head_a, head_b, out_ref, rows_in, peak, total, found, logits_a, logits_b = refs
    step = pl.program_id(0)
    last = pl.num_programs(0) - 1
    tile, columns = logits_a.shape
    base_a, base_b = spots_ref[0], spots_ref[1]

    def product(head_ref, logits):
        logits[...] = lax.dot_general(
            head_ref[...], rows_in[...], (((1,), (1,)), ((), ())),
            preferred_element_type=jnp.float32,
        )

    def absorb(logits, first):
        for start in range(0, columns, 128):
            lanes = min(128, columns - start)
            band = pl.ds(start, lanes)
            row = lax.broadcasted_iota(jnp.int32, (tile, lanes), 0)
            values = logits[:, band]
            old = peak[:, band]
            new = jnp.maximum(old, jnp.max(values.reshape(tile // 8, 8, lanes), axis=0))
            grown = jnp.exp(values.reshape(tile // 8, 8, lanes) - new[None])
            total[:, band] = total[:, band] * jnp.exp(old - new) + jnp.sum(grown, axis=0)
            same = row == wanted_ref[:, band] - first
            kept = jnp.where(same, values, 0.0).reshape(tile // 8, 8, lanes)
            found[:, band] += jnp.sum(kept, axis=0)
            peak[:, band] = new

    @pl.when(step == 0)
    def _():
        start = 0
        for ref, (low, high) in zip(blocks, parts):
            rows_in[start:start + high - low, :] = ref[low:high, :]
            start += high - low
        peak[...] = jnp.full_like(peak, LOW)
        total[...] = jnp.zeros_like(total)
        found[...] = jnp.zeros_like(found)
        logits_b[...] = jnp.full_like(logits_b, LOW)

    product(head_a, logits_a)
    absorb(logits_b, jnp.where(step == 0, -(1 << 28), base_b + (step - 1) * tile))
    product(head_b, logits_b)
    absorb(logits_a, base_a + step * tile)

    @pl.when(step == last)
    def _():
        absorb(logits_b, base_b + step * tile)
        top = jnp.max(peak[...], axis=0, keepdims=True)
        full = jnp.sum(total[...] * jnp.exp(peak[...] - top), axis=0, keepdims=True)
        lse = top + jnp.log(full)
        hit = jnp.sum(found[...], axis=0, keepdims=True)
        lse = jnp.concatenate([ref[0:1, :] for ref in earlier] + [lse], axis=1)
        hit = jnp.concatenate([ref[1:2, :] for ref in earlier] + [hit], axis=1)
        if len(out_ref.shape) == 2:
            out_ref[0:1, :] = lse
            out_ref[1:2, :] = hit
        else:
            share = out_ref.shape[2]
            for index in range(out_ref.shape[0]):
                band = slice(index * share, (index + 1) * share)
                spot = spots_ref[2 + index]
                out_ref[spot, 0:1, :] = lse[:, band]
                out_ref[spot, 1:2, :] = hit[:, band]


def head_stats(spots, wanted, blocks, parts, earlier, head_a, head_b, shape):
    rows = sum(high - low for low, high in parts)
    width = head_a.shape[1]
    whole = pl.BlockSpec(shape, lambda s, spots: (0,) * len(shape))
    tile = largest_tile(head_a.shape[0], 608, 16)
    steps = head_a.shape[0] // tile
    return pl.pallas_call(
        functools.partial(head_kernel, parts, len(earlier)),
        out_shape=jax.ShapeDtypeStruct(shape, jnp.float32),
        grid_spec=pltpu.PrefetchScalarGridSpec(
            num_scalar_prefetch=1,
            grid=(steps,),
            in_specs=[pl.BlockSpec((1, rows), lambda s, spots: (0, 0))] + [
                pl.BlockSpec(block.shape, lambda s, spots: (0, 0), pipeline_mode=pl.Buffered(1))
                for block in blocks
            ] + [
                pl.BlockSpec(part.shape, lambda s, spots: (0, 0)) for part in earlier
            ] + [
                pl.BlockSpec((tile, width), lambda s, spots: (s, 0)),
                pl.BlockSpec((tile, width), lambda s, spots: (s, 0)),
            ],
            out_specs=whole,
            scratch_shapes=[
                pltpu.VMEM((rows, width), jnp.bfloat16),
                pltpu.VMEM((8, rows), jnp.float32),
                pltpu.VMEM((8, rows), jnp.float32),
                pltpu.VMEM((8, rows), jnp.float32),
                pltpu.VMEM((tile, rows), jnp.float32),
                pltpu.VMEM((tile, rows), jnp.float32),
            ],
        ),
        compiler_params=pltpu.CompilerParams(vmem_limit_bytes=58 * MIB),
        cost_estimate=pl.CostEstimate(
            flops=4 * rows * width * head_a.shape[0],
            bytes_accessed=head_a.size * 4 + rows * width * 2,
            transcendentals=2 * rows * head_a.shape[0],
        ),
    )(spots, wanted, *blocks, *earlier, head_a, head_b)


def combine(parts):
    top = functools.reduce(jnp.maximum, [part[:, 0] for part in parts])
    total = sum(jnp.exp(part[:, 0] - top) for part in parts)
    return top + jnp.log(total), sum(part[:, 1] for part in parts)


def across(value, offset):
    chips = lax.axis_size("chip")
    return lax.ppermute(value, "chip", [(c, c ^ offset) for c in range(chips)])


def along(value, offset):
    groups = lax.axis_size("grp")
    return lax.ppermute(value, "grp", [(g, (g + offset) % groups) for g in range(groups)])


def partner(value):
    return lax.ppermute(value, "core", ((0, 1), (1, 0)))


def local(
    pol_hidden, ref_hidden, pol_routes, ref_routes, pol_gates, ref_gates,
    w_gate, w_up, w_down, norm_gain, vocab_head, targets, seq_lengths, owners,
):
    chip, core, group = lax.axis_index("chip"), lax.axis_index("core"), lax.axis_index("grp")
    chips, groups = lax.axis_size("chip"), lax.axis_size("grp")
    device = (group * chips + chip) * 2 + core
    experts = w_gate.shape[0] * chips * 2
    tokens, width = pol_hidden.shape
    share = 2 * tokens
    capacity = tokens * pol_routes.shape[1] // experts + 2
    vocab_rows = vocab_head.shape[0]
    offsets = range(1, chips)

    send = pack_rows(
        pol_hidden, ref_hidden, pol_routes, ref_routes, pol_gates, ref_gates, experts
    )
    plane = [send] + [across(send, d) for d in offsets]
    plane = plane + [partner(rows) for rows in plane]

    home = (group - jnp.arange(groups, dtype=jnp.int32)) % groups
    spots = home[None, :] * chips + (chip ^ jnp.arange(chips, dtype=jnp.int32))[:, None]
    spots = spots.reshape(-1)
    goal = targets.astype(jnp.float32).reshape(1, tokens)
    goal = jnp.concatenate((goal, goal), axis=1)
    goal = jnp.concatenate([goal] + [along(goal, k) for k in range(1, groups)], axis=1)
    other_head = partner(vocab_head)

    place = jnp.stack((chip, core)).astype(jnp.int32)
    keep, give = expert_sums(
        place, goal, plane, w_gate, w_up, w_down, tokens, capacity, width, experts
    )
    own, *sends = pair_sums(keep, partner(give), goal)
    came = [across(rows, d) for d, rows in zip(offsets, sends)]
    normed, wanted = norm_rows(send, norm_gain, goal, own, came)
    wanted = wanted.reshape(1, -1)

    column = [normed] + [along(normed, k) for k in range(1, groups)]
    if chips == 4:
        near = [across(rows, 1) for rows in column]
        far = [across(rows, 2) for rows in column]
        half = groups // 2
        cross = [across(rows, 2) for rows in near[:half]] + [
            across(rows, 1) for rows in far[half:]
        ]
    else:
        column = jnp.concatenate(column, axis=0)
        blocks = [column] + [across(column, d) for d in offsets]
    base = jnp.stack((device, device + 1 - 2 * core)).astype(jnp.int32) * vocab_rows
    lines = groups * share

    def stats_of(places, start, pieces, earlier, shape):
        blocks, parts = [block for block, _ in pieces], tuple(part for _, part in pieces)
        end = start + sum(high - low for low, high in parts)
        places = jnp.concatenate((base, places))
        return head_stats(
            places, wanted[:, start:end], blocks, parts, earlier, vocab_head, other_head, shape
        )

    if chips == 4:
        blocks = column + near + far + cross
        cut = max(256, (3 * lines - share) // 256 * 256)
        before, after = [], []
        for index, block in enumerate(blocks):
            border = min(max(cut - index * share, 0), share)
            if border > 0:
                before.append((block, (0, border)))
            if border < share:
                after.append((block, (border, share)))
        first = stats_of(spots, 0, before, (), (2, cut))
        stats = stats_of(spots, cut, after, (first,), (groups * chips, 2, share))
    else:
        fixed = jnp.arange(groups, dtype=jnp.int32)
        pieces = [
            stats_of(fixed, d * lines, [(block, (0, lines))], (), (groups, 2, share))
            for d, block in enumerate(blocks)
        ]
        pieces = jnp.concatenate(pieces, axis=0)
        stats = jnp.zeros_like(pieces).at[spots].set(pieces)

    lse, hit = combine([stats] + [along(stats, k) for k in range(1, groups)])
    stats = jnp.stack((lse, hit), axis=1)
    lse, hit = combine([stats] + [across(stats, d) for d in offsets])
    logprob = hit - lse
    ratio = logprob[:, :tokens] - logprob[:, tokens:]
    other = partner(ratio)
    token_ratio = lax.dynamic_index_in_dim(ratio, group * chips + chip, keepdims=False)

    mine = owners == device
    ends = jnp.cumsum(seq_lengths)
    length = jnp.sum(jnp.where(mine, seq_lengths, 0))
    end = jnp.sum(jnp.where(mine, ends, 0))
    row = jnp.arange(groups * chips, dtype=jnp.int32)[:, None]
    lane = jnp.arange(tokens, dtype=jnp.int32)[None, :]
    position = (2 * row + core) * tokens + lane
    inside = (position >= end - length) & (position < end)
    position = (2 * row + 1 - core) * tokens + lane
    inside_other = (position >= end - length) & (position < end)
    mean = jnp.sum(jnp.where(inside, ratio, 0.0) + jnp.where(inside_other, other, 0.0))
    return (token_ratio, (mean / length.astype(jnp.float32)).reshape(1))


def solution(mesh):
    names = ("grp", "chip", "core")
    groups, plane = mesh.devices.shape
    fine = Mesh(mesh.devices.reshape(groups, plane // 2, 2), names)
    return jax.shard_map(
        local,
        mesh=fine,
        in_specs=(
            P(names, None), P(names, None), P(names, None), P(names, None),
            P(names, None), P(names, None),
            P(names[1:], None, None), P(names[1:], None, None), P(names[1:], None, None),
            P(), P(names, None), P(names), P(), P(),
        ),
        out_specs=(P(names), P(names)),
        check_vma=False,
    )
```

```python
import functools
import math

import jax
import jax.numpy as jnp
from jax import lax
from jax.experimental import pallas as pl
from jax.experimental.pallas import tpu as pltpu
from jax.sharding import Mesh, PartitionSpec as P

MIB = 1 << 20
LOW = -1e30


def round_up(value, step):
    return -(-value // step) * step


def largest_tile(rows, limit, step):
    best = rows
    for tile in range(step, min(rows, limit) + 1, step):
        if rows % tile == 0:
            best = tile
    return best


def pack_kernel(pol_ref, ref_ref, pol_routes, ref_routes, pol_gates, ref_gates, out_ref, room):
    tokens, width = pol_ref.shape
    experts = (room.shape[1] - width) // 2
    parts = ((pol_ref, pol_routes, pol_gates), (ref_ref, ref_routes, ref_gates))
    for index, (hidden, routes, gates) in enumerate(parts):
        band = pl.ds(index * tokens, tokens)
        room[band, :width] = hidden[...].astype(jnp.float32)
        expert = lax.broadcasted_iota(jnp.int32, (experts, tokens), 0)
        dense = jnp.zeros((experts, tokens), jnp.float32)
        for k in range(routes.shape[0]):
            dense = jnp.where(expert == routes[pl.ds(k, 1), :], gates[pl.ds(k, 1), :], dense)
        high = dense.astype(jnp.bfloat16).astype(jnp.float32)
        table = jnp.concatenate((high, dense - high), axis=0)
        room[band, width:] = table.T
    out_ref[...] = room[...].astype(jnp.bfloat16)


def pack_rows(pol_hidden, ref_hidden, pol_routes, ref_routes, pol_gates, ref_gates, experts):
    tokens, width = pol_hidden.shape
    shape = (2 * tokens, width + 2 * experts)
    return pl.pallas_call(
        pack_kernel,
        out_shape=jax.ShapeDtypeStruct(shape, jnp.bfloat16),
        scratch_shapes=[pltpu.VMEM(shape, jnp.float32)],
        compiler_params=pltpu.CompilerParams(vmem_limit_bytes=58 * MIB),
    )(pol_hidden, ref_hidden, pol_routes.T, ref_routes.T, pol_gates.T, ref_gates.T)


def expert_kernel(block, slots, width, experts, chips, place_ref, early_ref, *refs):
    del early_ref
    count = 2 * chips
    blocks, refs = refs[:count], refs[count:]
    gate_ref, up_ref, down_ref, keep_ref, give_ref = refs[:5]
    rows_in, table, pick, weight, picked, made, gate_buf, up_buf, down_buf, arrived = refs[5:]
    step = pl.program_id(0)
    last = pl.num_programs(0) - 1
    rows = rows_in.shape[0]
    share = rows // count
    local_experts = pick.shape[0] // slots
    chip, core = place_ref[0], place_ref[1]

    def weight_copies(e):
        pairs = ((gate_ref, gate_buf), (up_ref, up_buf), (down_ref, down_buf))
        return [
            pltpu.make_async_copy(source.at[e], buffer.at[e], arrived.at[index, e])
            for index, (source, buffer) in enumerate(pairs)
        ]

    @pl.when(step == 0)
    def _():
        for e in range(local_experts):
            for copy in weight_copies(e):
                copy.start()
        for index, ref in enumerate(blocks):
            owner = 2 * (chip ^ (index % chips)) + (core ^ (index // chips))
            rows_in[pl.ds(pl.multiple_of(owner * share, 16), share), :] = ref[...]
        gates = rows_in[:, width:].astype(jnp.float32).T
        hits = (gates > 0.0).astype(jnp.bfloat16)
        span = math.gcd(rows, 16 * block)
        before = lax.broadcasted_iota(jnp.int32, (span, span), 0)
        after = lax.broadcasted_iota(jnp.int32, (1, span), 1)
        first = after - after % block
        order = ((before < after) & (before >= first)).astype(jnp.bfloat16)
        per_block = slots // (rows // block)
        for start in range(0, rows, span):
            band = slice(start, start + span)
            rank = jnp.dot(hits[:, band], order, preferred_element_type=jnp.float32)
            slot = rank + ((start + after) // block * per_block).astype(jnp.float32)
            table[0, :, band] = jnp.where(gates[:, band] > 0.0, slot, -1.0)
        table[1] = gates
        spot = lax.broadcasted_iota(jnp.int32, (slots, rows), 0).astype(jnp.float32)
        for e in range(local_experts):
            row = (2 * chip + core) * local_experts + e
            chosen = table[0, pl.ds(row, 1), :] == spot
            band = pl.ds(e * slots, slots)
            pick[band, :] = jnp.where(chosen, 1.0, 0.0).astype(jnp.bfloat16)
            gate = table[1, pl.ds(row, 1), :] + table[1, pl.ds(row + experts, 1), :]
            weight[band, :] = jnp.sum(jnp.where(chosen, gate, 0.0), axis=1, keepdims=True)
        picked[...] = jnp.dot(
            pick[...], rows_in[:, :width], preferred_element_type=jnp.float32
        ).astype(jnp.bfloat16)

    band = pl.ds(pl.multiple_of(step * slots, slots), slots)
    mine = picked[band, :]
    for copy in weight_copies(step):
        copy.wait()
    gate_act = jnp.dot(mine, gate_buf[step], preferred_element_type=jnp.float32)
    up_act = jnp.dot(mine, up_buf[step], preferred_element_type=jnp.float32)
    inner = (gate_act / (1.0 + jnp.exp(-gate_act)) * up_act).astype(jnp.bfloat16)
    output = jnp.dot(inner, down_buf[step], preferred_element_type=jnp.float32).astype(jnp.bfloat16)
    scaled = output.astype(jnp.float32) * weight[band, :]
    high = scaled.astype(jnp.bfloat16)
    made[band, :width] = high
    made[band, width:] = (scaled - high.astype(jnp.float32)).astype(jnp.bfloat16)

    @pl.when(step == last)
    def _():
        over_slots = (((0,), (0,)), ((), ()))
        span = math.gcd(rows, 16 * block)
        for start in range(0, rows, span):
            band = pl.ds(start, span)
            total = lax.dot_general(
                pick[:, band], made[...], over_slots, preferred_element_type=jnp.float32
            )
            total = total[:, :width] + total[:, width:]
            for index in range(span // share):
                c, owner = divmod(start // share + index, 2)
                target = total[index * share:(index + 1) * share]

                @pl.when(core == owner)
                def _():
                    keep_ref[c ^ chip] = target

                @pl.when(core != owner)
                def _():
                    give_ref[c ^ chip] = target


def expert_sums(place, early, blocks, w_gate, w_up, w_down, block, capacity, width, experts):
    count = len(blocks)
    share, wide = blocks[0].shape
    rows = count * share
    local_experts, _, hidden = w_gate.shape
    slots = round_up(capacity, 8) * (rows // block)
    every = local_experts * slots
    half = jax.ShapeDtypeStruct((count // 2, share, width), jnp.float32)
    whole = pl.BlockSpec(
        (share, wide), lambda e, place: (0, 0), pipeline_mode=pl.Buffered(1)
    )
    return pl.pallas_call(
        functools.partial(expert_kernel, block, slots, width, experts, count // 2),
        out_shape=(half, half),
        grid_spec=pltpu.PrefetchScalarGridSpec(
            num_scalar_prefetch=1,
            grid=(local_experts,),
            in_specs=[pl.BlockSpec(memory_space=pl.ANY)] + [whole] * count + [
                pl.BlockSpec(memory_space=pl.ANY) for _ in range(3)
            ],
            out_specs=(
                pl.BlockSpec(
                    half.shape, lambda e, place: (0, 0, 0), pipeline_mode=pl.Buffered(1)
                ),
                pl.BlockSpec(
                    half.shape, lambda e, place: (0, 0, 0), pipeline_mode=pl.Buffered(1)
                ),
            ),
            scratch_shapes=[
                pltpu.VMEM((rows, wide), jnp.bfloat16),
                pltpu.VMEM((2, wide - width, rows), jnp.float32),
                pltpu.VMEM((every, rows), jnp.bfloat16),
                pltpu.VMEM((every, 1), jnp.float32),
                pltpu.VMEM((every, width), jnp.bfloat16),
                pltpu.VMEM((every, 2 * width), jnp.bfloat16),
                pltpu.VMEM(w_gate.shape, jnp.bfloat16),
                pltpu.VMEM(w_up.shape, jnp.bfloat16),
                pltpu.VMEM(w_down.shape, jnp.bfloat16),
                pltpu.SemaphoreType.DMA((3, local_experts)),
            ],
        ),
        compiler_params=pltpu.CompilerParams(
            vmem_limit_bytes=60 * MIB
        ),
        cost_estimate=pl.CostEstimate(
            flops=2 * every * width * (3 * hidden + 3 * rows),
            bytes_accessed=w_gate.size * 6 + rows * wide * 2 + rows * width * 4,
            transcendentals=every * hidden,
        ),
    )(place, early, *blocks, w_gate, w_up, w_down)


def pair_kernel(keep_ref, came_ref, goal_ref, own_ref, *sends):
    own_ref[...] = keep_ref[0] + came_ref[0]
    share, lines = keep_ref.shape[1], goal_ref.shape[1]
    for index, send in enumerate(sends):
        send[:share] = keep_ref[index + 1] + came_ref[index + 1]
        send[share:] = jnp.zeros((send.shape[0] - share, send.shape[1]), jnp.float32)
        send[share:share + 1, :lines] = goal_ref[...]


def pair_sums(keep, came, goal):
    chips, share, width = keep.shape
    own = jax.ShapeDtypeStruct((share, width), jnp.float32)
    send = jax.ShapeDtypeStruct((share + 8, width), jnp.float32)
    return pl.pallas_call(
        pair_kernel,
        out_shape=(own,) + (send,) * (chips - 1),
        compiler_params=pltpu.CompilerParams(vmem_limit_bytes=24 * MIB),
    )(keep, came, goal)


def norm_kernel(hidden_ref, gain_ref, goal_ref, own_ref, *refs):
    came, normed_ref, wanted_ref = refs[:-2], refs[-2], refs[-1]
    share, width = own_ref.shape
    lines = goal_ref.shape[1]
    mixed = hidden_ref[:, :width].astype(jnp.float32) + own_ref[...]
    wanted_ref[0:1, :] = goal_ref[...].astype(jnp.int32)
    for index, ref in enumerate(came):
        mixed += ref[:share]
        wanted_ref[index + 1:index + 2, :] = ref[share:share + 1, :lines].astype(jnp.int32)
    scale = lax.rsqrt(jnp.mean(mixed * mixed, axis=1, keepdims=True) + 1e-06)
    normed_ref[...] = (mixed * scale * gain_ref[...]).astype(jnp.bfloat16)


def norm_rows(hidden, gain, goal, own, came):
    return pl.pallas_call(
        norm_kernel,
        out_shape=(
            jax.ShapeDtypeStruct(own.shape, jnp.bfloat16),
            jax.ShapeDtypeStruct((len(came) + 1, goal.shape[1]), jnp.int32),
        ),
        compiler_params=pltpu.CompilerParams(vmem_limit_bytes=16 * MIB),
    )(hidden, gain.reshape(1, -1), goal, own, *came)


def head_kernel(parts, before, spots_ref, wanted_ref, *refs):
    blocks, refs = refs[:len(parts)], refs[len(parts):]
    earlier, refs = refs[:before], refs[before:]
    head_a, head_b, out_ref, rows_in, peak, total, found, logits_a, logits_b = refs
    step = pl.program_id(0)
    last = pl.num_programs(0) - 1
    tile, columns = logits_a.shape
    base_a, base_b = spots_ref[0], spots_ref[1]

    def product(head_ref, logits):
        logits[...] = lax.dot_general(
            head_ref[...], rows_in[...], (((1,), (1,)), ((), ())),
            preferred_element_type=jnp.float32,
        )

    def absorb(logits, first):
        for start in range(0, columns, 128):
            lanes = min(128, columns - start)
            band = pl.ds(start, lanes)
            row = lax.broadcasted_iota(jnp.int32, (tile, lanes), 0)
            values = logits[:, band]
            old = peak[:, band]
            new = jnp.maximum(old, jnp.max(values.reshape(tile // 8, 8, lanes), axis=0))
            grown = jnp.exp(values.reshape(tile // 8, 8, lanes) - new[None])
            total[:, band] = total[:, band] * jnp.exp(old - new) + jnp.sum(grown, axis=0)
            same = row == wanted_ref[:, band] - first
            kept = jnp.where(same, values, 0.0).reshape(tile // 8, 8, lanes)
            found[:, band] += jnp.sum(kept, axis=0)
            peak[:, band] = new

    @pl.when(step == 0)
    def _():
        start = 0
        for ref, (low, high) in zip(blocks, parts):
            rows_in[start:start + high - low, :] = ref[low:high, :]
            start += high - low
        peak[...] = jnp.full_like(peak, LOW)
        total[...] = jnp.zeros_like(total)
        found[...] = jnp.zeros_like(found)
        logits_b[...] = jnp.full_like(logits_b, LOW)

    product(head_a, logits_a)
    absorb(logits_b, jnp.where(step == 0, -(1 << 28), base_b + (step - 1) * tile))
    product(head_b, logits_b)
    absorb(logits_a, base_a + step * tile)

    @pl.when(step == last)
    def _():
        absorb(logits_b, base_b + step * tile)
        top = jnp.max(peak[...], axis=0, keepdims=True)
        full = jnp.sum(total[...] * jnp.exp(peak[...] - top), axis=0, keepdims=True)
        lse = top + jnp.log(full)
        hit = jnp.sum(found[...], axis=0, keepdims=True)
        lse = jnp.concatenate([ref[0:1, :] for ref in earlier] + [lse], axis=1)
        hit = jnp.concatenate([ref[1:2, :] for ref in earlier] + [hit], axis=1)
        if len(out_ref.shape) == 2:
            out_ref[0:1, :] = lse
            out_ref[1:2, :] = hit
        else:
            share = out_ref.shape[2]
            for index in range(out_ref.shape[0]):
                band = slice(index * share, (index + 1) * share)
                spot = spots_ref[2 + index]
                out_ref[spot, 0:1, :] = lse[:, band]
                out_ref[spot, 1:2, :] = hit[:, band]


def head_stats(spots, wanted, blocks, parts, earlier, head_a, head_b, shape):
    rows = sum(high - low for low, high in parts)
    width = head_a.shape[1]
    whole = pl.BlockSpec(shape, lambda s, spots: (0,) * len(shape))
    tile = largest_tile(head_a.shape[0], 608, 16)
    steps = head_a.shape[0] // tile
    return pl.pallas_call(
        functools.partial(head_kernel, parts, len(earlier)),
        out_shape=jax.ShapeDtypeStruct(shape, jnp.float32),
        grid_spec=pltpu.PrefetchScalarGridSpec(
            num_scalar_prefetch=1,
            grid=(steps,),
            in_specs=[pl.BlockSpec((1, rows), lambda s, spots: (0, 0))] + [
                pl.BlockSpec(block.shape, lambda s, spots: (0, 0), pipeline_mode=pl.Buffered(1))
                for block in blocks
            ] + [
                pl.BlockSpec(part.shape, lambda s, spots: (0, 0)) for part in earlier
            ] + [
                pl.BlockSpec((tile, width), lambda s, spots: (s, 0)),
                pl.BlockSpec((tile, width), lambda s, spots: (s, 0)),
            ],
            out_specs=whole,
            scratch_shapes=[
                pltpu.VMEM((rows, width), jnp.bfloat16),
                pltpu.VMEM((8, rows), jnp.float32),
                pltpu.VMEM((8, rows), jnp.float32),
                pltpu.VMEM((8, rows), jnp.float32),
                pltpu.VMEM((tile, rows), jnp.float32),
                pltpu.VMEM((tile, rows), jnp.float32),
            ],
        ),
        compiler_params=pltpu.CompilerParams(vmem_limit_bytes=60 * MIB),
        cost_estimate=pl.CostEstimate(
            flops=4 * rows * width * head_a.shape[0],
            bytes_accessed=head_a.size * 4 + rows * width * 2,
            transcendentals=2 * rows * head_a.shape[0],
        ),
    )(spots, wanted, *blocks, *earlier, head_a, head_b)


def combine(parts):
    top = functools.reduce(jnp.maximum, [part[:, 0] for part in parts])
    total = sum(jnp.exp(part[:, 0] - top) for part in parts)
    return top + jnp.log(total), sum(part[:, 1] for part in parts)


def across(value, offset):
    chips = lax.axis_size("chip")
    return lax.ppermute(value, "chip", [(c, c ^ offset) for c in range(chips)])


def along(value, offset):
    groups = lax.axis_size("grp")
    return lax.ppermute(value, "grp", [(g, (g + offset) % groups) for g in range(groups)])


def partner(value):
    return lax.ppermute(value, "core", ((0, 1), (1, 0)))


def local(
    pol_hidden, ref_hidden, pol_routes, ref_routes, pol_gates, ref_gates,
    w_gate, w_up, w_down, norm_gain, vocab_head, targets, seq_lengths, owners,
):
    chip, core, group = lax.axis_index("chip"), lax.axis_index("core"), lax.axis_index("grp")
    chips, groups = lax.axis_size("chip"), lax.axis_size("grp")
    device = (group * chips + chip) * 2 + core
    experts = w_gate.shape[0] * chips * 2
    tokens, width = pol_hidden.shape
    share = 2 * tokens
    capacity = tokens * pol_routes.shape[1] // experts + 2
    vocab_rows = vocab_head.shape[0]
    offsets = range(1, chips)

    send = pack_rows(
        pol_hidden, ref_hidden, pol_routes, ref_routes, pol_gates, ref_gates, experts
    )
    plane = [send] + [across(send, d) for d in offsets]
    plane = plane + [partner(rows) for rows in plane]

    home = (group - jnp.arange(groups, dtype=jnp.int32)) % groups
    spots = home[None, :] * chips + (chip ^ jnp.arange(chips, dtype=jnp.int32))[:, None]
    spots = spots.reshape(-1)
    goal = targets.astype(jnp.float32).reshape(1, tokens)
    goal = jnp.concatenate((goal, goal), axis=1)
    goal = jnp.broadcast_to(goal, (groups, share))
    goal = lax.all_to_all(goal, "grp", split_axis=0, concat_axis=0, tiled=True)
    match = home[:, None] == jnp.arange(groups, dtype=jnp.int32)[None, :]
    goal = jnp.sum(jnp.where(match[:, :, None], goal[None], 0.0), axis=1).reshape(1, -1)
    other_head = partner(vocab_head)

    place = jnp.stack((chip, core)).astype(jnp.int32)
    keep, give = expert_sums(
        place, goal, plane, w_gate, w_up, w_down, tokens, capacity, width, experts
    )
    own, *sends = pair_sums(keep, partner(give), goal)
    came = [across(rows, d) for d, rows in zip(offsets, sends)]
    normed, wanted = norm_rows(send, norm_gain, goal, own, came)
    wanted = wanted.reshape(1, -1)

    column = [normed] + [along(normed, k) for k in range(1, groups)]
    if chips == 4:
        near = [across(rows, 1) for rows in column]
        far = [across(rows, 2) for rows in column]
        half = groups // 2
        cross = [across(rows, 2) for rows in near[:half]] + [
            across(rows, 1) for rows in far[half:]
        ]
    else:
        column = jnp.concatenate(column, axis=0)
        blocks = [column] + [across(column, d) for d in offsets]
    base = jnp.stack((device, device + 1 - 2 * core)).astype(jnp.int32) * vocab_rows
    lines = groups * share

    def stats_of(places, start, pieces, earlier, shape):
        blocks, parts = [block for block, _ in pieces], tuple(part for _, part in pieces)
        end = start + sum(high - low for low, high in parts)
        places = jnp.concatenate((base, places))
        return head_stats(
            places, wanted[:, start:end], blocks, parts, earlier, vocab_head, other_head, shape
        )

    if chips == 4:
        blocks = column + near + far + cross
        cut = max(256, (3 * lines - share) // 256 * 256)
        before, after = [], []
        for index, block in enumerate(blocks):
            border = min(max(cut - index * share, 0), share)
            if border > 0:
                before.append((block, (0, border)))
            if border < share:
                after.append((block, (border, share)))
        first = stats_of(spots, 0, before, (), (2, cut))
        stats = stats_of(spots, cut, after, (first,), (groups * chips, 2, share))
    else:
        fixed = jnp.arange(groups, dtype=jnp.int32)
        pieces = [
            stats_of(fixed, d * lines, [(block, (0, lines))], (), (groups, 2, share))
            for d, block in enumerate(blocks)
        ]
        pieces = jnp.concatenate(pieces, axis=0)
        stats = jnp.zeros_like(pieces).at[spots].set(pieces)

    lse, hit = combine([stats] + [along(stats, k) for k in range(1, groups)])
    stats = jnp.stack((lse, hit), axis=1)
    lse, hit = combine([stats] + [across(stats, d) for d in offsets])
    logprob = hit - lse
    ratio = logprob[:, :tokens] - logprob[:, tokens:]
    other = partner(ratio)
    token_ratio = lax.dynamic_index_in_dim(ratio, group * chips + chip, keepdims=False)

    mine = owners == device
    ends = jnp.cumsum(seq_lengths)
    length = jnp.sum(jnp.where(mine, seq_lengths, 0))
    end = jnp.sum(jnp.where(mine, ends, 0))
    row = jnp.arange(groups * chips, dtype=jnp.int32)[:, None]
    lane = jnp.arange(tokens, dtype=jnp.int32)[None, :]
    position = (2 * row + core) * tokens + lane
    inside = (position >= end - length) & (position < end)
    position = (2 * row + 1 - core) * tokens + lane
    inside_other = (position >= end - length) & (position < end)
    mean = jnp.sum(jnp.where(inside, ratio, 0.0) + jnp.where(inside_other, other, 0.0))
    return (token_ratio, (mean / length.astype(jnp.float32)).reshape(1))


def solution(mesh):
    names = ("grp", "chip", "core")
    groups, plane = mesh.devices.shape
    fine = Mesh(mesh.devices.reshape(groups, plane // 2, 2), names)
    return jax.shard_map(
        local,
        mesh=fine,
        in_specs=(
            P(names, None), P(names, None), P(names, None), P(names, None),
            P(names, None), P(names, None),
            P(names[1:], None, None), P(names[1:], None, None), P(names[1:], None, None),
            P(), P(names, None), P(names), P(), P(),
        ),
        out_specs=(P(names), P(names)),
        check_vma=False,
    )
```

```python
import functools
import math

import jax
import jax.numpy as jnp
from jax import lax
from jax.experimental import pallas as pl
from jax.experimental.pallas import tpu as pltpu
from jax.sharding import Mesh, PartitionSpec as P

MIB = 1 << 20
LOW = -1e30


def round_up(value, step):
    return -(-value // step) * step


def largest_tile(rows, limit, step):
    best = rows
    for tile in range(step, min(rows, limit) + 1, step):
        if rows % tile == 0:
            best = tile
    return best


def pack_kernel(pol_ref, ref_ref, pol_routes, ref_routes, pol_gates, ref_gates, out_ref, room):
    tokens, width = pol_ref.shape
    experts = (room.shape[1] - width) // 2
    parts = ((pol_ref, pol_routes, pol_gates), (ref_ref, ref_routes, ref_gates))
    for index, (hidden, routes, gates) in enumerate(parts):
        band = pl.ds(index * tokens, tokens)
        room[band, :width] = hidden[...].astype(jnp.float32)
        expert = lax.broadcasted_iota(jnp.int32, (experts, tokens), 0)
        dense = jnp.zeros((experts, tokens), jnp.float32)
        for k in range(routes.shape[0]):
            dense = jnp.where(expert == routes[pl.ds(k, 1), :], gates[pl.ds(k, 1), :], dense)
        high = dense.astype(jnp.bfloat16).astype(jnp.float32)
        table = jnp.concatenate((high, dense - high), axis=0)
        room[band, width:] = table.T
    out_ref[...] = room[...].astype(jnp.bfloat16)


def pack_rows(pol_hidden, ref_hidden, pol_routes, ref_routes, pol_gates, ref_gates, experts):
    tokens, width = pol_hidden.shape
    shape = (2 * tokens, width + 2 * experts)
    return pl.pallas_call(
        pack_kernel,
        out_shape=jax.ShapeDtypeStruct(shape, jnp.bfloat16),
        scratch_shapes=[pltpu.VMEM(shape, jnp.float32)],
        compiler_params=pltpu.CompilerParams(vmem_limit_bytes=58 * MIB),
    )(pol_hidden, ref_hidden, pol_routes.T, ref_routes.T, pol_gates.T, ref_gates.T)


def expert_kernel(block, slots, width, experts, chips, place_ref, early_ref, *refs):
    del early_ref
    count = 2 * chips
    blocks, refs = refs[:count], refs[count:]
    gate_ref, up_ref, down_ref, keep_ref, give_ref = refs[:5]
    rows_in, table, pick, weight, picked, made, gate_buf, up_buf, down_buf, arrived = refs[5:]
    step = pl.program_id(0)
    last = pl.num_programs(0) - 1
    rows = rows_in.shape[0]
    share = rows // count
    local_experts = pick.shape[0] // slots
    chip, core = place_ref[0], place_ref[1]

    def weight_copies(e):
        pairs = ((gate_ref, gate_buf), (up_ref, up_buf), (down_ref, down_buf))
        return [
            pltpu.make_async_copy(source.at[e], buffer.at[e], arrived.at[index, e])
            for index, (source, buffer) in enumerate(pairs)
        ]

    @pl.when(step == 0)
    def _():
        for e in range(local_experts):
            for copy in weight_copies(e):
                copy.start()
        for index, ref in enumerate(blocks):
            owner = 2 * (chip ^ (index % chips)) + (core ^ (index // chips))
            rows_in[pl.ds(pl.multiple_of(owner * share, 16), share), :] = ref[...]
        gates = rows_in[:, width:].astype(jnp.float32).T
        hits = (gates > 0.0).astype(jnp.bfloat16)
        span = math.gcd(rows, 16 * block)
        before = lax.broadcasted_iota(jnp.int32, (span, span), 0)
        after = lax.broadcasted_iota(jnp.int32, (1, span), 1)
        first = after - after % block
        order = ((before < after) & (before >= first)).astype(jnp.bfloat16)
        per_block = slots // (rows // block)
        for start in range(0, rows, span):
            band = slice(start, start + span)
            rank = jnp.dot(hits[:, band], order, preferred_element_type=jnp.float32)
            slot = rank + ((start + after) // block * per_block).astype(jnp.float32)
            table[0, :, band] = jnp.where(gates[:, band] > 0.0, slot, -1.0)
        table[1] = gates
        spot = lax.broadcasted_iota(jnp.int32, (slots, rows), 0).astype(jnp.float32)
        for e in range(local_experts):
            row = (2 * chip + core) * local_experts + e
            chosen = table[0, pl.ds(row, 1), :] == spot
            band = pl.ds(e * slots, slots)
            pick[band, :] = jnp.where(chosen, 1.0, 0.0).astype(jnp.bfloat16)
            gate = table[1, pl.ds(row, 1), :] + table[1, pl.ds(row + experts, 1), :]
            weight[band, :] = jnp.sum(jnp.where(chosen, gate, 0.0), axis=1, keepdims=True)
        picked[...] = jnp.dot(
            pick[...], rows_in[:, :width], preferred_element_type=jnp.float32
        ).astype(jnp.bfloat16)

    band = pl.ds(pl.multiple_of(step * slots, slots), slots)
    mine = picked[band, :]
    for copy in weight_copies(step):
        copy.wait()
    gate_act = jnp.dot(mine, gate_buf[step], preferred_element_type=jnp.float32)
    up_act = jnp.dot(mine, up_buf[step], preferred_element_type=jnp.float32)
    inner = (gate_act / (1.0 + jnp.exp(-gate_act)) * up_act).astype(jnp.bfloat16)
    output = jnp.dot(inner, down_buf[step], preferred_element_type=jnp.float32).astype(jnp.bfloat16)
    scaled = output.astype(jnp.float32) * weight[band, :]
    high = scaled.astype(jnp.bfloat16)
    made[band, :width] = high
    made[band, width:] = (scaled - high.astype(jnp.float32)).astype(jnp.bfloat16)

    @pl.when(step == last)
    def _():
        over_slots = (((0,), (0,)), ((), ()))
        span = math.gcd(rows, 16 * block)
        for start in range(0, rows, span):
            band = pl.ds(start, span)
            total = lax.dot_general(
                pick[:, band], made[...], over_slots, preferred_element_type=jnp.float32
            )
            total = total[:, :width] + total[:, width:]
            for index in range(span // share):
                c, owner = divmod(start // share + index, 2)
                target = total[index * share:(index + 1) * share]

                @pl.when(core == owner)
                def _():
                    keep_ref[c ^ chip] = target

                @pl.when(core != owner)
                def _():
                    give_ref[c ^ chip] = target


def expert_sums(place, early, blocks, w_gate, w_up, w_down, block, capacity, width, experts):
    count = len(blocks)
    share, wide = blocks[0].shape
    rows = count * share
    local_experts, _, hidden = w_gate.shape
    slots = round_up(capacity, 8) * (rows // block)
    every = local_experts * slots
    half = jax.ShapeDtypeStruct((count // 2, share, width), jnp.float32)
    whole = pl.BlockSpec(
        (share, wide), lambda e, place: (0, 0), pipeline_mode=pl.Buffered(1)
    )
    return pl.pallas_call(
        functools.partial(expert_kernel, block, slots, width, experts, count // 2),
        out_shape=(half, half),
        grid_spec=pltpu.PrefetchScalarGridSpec(
            num_scalar_prefetch=1,
            grid=(local_experts,),
            in_specs=[pl.BlockSpec(memory_space=pl.ANY)] + [whole] * count + [
                pl.BlockSpec(memory_space=pl.ANY) for _ in range(3)
            ],
            out_specs=(
                pl.BlockSpec(
                    half.shape, lambda e, place: (0, 0, 0), pipeline_mode=pl.Buffered(1)
                ),
                pl.BlockSpec(
                    half.shape, lambda e, place: (0, 0, 0), pipeline_mode=pl.Buffered(1)
                ),
            ),
            scratch_shapes=[
                pltpu.VMEM((rows, wide), jnp.bfloat16),
                pltpu.VMEM((2, wide - width, rows), jnp.float32),
                pltpu.VMEM((every, rows), jnp.bfloat16),
                pltpu.VMEM((every, 1), jnp.float32),
                pltpu.VMEM((every, width), jnp.bfloat16),
                pltpu.VMEM((every, 2 * width), jnp.bfloat16),
                pltpu.VMEM(w_gate.shape, jnp.bfloat16),
                pltpu.VMEM(w_up.shape, jnp.bfloat16),
                pltpu.VMEM(w_down.shape, jnp.bfloat16),
                pltpu.SemaphoreType.DMA((3, local_experts)),
            ],
        ),
        compiler_params=pltpu.CompilerParams(
            vmem_limit_bytes=60 * MIB
        ),
        cost_estimate=pl.CostEstimate(
            flops=2 * every * width * (3 * hidden + 3 * rows),
            bytes_accessed=w_gate.size * 6 + rows * wide * 2 + rows * width * 4,
            transcendentals=every * hidden,
        ),
    )(place, early, *blocks, w_gate, w_up, w_down)


def pair_kernel(keep_ref, came_ref, goal_ref, own_ref, *sends):
    own_ref[...] = keep_ref[0] + came_ref[0]
    share, lines = keep_ref.shape[1], goal_ref.shape[1]
    for index, send in enumerate(sends):
        send[:share] = keep_ref[index + 1] + came_ref[index + 1]
        send[share:] = jnp.zeros((send.shape[0] - share, send.shape[1]), jnp.float32)
        send[share:share + 1, :lines] = goal_ref[...]


def pair_sums(keep, came, goal):
    chips, share, width = keep.shape
    own = jax.ShapeDtypeStruct((share, width), jnp.float32)
    send = jax.ShapeDtypeStruct((share + 8, width), jnp.float32)
    return pl.pallas_call(
        pair_kernel,
        out_shape=(own,) + (send,) * (chips - 1),
        compiler_params=pltpu.CompilerParams(vmem_limit_bytes=24 * MIB),
    )(keep, came, goal)


def norm_kernel(hidden_ref, gain_ref, goal_ref, own_ref, *refs):
    came, normed_ref, wanted_ref = refs[:-2], refs[-2], refs[-1]
    share, width = own_ref.shape
    lines = goal_ref.shape[1]
    mixed = hidden_ref[:, :width].astype(jnp.float32) + own_ref[...]
    wanted_ref[0:1, :] = goal_ref[...].astype(jnp.int32)
    for index, ref in enumerate(came):
        mixed += ref[:share]
        wanted_ref[index + 1:index + 2, :] = ref[share:share + 1, :lines].astype(jnp.int32)
    scale = lax.rsqrt(jnp.mean(mixed * mixed, axis=1, keepdims=True) + 1e-06)
    normed_ref[...] = (mixed * scale * gain_ref[...]).astype(jnp.bfloat16)


def norm_rows(hidden, gain, goal, own, came):
    return pl.pallas_call(
        norm_kernel,
        out_shape=(
            jax.ShapeDtypeStruct(own.shape, jnp.bfloat16),
            jax.ShapeDtypeStruct((len(came) + 1, goal.shape[1]), jnp.int32),
        ),
        compiler_params=pltpu.CompilerParams(vmem_limit_bytes=16 * MIB),
    )(hidden, gain.reshape(1, -1), goal, own, *came)


def split_kernel(keep_ref, came_ref, goal_ref, own_ref, mid_x, mid_y, send_x, send_y):
    share, width = own_ref.shape
    half, lines = width // 2, goal_ref.shape[1]
    left, right = slice(0, half), slice(half, width)

    def total(d, side):
        return keep_ref[d, :, side] + came_ref[d, :, side]

    own_ref[...] = keep_ref[0] + came_ref[0]
    mid_x[...] = total(1, right)
    mid_y[...] = total(2, left)
    for send, near, side in ((send_x, 1, left), (send_y, 2, right)):
        send[:share] = total(near, side)
        send[share:2 * share] = total(3, side)
        send[2 * share:] = jnp.zeros((8, half), jnp.float32)
        send[2 * share:2 * share + 1, :lines] = goal_ref[...]


def split_sums(keep, came, goal):
    _, share, width = keep.shape
    own = jax.ShapeDtypeStruct((share, width), jnp.float32)
    middle = jax.ShapeDtypeStruct((share, width // 2), jnp.float32)
    send = jax.ShapeDtypeStruct((2 * share + 8, width // 2), jnp.float32)
    return pl.pallas_call(
        split_kernel,
        out_shape=(own, middle, middle, send, send),
        compiler_params=pltpu.CompilerParams(vmem_limit_bytes=24 * MIB),
    )(keep, came, goal)


def middle_kernel(mid_x, mid_y, from_x, from_y, next_x, next_y):
    share = mid_x.shape[0]
    next_x[...] = mid_x[...] + from_y[share:2 * share]
    next_y[:share] = mid_y[...] + from_x[share:2 * share]
    next_y[share:] = from_x[2 * share:]


def middle_sums(mid_x, mid_y, from_x, from_y):
    share, half = mid_x.shape
    return pl.pallas_call(
        middle_kernel,
        out_shape=(
            jax.ShapeDtypeStruct((share, half), jnp.float32),
            jax.ShapeDtypeStruct((share + 8, half), jnp.float32),
        ),
        compiler_params=pltpu.CompilerParams(vmem_limit_bytes=16 * MIB),
    )(mid_x, mid_y, from_x, from_y)


def join_kernel(
    hidden_ref, gain_ref, goal_ref, own_ref, from_x, from_y, last_x, last_y, normed_ref, wanted_ref
):
    share, width = own_ref.shape
    lines = goal_ref.shape[1]
    came = jnp.concatenate(
        (from_x[:share] + last_y[:share], from_y[:share] + last_x[...]), axis=1
    )
    mixed = hidden_ref[:, :width].astype(jnp.float32) + own_ref[...] + came
    scale = lax.rsqrt(jnp.mean(mixed * mixed, axis=1, keepdims=True) + 1e-06)
    normed_ref[...] = (mixed * scale * gain_ref[...]).astype(jnp.bfloat16)
    wanted_ref[0:1, :] = goal_ref[...].astype(jnp.int32)
    wanted_ref[1:2, :] = from_x[2 * share:2 * share + 1, :lines].astype(jnp.int32)
    wanted_ref[2:3, :] = from_y[2 * share:2 * share + 1, :lines].astype(jnp.int32)
    wanted_ref[3:4, :] = last_y[share:share + 1, :lines].astype(jnp.int32)


def join_rows(hidden, gain, goal, own, *parts):
    return pl.pallas_call(
        join_kernel,
        out_shape=(
            jax.ShapeDtypeStruct(own.shape, jnp.bfloat16),
            jax.ShapeDtypeStruct((4, goal.shape[1]), jnp.int32),
        ),
        compiler_params=pltpu.CompilerParams(vmem_limit_bytes=16 * MIB),
    )(hidden, gain.reshape(1, -1), goal, own, *parts)


def head_kernel(parts, before, spots_ref, wanted_ref, *refs):
    blocks, refs = refs[:len(parts)], refs[len(parts):]
    earlier, refs = refs[:before], refs[before:]
    head_a, head_b, out_ref, rows_in, peak, total, found, logits_a, logits_b = refs
    step = pl.program_id(0)
    last = pl.num_programs(0) - 1
    tile, columns = logits_a.shape
    base_a, base_b = spots_ref[0], spots_ref[1]

    def product(head_ref, logits):
        logits[...] = lax.dot_general(
            head_ref[...], rows_in[...], (((1,), (1,)), ((), ())),
            preferred_element_type=jnp.float32,
        )

    def absorb(logits, first):
        for start in range(0, columns, 128):
            lanes = min(128, columns - start)
            band = pl.ds(start, lanes)
            row = lax.broadcasted_iota(jnp.int32, (tile, lanes), 0)
            values = logits[:, band]
            old = peak[:, band]
            new = jnp.maximum(old, jnp.max(values.reshape(tile // 8, 8, lanes), axis=0))
            grown = jnp.exp(values.reshape(tile // 8, 8, lanes) - new[None])
            total[:, band] = total[:, band] * jnp.exp(old - new) + jnp.sum(grown, axis=0)
            same = row == wanted_ref[:, band] - first
            kept = jnp.where(same, values, 0.0).reshape(tile // 8, 8, lanes)
            found[:, band] += jnp.sum(kept, axis=0)
            peak[:, band] = new

    @pl.when(step == 0)
    def _():
        start = 0
        for ref, (low, high) in zip(blocks, parts):
            rows_in[start:start + high - low, :] = ref[low:high, :]
            start += high - low
        peak[...] = jnp.full_like(peak, LOW)
        total[...] = jnp.zeros_like(total)
        found[...] = jnp.zeros_like(found)
        logits_b[...] = jnp.full_like(logits_b, LOW)

    product(head_a, logits_a)
    absorb(logits_b, jnp.where(step == 0, -(1 << 28), base_b + (step - 1) * tile))
    product(head_b, logits_b)
    absorb(logits_a, base_a + step * tile)

    @pl.when(step == last)
    def _():
        absorb(logits_b, base_b + step * tile)
        top = jnp.max(peak[...], axis=0, keepdims=True)
        full = jnp.sum(total[...] * jnp.exp(peak[...] - top), axis=0, keepdims=True)
        lse = top + jnp.log(full)
        hit = jnp.sum(found[...], axis=0, keepdims=True)
        lse = jnp.concatenate([ref[0:1, :] for ref in earlier] + [lse], axis=1)
        hit = jnp.concatenate([ref[1:2, :] for ref in earlier] + [hit], axis=1)
        if len(out_ref.shape) == 2:
            out_ref[0:1, :] = lse
            out_ref[1:2, :] = hit
        else:
            share = out_ref.shape[2]
            for index in range(out_ref.shape[0]):
                band = slice(index * share, (index + 1) * share)
                spot = spots_ref[2 + index]
                out_ref[spot, 0:1, :] = lse[:, band]
                out_ref[spot, 1:2, :] = hit[:, band]


def head_stats(spots, wanted, blocks, parts, earlier, head_a, head_b, shape):
    rows = sum(high - low for low, high in parts)
    width = head_a.shape[1]
    whole = pl.BlockSpec(shape, lambda s, spots: (0,) * len(shape))
    tile = largest_tile(head_a.shape[0], 608, 16)
    steps = head_a.shape[0] // tile
    return pl.pallas_call(
        functools.partial(head_kernel, parts, len(earlier)),
        out_shape=jax.ShapeDtypeStruct(shape, jnp.float32),
        grid_spec=pltpu.PrefetchScalarGridSpec(
            num_scalar_prefetch=1,
            grid=(steps,),
            in_specs=[pl.BlockSpec((1, rows), lambda s, spots: (0, 0))] + [
                pl.BlockSpec(block.shape, lambda s, spots: (0, 0), pipeline_mode=pl.Buffered(1))
                for block in blocks
            ] + [
                pl.BlockSpec(part.shape, lambda s, spots: (0, 0)) for part in earlier
            ] + [
                pl.BlockSpec((tile, width), lambda s, spots: (s, 0)),
                pl.BlockSpec((tile, width), lambda s, spots: (s, 0)),
            ],
            out_specs=whole,
            scratch_shapes=[
                pltpu.VMEM((rows, width), jnp.bfloat16),
                pltpu.VMEM((8, rows), jnp.float32),
                pltpu.VMEM((8, rows), jnp.float32),
                pltpu.VMEM((8, rows), jnp.float32),
                pltpu.VMEM((tile, rows), jnp.float32),
                pltpu.VMEM((tile, rows), jnp.float32),
            ],
        ),
        compiler_params=pltpu.CompilerParams(vmem_limit_bytes=60 * MIB),
        cost_estimate=pl.CostEstimate(
            flops=4 * rows * width * head_a.shape[0],
            bytes_accessed=head_a.size * 4 + rows * width * 2,
            transcendentals=2 * rows * head_a.shape[0],
        ),
    )(spots, wanted, *blocks, *earlier, head_a, head_b)


def combine(parts):
    top = functools.reduce(jnp.maximum, [part[:, 0] for part in parts])
    total = sum(jnp.exp(part[:, 0] - top) for part in parts)
    return top + jnp.log(total), sum(part[:, 1] for part in parts)


def across(value, offset):
    chips = lax.axis_size("chip")
    return lax.ppermute(value, "chip", [(c, c ^ offset) for c in range(chips)])


def along(value, offset):
    groups = lax.axis_size("grp")
    return lax.ppermute(value, "grp", [(g, (g + offset) % groups) for g in range(groups)])


def partner(value):
    return lax.ppermute(value, "core", ((0, 1), (1, 0)))


def local(
    pol_hidden, ref_hidden, pol_routes, ref_routes, pol_gates, ref_gates,
    w_gate, w_up, w_down, norm_gain, vocab_head, targets, seq_lengths, owners,
):
    chip, core, group = lax.axis_index("chip"), lax.axis_index("core"), lax.axis_index("grp")
    chips, groups = lax.axis_size("chip"), lax.axis_size("grp")
    device = (group * chips + chip) * 2 + core
    experts = w_gate.shape[0] * chips * 2
    tokens, width = pol_hidden.shape
    share = 2 * tokens
    capacity = tokens * pol_routes.shape[1] // experts + 2
    vocab_rows = vocab_head.shape[0]
    offsets = range(1, chips)

    send = pack_rows(
        pol_hidden, ref_hidden, pol_routes, ref_routes, pol_gates, ref_gates, experts
    )
    plane = [send] + [across(send, d) for d in offsets]
    plane = plane + [partner(rows) for rows in plane]

    home = (group - jnp.arange(groups, dtype=jnp.int32)) % groups
    spots = home[None, :] * chips + (chip ^ jnp.arange(chips, dtype=jnp.int32))[:, None]
    spots = spots.reshape(-1)
    goal = targets.astype(jnp.float32).reshape(1, tokens)
    goal = jnp.concatenate((goal, goal), axis=1)
    goal = jnp.broadcast_to(goal, (groups, share))
    goal = lax.all_to_all(goal, "grp", split_axis=0, concat_axis=0, tiled=True)
    match = home[:, None] == jnp.arange(groups, dtype=jnp.int32)[None, :]
    goal = jnp.sum(jnp.where(match[:, :, None], goal[None], 0.0), axis=1).reshape(1, -1)
    other_head = partner(vocab_head)

    place = jnp.stack((chip, core)).astype(jnp.int32)
    keep, give = expert_sums(
        place, goal, plane, w_gate, w_up, w_down, tokens, capacity, width, experts
    )
    if chips == 4 and groups * share <= width // 2:
        own, mid_x, mid_y, send_x, send_y = split_sums(keep, partner(give), goal)
        from_x, from_y = across(send_x, 1), across(send_y, 2)
        next_x, next_y = middle_sums(mid_x, mid_y, from_x, from_y)
        last_x, last_y = across(next_x, 1), across(next_y, 2)
        normed, wanted = join_rows(
            send, norm_gain, goal, own, from_x, from_y, last_x, last_y
        )
    else:
        own, *sends = pair_sums(keep, partner(give), goal)
        came = [across(rows, d) for d, rows in zip(offsets, sends)]
        normed, wanted = norm_rows(send, norm_gain, goal, own, came)
    wanted = wanted.reshape(1, -1)

    column = [normed] + [along(normed, k) for k in range(1, groups)]
    if chips == 4:
        near = [across(rows, 1) for rows in column]
        far = [across(rows, 2) for rows in column]
        half = groups // 2
        cross = [across(rows, 2) for rows in near[:half]] + [
            across(rows, 1) for rows in far[half:]
        ]
    else:
        column = jnp.concatenate(column, axis=0)
        blocks = [column] + [across(column, d) for d in offsets]
    base = jnp.stack((device, device + 1 - 2 * core)).astype(jnp.int32) * vocab_rows
    lines = groups * share

    def stats_of(places, start, pieces, earlier, shape):
        blocks, parts = [block for block, _ in pieces], tuple(part for _, part in pieces)
        end = start + sum(high - low for low, high in parts)
        places = jnp.concatenate((base, places))
        return head_stats(
            places, wanted[:, start:end], blocks, parts, earlier, vocab_head, other_head, shape
        )

    if chips == 4:
        blocks = column + near + far + cross
        cut = max(256, (3 * lines - share) // 256 * 256)
        before, after = [], []
        for index, block in enumerate(blocks):
            border = min(max(cut - index * share, 0), share)
            if border > 0:
                before.append((block, (0, border)))
            if border < share:
                after.append((block, (border, share)))
        first = stats_of(spots, 0, before, (), (2, cut))
        stats = stats_of(spots, cut, after, (first,), (groups * chips, 2, share))
    else:
        fixed = jnp.arange(groups, dtype=jnp.int32)
        pieces = [
            stats_of(fixed, d * lines, [(block, (0, lines))], (), (groups, 2, share))
            for d, block in enumerate(blocks)
        ]
        pieces = jnp.concatenate(pieces, axis=0)
        stats = jnp.zeros_like(pieces).at[spots].set(pieces)

    lse, hit = combine([stats] + [along(stats, k) for k in range(1, groups)])
    stats = jnp.stack((lse, hit), axis=1)
    lse, hit = combine([stats] + [across(stats, d) for d in offsets])
    logprob = hit - lse
    ratio = logprob[:, :tokens] - logprob[:, tokens:]
    other = partner(ratio)
    token_ratio = lax.dynamic_index_in_dim(ratio, group * chips + chip, keepdims=False)

    mine = owners == device
    ends = jnp.cumsum(seq_lengths)
    length = jnp.sum(jnp.where(mine, seq_lengths, 0))
    end = jnp.sum(jnp.where(mine, ends, 0))
    row = jnp.arange(groups * chips, dtype=jnp.int32)[:, None]
    lane = jnp.arange(tokens, dtype=jnp.int32)[None, :]
    position = (2 * row + core) * tokens + lane
    inside = (position >= end - length) & (position < end)
    position = (2 * row + 1 - core) * tokens + lane
    inside_other = (position >= end - length) & (position < end)
    mean = jnp.sum(jnp.where(inside, ratio, 0.0) + jnp.where(inside_other, other, 0.0))
    return (token_ratio, (mean / length.astype(jnp.float32)).reshape(1))


def solution(mesh):
    names = ("grp", "chip", "core")
    groups, plane = mesh.devices.shape
    fine = Mesh(mesh.devices.reshape(groups, plane // 2, 2), names)
    return jax.shard_map(
        local,
        mesh=fine,
        in_specs=(
            P(names, None), P(names, None), P(names, None), P(names, None),
            P(names, None), P(names, None),
            P(names[1:], None, None), P(names[1:], None, None), P(names[1:], None, None),
            P(), P(names, None), P(names), P(), P(),
        ),
        out_specs=(P(names), P(names)),
        check_vma=False,
    )
```

```python
import functools
import math

import jax
import jax.numpy as jnp
from jax import lax
from jax.experimental import pallas as pl
from jax.experimental.pallas import tpu as pltpu
from jax.sharding import Mesh, PartitionSpec as P

MIB = 1 << 20
LOW = -1e30


def round_up(value, step):
    return -(-value // step) * step


def largest_tile(rows, limit, step):
    best = rows
    for tile in range(step, min(rows, limit) + 1, step):
        if rows % tile == 0:
            best = tile
    return best


def pack_kernel(pol_ref, ref_ref, pol_routes, ref_routes, pol_gates, ref_gates, out_ref, room):
    tokens, width = pol_ref.shape
    experts = (room.shape[1] - width) // 2
    parts = ((pol_ref, pol_routes, pol_gates), (ref_ref, ref_routes, ref_gates))
    for index, (hidden, routes, gates) in enumerate(parts):
        band = pl.ds(index * tokens, tokens)
        room[band, :width] = hidden[...].astype(jnp.float32)
        expert = lax.broadcasted_iota(jnp.int32, (experts, tokens), 0)
        dense = jnp.zeros((experts, tokens), jnp.float32)
        for k in range(routes.shape[0]):
            dense = jnp.where(expert == routes[pl.ds(k, 1), :], gates[pl.ds(k, 1), :], dense)
        high = dense.astype(jnp.bfloat16).astype(jnp.float32)
        table = jnp.concatenate((high, dense - high), axis=0)
        room[band, width:] = table.T
    out_ref[...] = room[...].astype(jnp.bfloat16)


def pack_rows(pol_hidden, ref_hidden, pol_routes, ref_routes, pol_gates, ref_gates, experts):
    tokens, width = pol_hidden.shape
    shape = (2 * tokens, width + 2 * experts)
    return pl.pallas_call(
        pack_kernel,
        out_shape=jax.ShapeDtypeStruct(shape, jnp.bfloat16),
        scratch_shapes=[pltpu.VMEM(shape, jnp.float32)],
        compiler_params=pltpu.CompilerParams(vmem_limit_bytes=58 * MIB),
    )(pol_hidden, ref_hidden, pol_routes.T, ref_routes.T, pol_gates.T, ref_gates.T)


def expert_kernel(block, slots, width, experts, chips, place_ref, early_ref, *refs):
    del early_ref
    count = 2 * chips
    blocks, refs = refs[:count], refs[count:]
    gate_ref, up_ref, down_ref, keep_ref, give_ref = refs[:5]
    rows_in, table, pick, weight, picked, made, gate_buf, up_buf, down_buf, arrived = refs[5:]
    step = pl.program_id(0)
    last = pl.num_programs(0) - 1
    rows = rows_in.shape[0]
    share = rows // count
    local_experts = pick.shape[0] // slots
    chip, core = place_ref[0], place_ref[1]

    def weight_copies(e):
        pairs = ((gate_ref, gate_buf), (up_ref, up_buf), (down_ref, down_buf))
        return [
            pltpu.make_async_copy(source.at[e], buffer.at[e], arrived.at[index, e])
            for index, (source, buffer) in enumerate(pairs)
        ]

    @pl.when(step == 0)
    def _():
        for e in range(local_experts):
            for copy in weight_copies(e):
                copy.start()
        for index, ref in enumerate(blocks):
            owner = 2 * (chip ^ (index % chips)) + (core ^ (index // chips))
            rows_in[pl.ds(pl.multiple_of(owner * share, 16), share), :] = ref[...]
        gates = rows_in[:, width:].astype(jnp.float32).T
        hits = (gates > 0.0).astype(jnp.bfloat16)
        span = math.gcd(rows, 16 * block)
        before = lax.broadcasted_iota(jnp.int32, (span, span), 0)
        after = lax.broadcasted_iota(jnp.int32, (1, span), 1)
        first = after - after % block
        order = ((before < after) & (before >= first)).astype(jnp.bfloat16)
        per_block = slots // (rows // block)
        for start in range(0, rows, span):
            band = slice(start, start + span)
            rank = jnp.dot(hits[:, band], order, preferred_element_type=jnp.float32)
            slot = rank + ((start + after) // block * per_block).astype(jnp.float32)
            table[0, :, band] = jnp.where(gates[:, band] > 0.0, slot, -1.0)
        table[1] = gates
        spot = lax.broadcasted_iota(jnp.int32, (slots, rows), 0).astype(jnp.float32)
        for e in range(local_experts):
            row = (2 * chip + core) * local_experts + e
            chosen = table[0, pl.ds(row, 1), :] == spot
            band = pl.ds(e * slots, slots)
            pick[band, :] = jnp.where(chosen, 1.0, 0.0).astype(jnp.bfloat16)
            gate = table[1, pl.ds(row, 1), :] + table[1, pl.ds(row + experts, 1), :]
            weight[band, :] = jnp.sum(jnp.where(chosen, gate, 0.0), axis=1, keepdims=True)
        picked[...] = jnp.dot(
            pick[...], rows_in[:, :width], preferred_element_type=jnp.float32
        ).astype(jnp.bfloat16)

    band = pl.ds(pl.multiple_of(step * slots, slots), slots)
    mine = picked[band, :]
    for copy in weight_copies(step):
        copy.wait()
    gate_act = jnp.dot(mine, gate_buf[step], preferred_element_type=jnp.float32)
    up_act = jnp.dot(mine, up_buf[step], preferred_element_type=jnp.float32)
    inner = (gate_act / (1.0 + jnp.exp(-gate_act)) * up_act).astype(jnp.bfloat16)
    output = jnp.dot(inner, down_buf[step], preferred_element_type=jnp.float32).astype(jnp.bfloat16)
    scaled = output.astype(jnp.float32) * weight[band, :]
    high = scaled.astype(jnp.bfloat16)
    made[band, :width] = high
    made[band, width:] = (scaled - high.astype(jnp.float32)).astype(jnp.bfloat16)

    @pl.when(step == last)
    def _():
        over_slots = (((0,), (0,)), ((), ()))
        span = math.gcd(rows, 16 * block)
        for start in range(0, rows, span):
            band = pl.ds(start, span)
            total = lax.dot_general(
                pick[:, band], made[...], over_slots, preferred_element_type=jnp.float32
            )
            total = total[:, :width] + total[:, width:]
            for index in range(span // share):
                c, owner = divmod(start // share + index, 2)
                target = total[index * share:(index + 1) * share]

                @pl.when(core == owner)
                def _():
                    keep_ref[c ^ chip] = target

                @pl.when(core != owner)
                def _():
                    give_ref[c ^ chip] = target


def expert_sums(place, early, blocks, w_gate, w_up, w_down, block, capacity, width, experts):
    count = len(blocks)
    share, wide = blocks[0].shape
    rows = count * share
    local_experts, _, hidden = w_gate.shape
    slots = round_up(capacity, 8) * (rows // block)
    every = local_experts * slots
    half = jax.ShapeDtypeStruct((count // 2, share, width), jnp.float32)
    whole = pl.BlockSpec(
        (share, wide), lambda e, place: (0, 0), pipeline_mode=pl.Buffered(1)
    )
    return pl.pallas_call(
        functools.partial(expert_kernel, block, slots, width, experts, count // 2),
        out_shape=(half, half),
        grid_spec=pltpu.PrefetchScalarGridSpec(
            num_scalar_prefetch=1,
            grid=(local_experts,),
            in_specs=[pl.BlockSpec(memory_space=pl.ANY)] + [whole] * count + [
                pl.BlockSpec(memory_space=pl.ANY) for _ in range(3)
            ],
            out_specs=(
                pl.BlockSpec(
                    half.shape, lambda e, place: (0, 0, 0), pipeline_mode=pl.Buffered(1)
                ),
                pl.BlockSpec(
                    half.shape, lambda e, place: (0, 0, 0), pipeline_mode=pl.Buffered(1)
                ),
            ),
            scratch_shapes=[
                pltpu.VMEM((rows, wide), jnp.bfloat16),
                pltpu.VMEM((2, wide - width, rows), jnp.float32),
                pltpu.VMEM((every, rows), jnp.bfloat16),
                pltpu.VMEM((every, 1), jnp.float32),
                pltpu.VMEM((every, width), jnp.bfloat16),
                pltpu.VMEM((every, 2 * width), jnp.bfloat16),
                pltpu.VMEM(w_gate.shape, jnp.bfloat16),
                pltpu.VMEM(w_up.shape, jnp.bfloat16),
                pltpu.VMEM(w_down.shape, jnp.bfloat16),
                pltpu.SemaphoreType.DMA((3, local_experts)),
            ],
        ),
        compiler_params=pltpu.CompilerParams(
            vmem_limit_bytes=60 * MIB
        ),
        cost_estimate=pl.CostEstimate(
            flops=2 * every * width * (3 * hidden + 3 * rows),
            bytes_accessed=w_gate.size * 6 + rows * wide * 2 + rows * width * 4,
            transcendentals=every * hidden,
        ),
    )(place, early, *blocks, w_gate, w_up, w_down)


def pair_kernel(keep_ref, came_ref, goal_ref, own_ref, *sends):
    own_ref[...] = keep_ref[0] + came_ref[0]
    share, lines = keep_ref.shape[1], goal_ref.shape[1]
    for index, send in enumerate(sends):
        send[:share] = keep_ref[index + 1] + came_ref[index + 1]
        send[share:] = jnp.zeros((send.shape[0] - share, send.shape[1]), jnp.float32)
        send[share:share + 1, :lines] = goal_ref[...]


def pair_sums(keep, came, goal):
    chips, share, width = keep.shape
    own = jax.ShapeDtypeStruct((share, width), jnp.float32)
    send = jax.ShapeDtypeStruct((share + 8, width), jnp.float32)
    return pl.pallas_call(
        pair_kernel,
        out_shape=(own,) + (send,) * (chips - 1),
        compiler_params=pltpu.CompilerParams(vmem_limit_bytes=24 * MIB),
    )(keep, came, goal)


def norm_kernel(hidden_ref, gain_ref, goal_ref, own_ref, *refs):
    came, normed_ref, wanted_ref = refs[:-2], refs[-2], refs[-1]
    share, width = own_ref.shape
    lines = goal_ref.shape[1]
    mixed = hidden_ref[:, :width].astype(jnp.float32) + own_ref[...]
    wanted_ref[0:1, :] = goal_ref[...].astype(jnp.int32)
    for index, ref in enumerate(came):
        mixed += ref[:share]
        wanted_ref[index + 1:index + 2, :] = ref[share:share + 1, :lines].astype(jnp.int32)
    scale = lax.rsqrt(jnp.mean(mixed * mixed, axis=1, keepdims=True) + 1e-06)
    normed_ref[...] = (mixed * scale * gain_ref[...]).astype(jnp.bfloat16)


def norm_rows(hidden, gain, goal, own, came):
    return pl.pallas_call(
        norm_kernel,
        out_shape=(
            jax.ShapeDtypeStruct(own.shape, jnp.bfloat16),
            jax.ShapeDtypeStruct((len(came) + 1, goal.shape[1]), jnp.int32),
        ),
        compiler_params=pltpu.CompilerParams(vmem_limit_bytes=16 * MIB),
    )(hidden, gain.reshape(1, -1), goal, own, *came)


def split_kernel(keep_ref, came_ref, goal_ref, own_ref, mid_x, mid_y, send_x, send_y):
    share, width = own_ref.shape
    half, lines = width // 2, goal_ref.shape[1]
    left, right = slice(0, half), slice(half, width)

    def total(d, side):
        return keep_ref[d, :, side] + came_ref[d, :, side]

    own_ref[...] = keep_ref[0] + came_ref[0]
    mid_x[...] = total(1, right)
    mid_y[...] = total(2, left)
    for send, near, side in ((send_x, 1, left), (send_y, 2, right)):
        send[:share] = total(near, side)
        send[share:2 * share] = total(3, side)
        send[2 * share:] = jnp.zeros((8, half), jnp.float32)
        send[2 * share:2 * share + 1, :lines] = goal_ref[...]


def split_sums(keep, came, goal):
    _, share, width = keep.shape
    own = jax.ShapeDtypeStruct((share, width), jnp.float32)
    middle = jax.ShapeDtypeStruct((share, width // 2), jnp.float32)
    send = jax.ShapeDtypeStruct((2 * share + 8, width // 2), jnp.float32)
    return pl.pallas_call(
        split_kernel,
        out_shape=(own, middle, middle, send, send),
        compiler_params=pltpu.CompilerParams(vmem_limit_bytes=24 * MIB),
    )(keep, came, goal)


def middle_kernel(mid_x, mid_y, from_x, from_y, next_x, next_y):
    share = mid_x.shape[0]
    next_x[...] = mid_x[...] + from_y[share:2 * share]
    next_y[:share] = mid_y[...] + from_x[share:2 * share]
    next_y[share:] = from_x[2 * share:]


def middle_sums(mid_x, mid_y, from_x, from_y):
    share, half = mid_x.shape
    return pl.pallas_call(
        middle_kernel,
        out_shape=(
            jax.ShapeDtypeStruct((share, half), jnp.float32),
            jax.ShapeDtypeStruct((share + 8, half), jnp.float32),
        ),
        compiler_params=pltpu.CompilerParams(vmem_limit_bytes=16 * MIB),
    )(mid_x, mid_y, from_x, from_y)


def join_kernel(
    hidden_ref, gain_ref, goal_ref, own_ref, from_x, from_y, last_x, last_y, normed_ref, wanted_ref
):
    share, width = own_ref.shape
    lines = goal_ref.shape[1]
    came = jnp.concatenate(
        (from_x[:share] + last_y[:share], from_y[:share] + last_x[...]), axis=1
    )
    mixed = hidden_ref[:, :width].astype(jnp.float32) + own_ref[...] + came
    scale = lax.rsqrt(jnp.mean(mixed * mixed, axis=1, keepdims=True) + 1e-06)
    normed_ref[...] = (mixed * scale * gain_ref[...]).astype(jnp.bfloat16)
    wanted_ref[0:1, :] = goal_ref[...].astype(jnp.int32)
    wanted_ref[1:2, :] = from_x[2 * share:2 * share + 1, :lines].astype(jnp.int32)
    wanted_ref[2:3, :] = from_y[2 * share:2 * share + 1, :lines].astype(jnp.int32)
    wanted_ref[3:4, :] = last_y[share:share + 1, :lines].astype(jnp.int32)


def join_rows(hidden, gain, goal, own, *parts):
    return pl.pallas_call(
        join_kernel,
        out_shape=(
            jax.ShapeDtypeStruct(own.shape, jnp.bfloat16),
            jax.ShapeDtypeStruct((4, goal.shape[1]), jnp.int32),
        ),
        compiler_params=pltpu.CompilerParams(vmem_limit_bytes=16 * MIB),
    )(hidden, gain.reshape(1, -1), goal, own, *parts)


def head_kernel(parts, before, spots_ref, wanted_ref, *refs):
    blocks, refs = refs[:len(parts)], refs[len(parts):]
    earlier, refs = refs[:before], refs[before:]
    head_a, head_b, out_ref, rows_in, peak, total, found, logits_a, logits_b = refs
    step = pl.program_id(0)
    last = pl.num_programs(0) - 1
    tile, columns = logits_a.shape
    base_a, base_b = spots_ref[0], spots_ref[1]

    def product(head_ref, logits):
        logits[...] = lax.dot_general(
            head_ref[...], rows_in[...], (((1,), (1,)), ((), ())),
            preferred_element_type=jnp.float32,
        )

    def absorb(logits, first):
        for start in range(0, columns, 128):
            lanes = min(128, columns - start)
            band = pl.ds(start, lanes)
            row = lax.broadcasted_iota(jnp.int32, (tile, lanes), 0)
            values = logits[:, band]
            old = peak[:, band]
            new = jnp.maximum(old, jnp.max(values.reshape(tile // 8, 8, lanes), axis=0))
            grown = jnp.exp(values.reshape(tile // 8, 8, lanes) - new[None])
            total[:, band] = total[:, band] * jnp.exp(old - new) + jnp.sum(grown, axis=0)
            same = row == wanted_ref[:, band] - first
            kept = jnp.where(same, values, 0.0).reshape(tile // 8, 8, lanes)
            found[:, band] += jnp.sum(kept, axis=0)
            peak[:, band] = new

    @pl.when(step == 0)
    def _():
        start = 0
        for ref, (low, high) in zip(blocks, parts):
            rows_in[start:start + high - low, :] = ref[low:high, :]
            start += high - low
        peak[...] = jnp.full_like(peak, LOW)
        total[...] = jnp.zeros_like(total)
        found[...] = jnp.zeros_like(found)
        logits_b[...] = jnp.full_like(logits_b, LOW)

    product(head_a, logits_a)
    absorb(logits_b, jnp.where(step == 0, -(1 << 28), base_b + (step - 1) * tile))
    product(head_b, logits_b)
    absorb(logits_a, base_a + step * tile)

    @pl.when(step == last)
    def _():
        absorb(logits_b, base_b + step * tile)
        top = jnp.max(peak[...], axis=0, keepdims=True)
        full = jnp.sum(total[...] * jnp.exp(peak[...] - top), axis=0, keepdims=True)
        lse = top + jnp.log(full)
        hit = jnp.sum(found[...], axis=0, keepdims=True)
        lse = jnp.concatenate([ref[0:1, :] for ref in earlier] + [lse], axis=1)
        hit = jnp.concatenate([ref[1:2, :] for ref in earlier] + [hit], axis=1)
        if len(out_ref.shape) == 2:
            out_ref[0:1, :] = lse
            out_ref[1:2, :] = hit
        else:
            share = out_ref.shape[2]
            for index in range(out_ref.shape[0]):
                band = slice(index * share, (index + 1) * share)
                spot = spots_ref[2 + index]
                out_ref[spot, 0:1, :] = lse[:, band]
                out_ref[spot, 1:2, :] = hit[:, band]


def head_stats(spots, wanted, blocks, parts, earlier, head_a, head_b, shape):
    rows = sum(high - low for low, high in parts)
    width = head_a.shape[1]
    whole = pl.BlockSpec(shape, lambda s, spots: (0,) * len(shape))
    tile = largest_tile(head_a.shape[0], 608, 16)
    steps = head_a.shape[0] // tile
    return pl.pallas_call(
        functools.partial(head_kernel, parts, len(earlier)),
        out_shape=jax.ShapeDtypeStruct(shape, jnp.float32),
        grid_spec=pltpu.PrefetchScalarGridSpec(
            num_scalar_prefetch=1,
            grid=(steps,),
            in_specs=[pl.BlockSpec((1, rows), lambda s, spots: (0, 0))] + [
                pl.BlockSpec(block.shape, lambda s, spots: (0, 0), pipeline_mode=pl.Buffered(1))
                for block in blocks
            ] + [
                pl.BlockSpec(part.shape, lambda s, spots: (0, 0)) for part in earlier
            ] + [
                pl.BlockSpec((tile, width), lambda s, spots: (s, 0)),
                pl.BlockSpec((tile, width), lambda s, spots: (s, 0)),
            ],
            out_specs=whole,
            scratch_shapes=[
                pltpu.VMEM((rows, width), jnp.bfloat16),
                pltpu.VMEM((8, rows), jnp.float32),
                pltpu.VMEM((8, rows), jnp.float32),
                pltpu.VMEM((8, rows), jnp.float32),
                pltpu.VMEM((tile, rows), jnp.float32),
                pltpu.VMEM((tile, rows), jnp.float32),
            ],
        ),
        compiler_params=pltpu.CompilerParams(vmem_limit_bytes=60 * MIB),
        cost_estimate=pl.CostEstimate(
            flops=4 * rows * width * head_a.shape[0],
            bytes_accessed=head_a.size * 4 + rows * width * 2,
            transcendentals=2 * rows * head_a.shape[0],
        ),
    )(spots, wanted, *blocks, *earlier, head_a, head_b)


def combine(parts):
    top = functools.reduce(jnp.maximum, [part[:, 0] for part in parts])
    total = sum(jnp.exp(part[:, 0] - top) for part in parts)
    return top + jnp.log(total), sum(part[:, 1] for part in parts)


def across(value, offset):
    chips = lax.axis_size("chip")
    return lax.ppermute(value, "chip", [(c, c ^ offset) for c in range(chips)])


def along(value, offset):
    groups = lax.axis_size("grp")
    return lax.ppermute(value, "grp", [(g, (g + offset) % groups) for g in range(groups)])


def partner(value):
    return lax.ppermute(value, "core", ((0, 1), (1, 0)))


def local(
    pol_hidden, ref_hidden, pol_routes, ref_routes, pol_gates, ref_gates,
    w_gate, w_up, w_down, norm_gain, vocab_head, targets, seq_lengths, owners,
):
    chip, core, group = lax.axis_index("chip"), lax.axis_index("core"), lax.axis_index("grp")
    chips, groups = lax.axis_size("chip"), lax.axis_size("grp")
    device = (group * chips + chip) * 2 + core
    experts = w_gate.shape[0] * chips * 2
    tokens, width = pol_hidden.shape
    share = 2 * tokens
    capacity = tokens * pol_routes.shape[1] // experts + 2
    vocab_rows = vocab_head.shape[0]
    offsets = range(1, chips)

    send = pack_rows(
        pol_hidden, ref_hidden, pol_routes, ref_routes, pol_gates, ref_gates, experts
    )
    plane = [send] + [across(send, d) for d in offsets]
    plane = plane + [partner(rows) for rows in plane]

    home = (group - jnp.arange(groups, dtype=jnp.int32)) % groups
    spots = home[None, :] * chips + (chip ^ jnp.arange(chips, dtype=jnp.int32))[:, None]
    spots = spots.reshape(-1)
    goal = targets.astype(jnp.float32).reshape(1, tokens)
    goal = jnp.concatenate((goal, goal), axis=1)
    goal = jnp.broadcast_to(goal, (groups, share))
    goal = lax.all_to_all(goal, "grp", split_axis=0, concat_axis=0, tiled=True)
    match = home[:, None] == jnp.arange(groups, dtype=jnp.int32)[None, :]
    goal = jnp.sum(jnp.where(match[:, :, None], goal[None], 0.0), axis=1).reshape(1, -1)
    other_head = partner(vocab_head)

    place = jnp.stack((chip, core)).astype(jnp.int32)
    keep, give = expert_sums(
        place, goal, plane, w_gate, w_up, w_down, tokens, capacity, width, experts
    )
    if chips == 4 and groups * share <= width // 2:
        own, mid_x, mid_y, send_x, send_y = split_sums(keep, partner(give), goal)
        from_x, from_y = across(send_x, 1), across(send_y, 2)
        next_x, next_y = middle_sums(mid_x, mid_y, from_x, from_y)
        last_x, last_y = across(next_x, 1), across(next_y, 2)
        normed, wanted = join_rows(
            send, norm_gain, goal, own, from_x, from_y, last_x, last_y
        )
    else:
        own, *sends = pair_sums(keep, partner(give), goal)
        came = [across(rows, d) for d, rows in zip(offsets, sends)]
        normed, wanted = norm_rows(send, norm_gain, goal, own, came)
    wanted = wanted.reshape(1, -1)

    column = [normed] + [along(normed, k) for k in range(1, groups)]
    if chips == 4:
        near = [across(rows, 1) for rows in column]
        far = [across(rows, 2) for rows in column]
        half = groups // 2
        cross = [across(rows, 2) for rows in near[:half]] + [
            across(rows, 1) for rows in far[half:]
        ]
    else:
        column = jnp.concatenate(column, axis=0)
        blocks = [column] + [across(column, d) for d in offsets]
    base = jnp.stack((device, device + 1 - 2 * core)).astype(jnp.int32) * vocab_rows
    lines = groups * share

    def stats_of(places, start, pieces, earlier, shape):
        blocks, parts = [block for block, _ in pieces], tuple(part for _, part in pieces)
        end = start + sum(high - low for low, high in parts)
        places = jnp.concatenate((base, places))
        return head_stats(
            places, wanted[:, start:end], blocks, parts, earlier, vocab_head, other_head, shape
        )

    if chips == 4:
        blocks = column + near + far + cross
        pieces = [(block, (0, share)) for block in blocks]
        stats = stats_of(spots, 0, pieces, (), (groups * chips, 2, share))
    else:
        fixed = jnp.arange(groups, dtype=jnp.int32)
        pieces = [
            stats_of(fixed, d * lines, [(block, (0, lines))], (), (groups, 2, share))
            for d, block in enumerate(blocks)
        ]
        pieces = jnp.concatenate(pieces, axis=0)
        stats = jnp.zeros_like(pieces).at[spots].set(pieces)

    lse, hit = combine([stats] + [along(stats, k) for k in range(1, groups)])
    stats = jnp.stack((lse, hit), axis=1)
    lse, hit = combine([stats] + [across(stats, d) for d in offsets])
    logprob = hit - lse
    ratio = logprob[:, :tokens] - logprob[:, tokens:]
    other = partner(ratio)
    token_ratio = lax.dynamic_index_in_dim(ratio, group * chips + chip, keepdims=False)

    mine = owners == device
    ends = jnp.cumsum(seq_lengths)
    length = jnp.sum(jnp.where(mine, seq_lengths, 0))
    end = jnp.sum(jnp.where(mine, ends, 0))
    row = jnp.arange(groups * chips, dtype=jnp.int32)[:, None]
    lane = jnp.arange(tokens, dtype=jnp.int32)[None, :]
    position = (2 * row + core) * tokens + lane
    inside = (position >= end - length) & (position < end)
    position = (2 * row + 1 - core) * tokens + lane
    inside_other = (position >= end - length) & (position < end)
    mean = jnp.sum(jnp.where(inside, ratio, 0.0) + jnp.where(inside_other, other, 0.0))
    return (token_ratio, (mean / length.astype(jnp.float32)).reshape(1))


def solution(mesh):
    names = ("grp", "chip", "core")
    groups, plane = mesh.devices.shape
    fine = Mesh(mesh.devices.reshape(groups, plane // 2, 2), names)
    return jax.shard_map(
        local,
        mesh=fine,
        in_specs=(
            P(names, None), P(names, None), P(names, None), P(names, None),
            P(names, None), P(names, None),
            P(names[1:], None, None), P(names[1:], None, None), P(names[1:], None, None),
            P(), P(names, None), P(names), P(), P(),
        ),
        out_specs=(P(names), P(names)),
        check_vma=False,
    )
```
